256 devices in a mesh: dp: 32 (over z_hi, y, core), hd: 8 (over x, z_lo).
Axes of the slice: x: 4, y: 4, z: 8 (z_hi: 4, z_lo: 2; z = z_hi * 2 + z_lo), core: 2. Of those that a mesh axis runs over, the one named last changes fastest.
Arguments:
- query_nope: bfloat16 [2048, 16384], P('dp', 'hd'), may hold values from -6 to 6
- query_rope: bfloat16 [2048, 8192], P('dp', 'hd')
- latent: bfloat16 [2048, 512], P('dp'), may hold values from -6 to 6
- key_rope: bfloat16 [2048, 64], P('dp'), may hold values from -6 to 6
- key_up: bfloat16 [512, 16384], P(None, 'hd'), may hold values from -0.25 to 0.25
- value_up: bfloat16 [512, 16384], P(None, 'hd'), may hold values from -0.25 to 0.25
- output_weight: bfloat16 [16384, 7168], P('hd', 'dp'), may hold values from -0.046875 to 0.046875
- residual: bfloat16 [2048, 7168], P('dp', 'hd'), may hold values from -6 to 6
- norm_gain: float32 [7168], P('hd'), may hold values from 0.1 to 1.9
- gate_weight: bfloat16 [7168, 18432], P('hd', 'dp'), may hold values from -0.0625 to 0.0625
- up_weight: bfloat16 [7168, 18432], P('hd', 'dp'), may hold values from -0.0625 to 0.0625
- down_weight: bfloat16 [18432, 7168], P('dp', 'hd'), may hold values from -0.046875 to 0.046875
- rank_tokens: int32 [32], replicated, may hold values from 1 to 64, 1024 in all
- request_ids: int32 [32, 64], P('dp'), may hold values from 0 to 3, never falling along the last dimension, each value on 1 to 32 neighbouring positions
Outputs:
- layer_out: bfloat16 [2048, 7168], P('dp', 'hd')
The draws below stay inside these ranges and needn't reach their ends.
Inputs may be any that keep to these rules, and one draw needn't show every extreme that they name: `rank_tokens`: the counts sum to 1024. `request_ids`: along each rank's slots the number never falls; one request covers at most 32 slots.
All inputs are finite; a program needn't handle non-finite values.
Results may differ from the reference program's by a relative error of at most 0.0085.
Values may be sent and summed in bfloat16 or wider, within the bound.
No kernel may reach another device: no remote copies, remote signals or barrier semaphores. Data moves between devices by JAX's collectives and lax.ppermute only.
A program may use at most 128 MiB of HBM per device.

```python
import math
import jax
import jax.numpy as jnp
import numpy as np
from jax import lax

D = 7168
FF = 18432
H = 128
NOPE = 128
ROPE = 64
VH = 128
KVR = 512
REQS = 4
SLOTS = 64
MOST = 32
NTOK = 2048
LIVE = 1024
N_DP = 32


def rope_base(key):
    total_rows = SLOTS * N_DP
    return jnp.clip(jax.random.normal(jax.random.fold_in(key, 11), (total_rows, ROPE), jnp.float32), -6.0, 6.0)


def draw_key_rope(key, part):
    return rope_base(key).astype(jnp.bfloat16)


def draw_query_rope(key, part):
    key = jax.random.fold_in(key, 5)
    total_rows = SLOTS * N_DP
    drawn = jnp.clip(jax.random.normal(jax.random.fold_in(key, 1), (total_rows, H, ROPE), jnp.float32), -6.0, 6.0)
    return drawn.reshape(total_rows, H * ROPE).astype(jnp.bfloat16)


def block_levels(rng, shape, split, smallest, top_value):
    level, own = 1.0, jax.random.fold_in(rng, 6)
    for dim, parts in split:
        heights = jnp.exp(jax.random.uniform(jax.random.fold_in(own, dim), (parts,), jnp.float32, smallest / len(split), top_value / len(split)))
        level = level * jnp.repeat(heights, shape[dim] // parts).reshape([-1 if axis == dim else 1 for axis in range(len(shape))])
    return level


def length_profile(number_of, total, bound, slope):
    portions = [(1 << 20) // math.isqrt(grade ** slope) + 1 for grade in range(2, number_of + 1)]
    surplus, given = total - bound - (number_of - 1), [1] * (number_of - 1)
    while surplus > 0:
        candidates = [i for i in range(number_of - 1) if given[i] < bound]
        pool, left = sum([portions[i] for i in candidates]), surplus
        for i in candidates:
            addition = min(bound - given[i], max(1, left * portions[i] // pool), surplus)
            given[i] = given[i] + addition
            surplus = surplus - addition
    return np.array([bound] + given)


def ragged_sizes(stream_key, number_of, total, most, lean):
    if number_of == 2:
        one = jax.random.randint(stream_key, (), max(1, total - most), min(most, total - 1) + 1)
        return jnp.stack([one, total - one])
    tallies = jnp.asarray(length_profile(number_of, total, most, lean), jnp.int32)
    couples = (number_of - 1) // 2
    source_of, sink = tallies[1:1 + 2 * couples:2], tallies[2:2 + 2 * couples:2]
    margin = jnp.minimum(source_of - 1, most - sink)
    moved = jax.random.randint(jax.random.fold_in(stream_key, 1), (couples,), 0, 1 << 20) % (margin + 1)
    tallies = tallies.at[1:1 + 2 * couples:2].set(source_of - moved).at[2:2 + 2 * couples:2].set(sink + moved)
    return tallies[jax.random.permutation(jax.random.fold_in(stream_key, 2), number_of)]


def gaussian(key, dims, width, limit, pieces=(), kind=jnp.bfloat16):
    values = jax.random.normal(key, dims, jnp.float32) * width
    if len(pieces) > 0:
        values = block_levels(key, dims, pieces, -0.22, 0.18) * values
    return jnp.clip(values, min=-limit, max=limit).astype(kind)


def setup_inputs(seed: int = 0) -> dict:
    keys = jax.random.split(jax.random.key(seed), 15)
    query_nope = gaussian(keys[0], (NTOK, H * NOPE), 1.0, 6.0, ((0, 32), (1, 8)))
    query_rope = draw_query_rope(jax.random.fold_in(keys[14], 71), 0)
    latent = gaussian(keys[2], (NTOK, KVR), 1.0, 6.0, ((0, 32),))
    key_rope = draw_key_rope(jax.random.fold_in(keys[14], 71), 0)
    key_up = gaussian(keys[4], (KVR, H * NOPE), KVR ** -0.5, 0.25, ((1, 8),))
    value_up = gaussian(keys[5], (KVR, H * VH), KVR ** -0.5, 0.25, ((1, 8),))
    output_weight = gaussian(keys[6], (H * VH, D), (H * VH) ** -0.5, 0.046875, ((0, 8), (1, 32)))
    residual = gaussian(keys[7], (NTOK, D), 1.0, 6.0, ((0, 32), (1, 8)))
    norm_gain = jnp.clip(1.0 + 0.18 * jax.random.normal(keys[8], (D,), jnp.float32), 0.1, 1.9)
    gate_weight = gaussian(keys[9], (D, FF), D ** -0.5, 0.0625, ((0, 8), (1, 32)))
    up_weight = gaussian(keys[10], (D, FF), D ** -0.5, 0.0625, ((0, 8), (1, 32)))
    down_weight = gaussian(keys[11], (FF, D), FF ** -0.5, 0.046875, ((0, 32), (1, 8)))
    rank_tokens = ragged_sizes(keys[12], N_DP, LIVE, SLOTS, 2).astype(jnp.int32)
    request_ids = jax.vmap(lambda own: jnp.searchsorted(jnp.cumsum(ragged_sizes(own, REQS, SLOTS, MOST, 1)), jnp.arange(SLOTS), side="right"))(jax.random.split(keys[13], N_DP)).reshape((N_DP, SLOTS)).astype(jnp.int32)
    return {"query_nope": query_nope, "query_rope": query_rope, "latent": latent, "key_rope": key_rope, "key_up": key_up, "value_up": value_up, "output_weight": output_weight, "residual": residual, "norm_gain": norm_gain, "gate_weight": gate_weight, "up_weight": up_weight, "down_weight": down_weight, "rank_tokens": rank_tokens, "request_ids": request_ids}


def attend(query_nope, query_rope, latent, key_rope, request_row, key_up, value_up):
    slots = latent.shape[0]
    heads = key_up.shape[1] // NOPE
    key_nope = jnp.dot(latent, key_up, preferred_element_type=jnp.float32).astype(jnp.bfloat16)
    values = jnp.dot(latent, value_up, preferred_element_type=jnp.float32).astype(jnp.bfloat16)
    query_heads = query_nope.reshape(slots, heads, NOPE).astype(jnp.float32)
    rotary_heads = query_rope.reshape(slots, heads, ROPE).astype(jnp.float32)
    key_heads = key_nope.reshape(slots, heads, NOPE).astype(jnp.float32)
    scores = jnp.einsum('shd,thd->hst', query_heads, key_heads)
    scores = scores + jnp.einsum('shd,td->hst', rotary_heads, key_rope.astype(jnp.float32))
    scores = scores * (NOPE + ROPE) ** (-0.5)
    position = jnp.arange(slots, dtype=jnp.int32)
    allowed = (request_row[:, None] == request_row[None, :]) & (position[None, :] <= position[:, None])
    scores = jnp.where(allowed[None, :, :], scores, jnp.float32(-1e+30))
    top = lax.optimization_barrier(jnp.max(scores, axis=-1, keepdims=True))
    raised = jnp.exp(scores - top)
    weights = (raised / lax.optimization_barrier(jnp.sum(raised, axis=-1, keepdims=True))).astype(jnp.bfloat16)
    value_heads = values.reshape(slots, heads, VH).astype(jnp.float32)
    attended = jnp.einsum('hst,thd->shd', weights.astype(jnp.float32), value_heads)
    return attended.astype(jnp.bfloat16).reshape(slots, heads * VH)

def reference(query_nope, query_rope, latent, key_rope, key_up, value_up, output_weight, residual, norm_gain, gate_weight, up_weight, down_weight, rank_tokens, request_ids):
    ranks = rank_tokens.shape[0]

    def one_rank(items):
        return attend(items[0], items[1], items[2], items[3], items[4], key_up, value_up)
    attended = lax.map(one_rank, (query_nope.reshape(ranks, SLOTS, -1), query_rope.reshape(ranks, SLOTS, -1), latent.reshape(ranks, SLOTS, -1), key_rope.reshape(ranks, SLOTS, -1), request_ids))
    attended = attended.reshape(NTOK, -1)
    projected = jnp.dot(attended, output_weight, preferred_element_type=jnp.float32)
    mixed = (residual.astype(jnp.float32) + projected).astype(jnp.bfloat16)
    widened = mixed.astype(jnp.float32)
    mean_square = lax.optimization_barrier(jnp.sum(widened * widened, axis=1, keepdims=True)) / D
    normed = (widened * lax.rsqrt(mean_square + 1e-06) * norm_gain).astype(jnp.bfloat16)
    gate = jnp.dot(normed, gate_weight, preferred_element_type=jnp.float32)
    up_value = jnp.dot(normed, up_weight, preferred_element_type=jnp.float32)
    hidden = (jax.nn.silu(gate) * up_value).astype(jnp.bfloat16)
    mlp = jnp.dot(hidden, down_weight, preferred_element_type=jnp.float32)
    row_index = jnp.arange(NTOK, dtype=jnp.int32)
    counts = rank_tokens[row_index // SLOTS]
    live = row_index % SLOTS < counts
    result = (widened + mlp).astype(jnp.bfloat16)
    return jnp.where(live[:, None], result, jnp.zeros_like(result))
```

```python
import jax
import jax.numpy as jnp
from jax import lax
from jax.experimental import pallas as pl
from jax.experimental.pallas import tpu as pltpu
from jax.sharding import Mesh, PartitionSpec as P

BF = jnp.bfloat16
F32 = jnp.float32
NOPE = 128
ROPE = 64
VH = 128
WIN = 32
LIVE = 1024
BLK = 128
DP = ("zh", "y", "c")
HD = ("x", "zl")


def dot(a, b):
    return jnp.dot(a, b, preferred_element_type=F32)


def shifted(x, axis, shift):
    n = lax.axis_size(axis)
    return lax.ppermute(x, axis, [(i, (i + shift) % n) for i in range(n)])


def iota(shape, dim):
    return lax.broadcasted_iota(jnp.int32, shape, dim)


def score_kernel(place_ref, counts_ref, qn_ref, qr_ref, lat_ref, kr_ref, ku_ref, req_ref, out_ref):
    slots = lat_ref.shape[0]
    heads = ku_ref.shape[1] // NOPE
    place = place_ref[0]
    before = lax.fori_loop(
        0,
        counts_ref.shape[0],
        lambda i, a: a + jnp.where(i < place, counts_ref[i], 0),
        jnp.int32(0),
    )
    keys = dot(lat_ref[...], ku_ref[...]).astype(BF)
    key_rope = kr_ref[...]
    s_at, t_at = iota((slots, slots), 0), iota((slots, slots), 1)
    across = jnp.broadcast_to(req_ref[...], (slots, slots))
    down = jnp.sum(jnp.where(s_at == t_at, across, 0), axis=1, keepdims=True)
    allowed = (across == down) & (t_at <= s_at)
    t_row, lane = iota((slots, BLK), 0), iota((slots, BLK), 1)
    lands = ((before + t_row) & (WIN - 1)) == (lane & (WIN - 1))
    nt = (((1,), (1,)), ((), ()))
    per = BLK // WIN
    for group in range(heads // per):
        total = jnp.zeros((slots, BLK), F32)
        for i in range(per):
            h = group * per + i
            s = lax.dot_general(
                qn_ref[:, h * NOPE : (h + 1) * NOPE],
                keys[:, h * NOPE : (h + 1) * NOPE],
                nt,
                preferred_element_type=F32,
            )
            s = s + lax.dot_general(
                qr_ref[:, h * ROPE : (h + 1) * ROPE], key_rope, nt, preferred_element_type=F32
            )
            s = jnp.where(allowed, s * (NOPE + ROPE) ** (-0.5), jnp.float32(-1e30))
            raised = jnp.exp(s - jnp.max(s, axis=-1, keepdims=True))
            w = (raised / jnp.sum(raised, axis=-1, keepdims=True)).astype(BF)
            fold = jnp.where(lands & ((lane >> 5) == i), 1.0, 0.0).astype(BF)
            total = total + dot(w, fold)
        out_ref[:, group * BLK : (group + 1) * BLK] = total.astype(BF)


def score_weights(place, counts, qn, qr, lat, kr, ku, req):
    heads = ku.shape[1] // NOPE
    smem = pl.BlockSpec(memory_space=pltpu.SMEM)
    vmem = pl.BlockSpec(memory_space=pltpu.VMEM)
    return pl.pallas_call(
        score_kernel,
        out_shape=jax.ShapeDtypeStruct((lat.shape[0], heads * WIN), BF),
        in_specs=[smem, smem] + [vmem] * 6,
        out_specs=vmem,
        compiler_params=pltpu.CompilerParams(vmem_limit_bytes=32 * 1024 * 1024),
        name="score_weights",
    )(place, counts, qn, qr, lat, kr, ku, req)


def mix_kernel(wp_ref, prev_ref, cur_ref, wo_ref, out_ref, att_ref):
    heads = cur_ref.shape[1] // VH
    r_at, l_at = iota((BLK, BLK), 0), iota((BLK, BLK), 1)
    in_prev = (BLK + r_at - l_at) < WIN
    gap = r_at - l_at
    in_cur = (gap >= 0) & (gap < WIN)
    per = BLK // WIN
    for group in range(heads // per):
        packed = wp_ref[:, group * BLK : (group + 1) * BLK].astype(F32)
        for i in range(per):
            h = group * per + i
            one = jnp.where((l_at >> 5) == i, packed, 0.0)
            one = one + pltpu.roll(one, WIN, 1)
            one = one + pltpu.roll(one, 2 * WIN, 1)
            band = jnp.concatenate(
                [jnp.where(in_prev, one, 0.0), jnp.where(in_cur, one, 0.0)], axis=1
            ).astype(BF)
            cols = slice(h * VH, (h + 1) * VH)
            both = jnp.concatenate([prev_ref[:, cols], cur_ref[:, cols]], axis=0)
            att_ref[:, cols] = dot(band, both).astype(BF)
    part = dot(att_ref[...], wo_ref[...]).astype(BF)
    order = ((r_at & 15) * 8 + (r_at >> 4)) == l_at
    part = dot(jnp.where(order, 1.0, 0.0).astype(BF), part).astype(BF)
    out_ref[...] = part.reshape(out_ref.shape)


def mix_project(wp, values, wo):
    rows, width = values.shape
    n = wo.shape[1]
    return pl.pallas_call(
        mix_kernel,
        grid=(rows // BLK,),
        out_shape=jax.ShapeDtypeStruct((8, rows // 8, n), BF),
        in_specs=[
            pl.BlockSpec((BLK, wp.shape[1]), lambda b: (b, 0)),
            pl.BlockSpec((BLK, width), lambda b: (jnp.maximum(b - 1, 0), 0)),
            pl.BlockSpec((BLK, width), lambda b: (b, 0)),
            pl.BlockSpec((width, n), lambda b: (0, 0)),
        ],
        out_specs=pl.BlockSpec((8, BLK // 8, n), lambda b: (0, b, 0)),
        scratch_shapes=[pltpu.VMEM((BLK, width), BF)],
        compiler_params=pltpu.CompilerParams(vmem_limit_bytes=32 * 1024 * 1024),
        name="mix_project",
    )(wp, values, values, wo)


def gate_up_kernel(x_ref, gain_ref, gate_ref, up_ref, out_ref):
    pieces, rows, k = x_ref.shape
    ff = gate_ref.shape[1]
    gate = jnp.zeros((rows, ff), F32)
    up = jnp.zeros((rows, ff), F32)
    squares = jnp.zeros((rows, 1), F32)
    for jj in range(pieces):
        j = (jj & 1) * 2 + (jj >> 1)
        x = x_ref[jj].astype(F32)
        squares = squares + jnp.sum(x * x, axis=1, keepdims=True)
        xg = (x * gain_ref[j]).astype(BF)
        gate = gate + dot(xg, gate_ref[j * k : (j + 1) * k, :])
        up = up + dot(xg, up_ref[j * k : (j + 1) * k, :])
    lane = iota((rows, BLK), 1)
    high = squares.astype(BF).astype(F32)
    extra = jnp.where(lane == 0, high, jnp.where(lane == 1, squares - high, 0.0))
    shape = out_ref.shape
    both = jnp.concatenate([gate, up, extra], axis=1).astype(BF)
    out_ref[...] = both.reshape(shape)


def gate_up(x4, gain, gate_weight, up_weight):
    pieces, tokens, k = x4.shape
    ff = gate_weight.shape[1]
    rows = 256
    chunk = tokens // 8
    per = rows // chunk
    return pl.pallas_call(
        gate_up_kernel,
        grid=(tokens // rows,),
        out_shape=jax.ShapeDtypeStruct((8, chunk, 2 * ff + BLK), BF),
        in_specs=[
            pl.BlockSpec((pieces, rows, k), lambda b: (0, b, 0)),
            pl.BlockSpec((pieces, 1, k), lambda b: (0, 0, 0)),
            pl.BlockSpec((pieces * k, ff), lambda b: (0, 0)),
            pl.BlockSpec((pieces * k, ff), lambda b: (0, 0)),
        ],
        out_specs=pl.BlockSpec((per, chunk, 2 * ff + BLK), lambda b: (b, 0, 0)),
        compiler_params=pltpu.CompilerParams(vmem_limit_bytes=32 * 1024 * 1024),
        name="gate_up",
    )(x4, gain.reshape(pieces, 1, k), gate_weight, up_weight)


def gather_relative(x):
    x = jnp.concatenate([x] + [shifted(x, "zh", s) for s in (1, 2, 3)], axis=0)
    x = jnp.concatenate([x] + [shifted(x, "y", s) for s in (1, 2, 3)], axis=0)
    return jnp.concatenate([x, shifted(x, "c", 1)], axis=0)


def place_blocks(x, axis, spot):
    n = lax.axis_size(axis)
    me = lax.axis_index(axis)
    out = jnp.zeros((n,) + x.shape, x.dtype)
    for s in range(n):
        piece = x if s == 0 else shifted(x, axis, s)
        at = spot((me - s + n) % n)
        out = lax.dynamic_update_slice(out, piece[None], (at,) + (0,) * x.ndim)
    return out


def pick(x, index):
    return lax.dynamic_index_in_dim(x, index, 0, keepdims=False)


def on_device(
    query_nope,
    query_rope,
    latent,
    key_rope,
    key_up,
    value_up,
    output_weight,
    residual,
    norm_gain,
    gate_weight,
    up_weight,
    down_weight,
    rank_tokens,
    request_ids,
):
    slots = latent.shape[0]
    ranks = rank_tokens.shape[0]
    zh, y, c = (lax.axis_index(a) for a in DP)
    x_at, zl = (lax.axis_index(a) for a in HD)
    rank = (zh * 4 + y) * 2 + c
    chunk = LIVE // 8
    width = residual.shape[1]
    quarter = width // 4
    model = 8 * width

    every = jnp.arange(ranks, dtype=jnp.int32)

    def starts(which):
        return jnp.sum(jnp.where(every < which[..., None], rank_tokens, 0), axis=-1)

    def lengths(which):
        return jnp.sum(jnp.where(every == which[..., None], rank_tokens, 0), axis=-1)

    own_start, own_length = starts(rank), lengths(rank)
    slot = jnp.arange(slots, dtype=jnp.int32)

    latents = gather_relative(latent)
    weights = score_weights(
        rank.reshape(1), rank_tokens, query_nope, query_rope, latent, key_rope, key_up, request_ids
    )
    weights = gather_relative(weights)

    back = jnp.arange(ranks, dtype=jnp.int32)
    source = (
        ((zh - (back & 3)) & 3) * 8 + ((y - ((back >> 2) & 3)) & 3) * 2 + (c ^ (back >> 4))
    )
    goes = jnp.where(
        slot[None, :] < lengths(source)[:, None], starts(source)[:, None] + slot[None, :], -1
    ).reshape(1, ranks * slots)
    compact = (goes == jnp.arange(LIVE, dtype=jnp.int32)[:, None]).astype(BF)
    latents = dot(compact, latents).astype(BF)
    values = dot(latents, value_up).astype(BF)
    weights = dot(compact, weights).astype(BF)

    eight = jnp.arange(8, dtype=jnp.int32)
    spread = ((eight[:, None] - own_start) & 7) + 8 * eight[None, :]
    roll = (spread.reshape(slots, 1) == slot[None, :]).astype(BF)
    rows = dot(roll, residual).astype(BF).reshape(2, 4, 8, 2, 2, quarter)
    rows = rows.transpose(1, 0, 3, 4, 2, 5).reshape(ranks, 8, quarter)
    rows = lax.all_to_all(rows, DP, split_axis=0, concat_axis=0, tiled=True)
    mine = (y >> 1) * 4 + zh
    place = ((mine - starts(every)[:, None]) & 7) + 8 * eight[None, :]
    goes = jnp.where(
        place < rank_tokens[:, None], (starts(every)[:, None] + place) >> 3, -1
    ).reshape(1, ranks * 8)
    gather = (goes == jnp.arange(chunk, dtype=jnp.int32)[:, None]).astype(BF)
    rows = dot(gather, rows.reshape(ranks * 8, quarter))

    part = mix_project(weights, values, output_weight)
    part = lax.all_to_all(part, HD, split_axis=0, concat_axis=0, tiled=True)
    projected = jnp.sum(part.astype(F32), axis=0).astype(BF)
    sends = []
    for a in range(4):
        for b in range(4):
            for e in range(2):
                for f in range(4):
                    for g in range(2):
                        m = f * 2 + g
                        to = ((m & 3) * 4 + (m >> 2) * 2 + (b & 1)) * 2 + e
                        h = a * 2 + (b >> 1)
                        sends.append((((a * 4 + b) * 2 + e) * 8 + m, to * 8 + h))
    projected = lax.ppermute(projected, DP + HD, sends)
    mixed = (rows + projected.astype(F32)).astype(BF)

    full = place_blocks(mixed, "zh", lambda i: i)
    full = place_blocks(full, "y", lambda i: (i & 1) * 2 + (i >> 1))
    full = place_blocks(full, "c", lambda i: i)
    full = full.reshape(4, LIVE, quarter)

    part = gate_up(full, norm_gain, gate_weight, up_weight)
    part = lax.all_to_all(part, HD, split_axis=0, concat_axis=0, tiled=True)
    total = jnp.sum(part.astype(F32), axis=0)
    ff = down_weight.shape[0]
    scale = lax.rsqrt((total[:, 2 * ff : 2 * ff + 1] + total[:, 2 * ff + 1 : 2 * ff + 2]) / model + 1e-06)
    hidden = (jax.nn.silu(total[:, :ff] * scale) * (total[:, ff : 2 * ff] * scale)).astype(BF)
    hidden = jnp.broadcast_to(hidden[None], (8,) + hidden.shape)
    hidden = lax.all_to_all(hidden, HD, split_axis=0, concat_axis=0, tiled=True)

    down = dot(hidden.reshape(LIVE, ff), down_weight).reshape(4, 2, chunk, width)
    down = jnp.swapaxes(down, 0, 1)
    down = pick(down, c) + shifted(pick(down, 1 - c).astype(BF), "c", 1).astype(F32)
    total = pick(down, y)
    for s in (1, 2, 3):
        total = total + shifted(pick(down, (y + s) & 3).astype(BF), "y", s).astype(F32)
    m = y * 2 + c
    first = starts(every)
    place = ((m - first[:, None]) & 7) + 8 * eight[None, :]
    comes = jnp.where(place < rank_tokens[:, None], (first[:, None] + place) >> 3, -1)
    expand = (comes.reshape(4, slots, 1) == jnp.arange(chunk, dtype=jnp.int32)).astype(BF)
    planes = dot(expand.reshape(4 * slots, chunk), total.astype(BF)).reshape(4, slots, width)
    own = full.reshape(4, 8, chunk, quarter)
    own = lax.dynamic_index_in_dim(own, m, 1, keepdims=False)
    own = jnp.concatenate([own[0], own[2], own[1], own[3]], axis=1)
    result = dot(pick(expand, zh), own) + pick(planes, zh)
    for s in (1, 2, 3):
        result = result + shifted(pick(planes, (zh + s) & 3).astype(BF), "zh", s).astype(F32)
    result = lax.all_to_all(
        result.astype(BF).reshape(8, 8, width), ("y", "c"), split_axis=0, concat_axis=0, tiled=True
    )
    at = ((own_start + slot) & 7) * 8 + (slot >> 3)
    at = jnp.where(slot < own_length, at, -1)
    back = (at[:, None] == slot[None, :]).astype(BF)
    return dot(back, result.reshape(slots, width)).astype(BF)


def solution(mesh):
    mesh = Mesh(mesh.devices.reshape(4, 4, 2, 4, 2), DP + HD)
    in_specs = (
        P(DP, HD),
        P(DP, HD),
        P(DP, None),
        P(DP, None),
        P(None, HD),
        P(None, HD),
        P(HD, DP),
        P(DP, HD),
        P(HD),
        P(HD, DP),
        P(HD, DP),
        P(DP, HD),
        P(),
        P(DP, None),
    )
    return jax.shard_map(
        on_device, mesh=mesh, in_specs=in_specs, out_specs=P(DP, HD), check_vma=False
    )
```

```python
import jax
import jax.numpy as jnp
from jax import lax
from jax.experimental import pallas as pl
from jax.experimental.pallas import tpu as pltpu
from jax.sharding import Mesh, PartitionSpec as P

BF = jnp.bfloat16
F32 = jnp.float32
NOPE = 128
ROPE = 64
VH = 128
WIN = 32
LIVE = 1024
BLK = 128
DP = ("zh", "y", "c")
HD = ("x", "zl")


def dot(a, b):
    return jnp.dot(a, b, preferred_element_type=F32)


def shifted(x, axis, shift):
    n = lax.axis_size(axis)
    return lax.ppermute(x, axis, [(i, (i + shift) % n) for i in range(n)])


def iota(shape, dim):
    return lax.broadcasted_iota(jnp.int32, shape, dim)


def nt(a, b):
    return lax.dot_general(a, b, (((1,), (1,)), ((), ())), preferred_element_type=F32)


def whole(shape):
    return pl.BlockSpec(shape, lambda *_: (0,) * len(shape))


def score_kernel(counts_ref, qn_ref, qr_ref, lat_ref, kr_ref, ku_ref, req_ref, out_ref):
    slots = lat_ref.shape[0]
    heads = ku_ref.shape[1] // NOPE
    place = (lax.axis_index("zh") * 4 + lax.axis_index("y")) * 2 + lax.axis_index("c")
    before = lax.fori_loop(
        0,
        counts_ref.shape[0],
        lambda i, a: a + jnp.where(i < place, counts_ref[i], 0),
        jnp.int32(0),
    )
    keys = dot(lat_ref[...], ku_ref[...]).astype(BF)
    key_rope = kr_ref[...]
    s_at, t_at = iota((slots, slots), 0), iota((slots, slots), 1)
    across = jnp.broadcast_to(req_ref[...], (slots, slots))
    down = jnp.sum(jnp.where(s_at == t_at, across, 0), axis=1, keepdims=True)
    allowed = (across == down) & (t_at <= s_at)
    t_row, lane = iota((slots, BLK), 0), iota((slots, BLK), 1)
    lands = ((before + t_row) & (WIN - 1)) == (lane & (WIN - 1))
    per = BLK // WIN
    for group in range(heads // per):
        total = jnp.zeros((slots, BLK), F32)
        for i in range(per):
            h = group * per + i
            s = nt(qn_ref[:, h * NOPE : (h + 1) * NOPE], keys[:, h * NOPE : (h + 1) * NOPE])
            s = s + nt(qr_ref[:, h * ROPE : (h + 1) * ROPE], key_rope)
            s = jnp.where(allowed, s * (NOPE + ROPE) ** (-0.5), jnp.float32(-1e30))
            raised = jnp.exp(s - jnp.max(s, axis=-1, keepdims=True))
            w = (raised / jnp.sum(raised, axis=-1, keepdims=True)).astype(BF)
            fold = jnp.where(lands & ((lane >> 5) == i), 1.0, 0.0).astype(BF)
            total = total + dot(w, fold)
        out_ref[:, group * BLK : (group + 1) * BLK] = total.astype(BF)


def score_weights(counts, *arrays):
    slots, heads = arrays[2].shape[0], arrays[4].shape[1] // NOPE
    shape = (slots, heads * WIN)
    return pl.pallas_call(
        score_kernel,
        grid=(1,),
        out_shape=jax.ShapeDtypeStruct(shape, BF),
        in_specs=[pl.BlockSpec(memory_space=pltpu.SMEM)] + [whole(a.shape) for a in arrays],
        out_specs=whole(shape),
        name="score_weights",
    )(counts, *arrays)


def live_rows(goes_ref, own_ref, other_ref):
    row = iota((BLK, own_ref.shape[0]), 0) + pl.program_id(0) * BLK
    out = dot(jnp.where(goes_ref[0] == row, 1.0, 0.0).astype(BF), own_ref[...])
    out = out + dot(jnp.where(goes_ref[1] == row, 1.0, 0.0).astype(BF), other_ref[...])
    return out.astype(BF)


def values_kernel(goes_ref, own_ref, other_ref, up_ref, out_ref):
    out_ref[...] = dot(live_rows(goes_ref, own_ref, other_ref), up_ref[...]).astype(BF)


def live_values(goes, own, other, up):
    width = up.shape[1]
    return pl.pallas_call(
        values_kernel,
        grid=(LIVE // BLK,),
        out_shape=jax.ShapeDtypeStruct((LIVE, width), BF),
        in_specs=[whole(a.shape) for a in (goes, own, other, up)],
        out_specs=pl.BlockSpec((BLK, width), lambda b: (b, 0)),
        name="live_values",
    )(goes, own, other, up)


def mix_kernel(goes_ref, own_ref, other_ref, prev_ref, cur_ref, wo_ref, out_ref, att_ref, all_ref):
    b = pl.program_id(0)
    heads = cur_ref.shape[1] // VH
    r_at, l_at = iota((BLK, BLK), 0), iota((BLK, BLK), 1)
    gap = r_at - l_at
    near = (gap >= 0) & (gap < WIN)
    per = BLK // WIN
    masks = [jnp.where(near & ((l_at >> 5) == q), 1.0, 0.0).astype(BF) for q in range(per)]
    r_at2, l_at2 = iota((WIN, BLK), 0), iota((WIN, BLK), 1)
    before = jnp.where((BLK + r_at2 - l_at2) < WIN, 1.0, 0.0).astype(BF)
    blank = jnp.zeros((BLK - WIN, BLK), BF)
    packed = live_rows(goes_ref, own_ref, other_ref)
    for group in range(heads // per):
        one = packed[:, group * BLK : (group + 1) * BLK].astype(F32)
        turned = [one.astype(BF)]
        for q in range(1, per):
            turned.append(pltpu.roll(one, q * WIN, 1).astype(BF))
        for i in range(per):
            cols = slice((group * per + i) * VH, (group * per + i + 1) * VH)
            band = turned[(-i) % per] * masks[0]
            for q in range(1, per):
                band = band + turned[(q - i) % per] * masks[q]
            old = jnp.concatenate([turned[(per - 1 - i) % per][:WIN] * before, blank], axis=0)
            band = jnp.concatenate([old, band], axis=1)
            both = jnp.concatenate([prev_ref[:, cols], cur_ref[:, cols]], axis=0)
            att_ref[:, cols] = dot(band, both).astype(BF)
    part = nt(att_ref[...], wo_ref[...]).astype(BF)
    order = ((r_at & 15) * 8 + (r_at >> 4)) == l_at
    part = dot(jnp.where(order, 1.0, 0.0).astype(BF), part)
    rows = pl.ds(pl.multiple_of(b * 16, 16), 16)
    for m in range(8):
        all_ref[m, rows, :] = part[m * 16 : (m + 1) * 16]

    @pl.when(b == pl.num_programs(0) - 1)
    def _():
        for m in range(8):
            out_ref[m] = all_ref[m].T.astype(BF)


def mix_project(goes, own, other, values, wo):
    width = values.shape[1]
    n = wo.shape[0]
    shape = (8, n, LIVE // 8)
    return pl.pallas_call(
        mix_kernel,
        grid=(LIVE // BLK,),
        out_shape=jax.ShapeDtypeStruct(shape, BF),
        in_specs=[
            whole(goes.shape),
            whole(own.shape),
            whole(other.shape),
            pl.BlockSpec((BLK, width), lambda b: (jnp.maximum(b - 1, 0), 0)),
            pl.BlockSpec((BLK, width), lambda b: (b, 0)),
            whole(wo.shape),
        ],
        out_specs=whole(shape),
        scratch_shapes=[pltpu.VMEM((BLK, width), BF), pltpu.VMEM((8, LIVE // 8, n), F32)],
        name="mix_project",
    )(goes, own, other, values, values, wo)


def gate_up_kernel(own_ref, other_ref, gain_ref, gate_ref, up_ref, out_ref, x_ref):
    core = lax.axis_index("c")
    _, lows, blocks, k, chunk = own_ref.shape
    ff = gate_ref.shape[0]
    squares = jnp.zeros((1, blocks * chunk), F32)
    for ref, flip in ((own_ref, core), (other_ref, 1 - core)):
        for low in range(lows):
            rows = pl.ds(pl.multiple_of((low * 2 + flip) * k, 32), k)
            x = jnp.concatenate([ref[0, low, i] for i in range(blocks)], axis=1).astype(F32)
            squares = squares + jnp.sum(x * x, axis=0, keepdims=True)
            x_ref[rows, :] = (x * gain_ref[rows, :]).astype(BF)
    x = x_ref[...]
    gate = dot(gate_ref[...], x).astype(BF)
    up = dot(up_ref[...], x).astype(BF)
    row = iota((16, blocks * chunk), 0)
    high = squares.astype(BF).astype(F32)
    extra = jnp.where(row == 0, high, jnp.where(row == 1, squares - high, 0.0)).astype(BF)
    for i in range(blocks):
        cols = slice(i * chunk, (i + 1) * chunk)
        out_ref[i, :ff, :] = gate[:, cols]
        out_ref[i, ff : 2 * ff, :] = up[:, cols]
        out_ref[i, 2 * ff :, :] = extra[:, cols]


def gate_up(own, other, gain, gate_weight, up_weight):
    highs, lows, planes, k, chunk = own.shape
    ff, width = gate_weight.shape
    blocks = 2
    spec = pl.BlockSpec(
        (1, lows, blocks, k, chunk),
        lambda b: (b // (planes // blocks), 0, b % (planes // blocks), 0, 0),
    )
    return pl.pallas_call(
        gate_up_kernel,
        grid=(highs * planes // blocks,),
        out_shape=jax.ShapeDtypeStruct((highs * planes, 2 * ff + 16, chunk), BF),
        in_specs=[spec, spec, whole((width, 1)), whole((ff, width)), whole((ff, width))],
        out_specs=pl.BlockSpec((blocks, 2 * ff + 16, chunk), lambda b: (b, 0, 0)),
        scratch_shapes=[pltpu.VMEM((width, blocks * chunk), BF)],
        name="gate_up",
    )(own, other, gain, gate_weight, up_weight)


def exchange(x, axes):
    return lax.all_to_all(x, axes, split_axis=0, concat_axis=0, tiled=True)


def gather(x, axes):
    n = lax.axis_size(axes)
    return exchange(jnp.broadcast_to(x[None], (n,) + x.shape), axes)


def pick(x, index):
    return lax.dynamic_index_in_dim(x, index, 0, keepdims=False)


def on_device(
    query_nope,
    query_rope,
    latent,
    key_rope,
    key_up,
    value_up,
    output_weight,
    residual,
    norm_gain,
    gate_weight,
    up_weight,
    down_weight,
    rank_tokens,
    request_ids,
):
    slots = latent.shape[0]
    ranks = rank_tokens.shape[0]
    zh, y, c = (lax.axis_index(a) for a in DP)
    x_at, zl = (lax.axis_index(a) for a in HD)
    rank = (zh * 4 + y) * 2 + c
    chunk = LIVE // 8
    width = residual.shape[1]
    quarter = width // 4
    model = 8 * width

    every = jnp.arange(ranks, dtype=jnp.int32)

    def starts(which):
        return jnp.sum(jnp.where(every < which[..., None], rank_tokens, 0), axis=-1)

    def lengths(which):
        return jnp.sum(jnp.where(every == which[..., None], rank_tokens, 0), axis=-1)

    own_start, own_length = starts(rank), lengths(rank)
    slot = jnp.arange(slots, dtype=jnp.int32)

    share = slots // 4
    latents = lax.dynamic_slice_in_dim(latent, x_at * share, share, 0)
    latents = gather(gather(latents, ("zh", "y")), "x").reshape(-1, latent.shape[1])
    latents_other = shifted(latents, "c", 1)

    weights = score_weights(
        rank_tokens, query_nope, query_rope, latent, key_rope, key_up, request_ids
    )
    weights = gather(gather(weights, "zh"), "y").reshape(-1, weights.shape[1])
    weights_other = shifted(weights, "c", 1)

    first, count = starts(every).reshape(4, 4, 2), rank_tokens.reshape(4, 4, 2)
    to = jnp.where(slot < count[..., None], first[..., None] + slot, -1)
    to = jnp.where(c == 0, jnp.stack([to[:, :, 0], to[:, :, 1]]), jnp.stack([to[:, :, 1], to[:, :, 0]]))
    goes = to.transpose(0, 2, 1, 3).reshape(2, 1, -1)
    goes_latent = to.reshape(2, 4, 4, 4, share).transpose(0, 3, 1, 2, 4).reshape(2, 1, -1)
    values = live_values(goes_latent, latents, latents_other, value_up)

    eight = jnp.arange(8, dtype=jnp.int32)
    spread = ((eight[:, None] - own_start) & 7) + 8 * eight[None, :]
    roll = (spread.reshape(slots, 1) == slot[None, :]).astype(BF)
    rows = dot(roll, residual).astype(BF).reshape(2, 4, 8, 2, 2, quarter)
    rows = rows.transpose(1, 0, 3, 4, 2, 5).reshape(ranks, 8, quarter)
    rows = exchange(rows, DP)
    mine = (y >> 1) * 4 + zh
    place = ((mine - starts(every)[:, None]) & 7) + 8 * eight[None, :]
    come = jnp.where(place < rank_tokens[:, None], (starts(every)[:, None] + place) >> 3, -1)
    come = (come.reshape(ranks * 8, 1) == jnp.arange(chunk, dtype=jnp.int32)).astype(BF)
    rows = lax.dot_general(
        rows.reshape(ranks * 8, quarter), come, (((0,), (0,)), ((), ())), preferred_element_type=F32
    )

    weights_other, rows = lax.optimization_barrier((weights_other, rows))
    part = mix_project(goes, weights, weights_other, values, output_weight.T)
    projected = jnp.sum(exchange(part, HD).astype(F32), axis=0).astype(BF)
    sends = []
    for a in range(4):
        for b in range(4):
            for e in range(2):
                for f in range(4):
                    for g in range(2):
                        m = f * 2 + g
                        to = ((m & 3) * 4 + (m >> 2) * 2 + (b & 1)) * 2 + e
                        h = a * 2 + (b >> 1)
                        sends.append((((a * 4 + b) * 2 + e) * 8 + m, to * 8 + h))
    projected = lax.ppermute(projected, DP + HD, sends)
    mixed = (rows + projected.astype(F32)).astype(BF)

    full = gather(gather(mixed, "zh"), "y").reshape(2, 2, 4, quarter, chunk)
    full_other = shifted(full, "c", 1)
    ff = down_weight.shape[0]
    part = gate_up(full, full_other, norm_gain[:, None], gate_weight.T, up_weight.T)
    total = jnp.sum(exchange(part, HD).astype(F32), axis=0)
    scale = lax.rsqrt((total[2 * ff : 2 * ff + 1] + total[2 * ff + 1 : 2 * ff + 2]) / model + 1e-06)
    hidden = (jax.nn.silu(total[:ff] * scale) * (total[ff : 2 * ff] * scale)).astype(BF)
    hidden = gather(hidden, HD).reshape(4, 2, ff, chunk)

    def down(core):
        piece = lax.dynamic_index_in_dim(hidden, core, 1, keepdims=False)
        return lax.dot_general(
            piece, down_weight, (((1,), (0,)), ((), ())), preferred_element_type=F32
        )

    sent = shifted(down(1 - c).astype(BF), "c", 1)
    total = (down(c) + sent.astype(F32)).astype(BF)
    total = jnp.sum(exchange(total, "y").astype(F32), axis=0)
    m = y * 2 + c
    first = starts(every)
    place = ((m - first[:, None]) & 7) + 8 * eight[None, :]
    comes = jnp.where(place < rank_tokens[:, None], (first[:, None] + place) >> 3, -1)
    expand = (comes.reshape(4, slots, 1) == jnp.arange(chunk, dtype=jnp.int32)).astype(BF)
    planes = dot(expand.reshape(4 * slots, chunk), total.astype(BF)).astype(BF)
    pair = [pick(a.reshape(2, 2, 4, quarter, chunk), m >> 2) for a in (full, full_other)]
    pair = [lax.dynamic_index_in_dim(a, m & 3, 1, keepdims=False) for a in pair]
    low = jnp.where(c == 0, pair[0], pair[1])
    high = jnp.where(c == 0, pair[1], pair[0])
    own = jnp.stack([low, high], axis=1).reshape(width, chunk)
    result = nt(pick(expand, zh), own)
    result = result + jnp.sum(exchange(planes.reshape(4, slots, width), "zh").astype(F32), axis=0)
    result = exchange(result.astype(BF).reshape(8, 8, width), ("y", "c"))
    at = ((own_start + slot) & 7) * 8 + (slot >> 3)
    at = jnp.where(slot < own_length, at, -1)
    back = (at[:, None] == slot[None, :]).astype(BF)
    return dot(back, result.reshape(slots, width)).astype(BF)


def solution(mesh):
    mesh = Mesh(mesh.devices.reshape(4, 4, 2, 4, 2), DP + HD)
    in_specs = (
        P(DP, HD),
        P(DP, HD),
        P(DP, None),
        P(DP, None),
        P(None, HD),
        P(None, HD),
        P(HD, DP),
        P(DP, HD),
        P(HD),
        P(HD, DP),
        P(HD, DP),
        P(DP, HD),
        P(),
        P(DP, None),
    )
    return jax.shard_map(
        on_device, mesh=mesh, in_specs=in_specs, out_specs=P(DP, HD), check_vma=False
    )
```

```python
import jax
import jax.numpy as jnp
from jax import lax
from jax.experimental import pallas as pl
from jax.experimental.pallas import tpu as pltpu
from jax.sharding import Mesh, PartitionSpec as P

BF = jnp.bfloat16
F32 = jnp.float32
NOPE = 128
ROPE = 64
VH = 128
WIN = 32
LIVE = 1024
BLK = 128
STEP = 256
DP = ("zh", "y", "c")
HD = ("x", "zl")


def dot(a, b):
    return jnp.dot(a, b, preferred_element_type=F32)


def shifted(x, axis, shift):
    n = lax.axis_size(axis)
    return lax.ppermute(x, axis, [(i, (i + shift) % n) for i in range(n)])


def iota(shape, dim):
    return lax.broadcasted_iota(jnp.int32, shape, dim)


def nt(a, b):
    return lax.dot_general(a, b, (((1,), (1,)), ((), ())), preferred_element_type=F32)


def whole(shape):
    return pl.BlockSpec(shape, lambda *_: (0,) * len(shape), pipeline_mode=pl.Buffered(1))


def cost(us):
    return pl.CostEstimate(flops=us * 10**9, bytes_accessed=us * 3 * 10**6, transcendentals=0)


def score_kernel(counts_ref, qn_ref, qr_ref, lat_ref, kr_ref, ku_ref, req_ref, out_ref, s_ref):
    slots = lat_ref.shape[0]
    heads = ku_ref.shape[1] // NOPE
    place = (lax.axis_index("zh") * 4 + lax.axis_index("y")) * 2 + lax.axis_index("c")
    before = lax.fori_loop(
        0,
        counts_ref.shape[0],
        lambda i, a: a + jnp.where(i < place, counts_ref[i], 0),
        jnp.int32(0),
    )
    keys = dot(lat_ref[...], ku_ref[...]).astype(BF)
    key_rope = kr_ref[...]
    s_at, t_at = iota((slots, slots), 0), iota((slots, slots), 1)
    across = jnp.broadcast_to(req_ref[...], (slots, slots))
    down = jnp.sum(jnp.where(s_at == t_at, across, 0), axis=1, keepdims=True)
    allowed = (across == down) & (t_at <= s_at)
    t_row, lane = iota((slots, BLK), 0), iota((slots, BLK), 1)
    lands = ((before + t_row) & (WIN - 1)) == (lane & (WIN - 1))
    per = BLK // WIN
    for h in range(heads):
        rows = slice(h * slots, (h + 1) * slots)
        s = nt(qn_ref[:, h * NOPE : (h + 1) * NOPE], keys[:, h * NOPE : (h + 1) * NOPE])
        s = s + nt(qr_ref[:, h * ROPE : (h + 1) * ROPE], key_rope)
        s_ref[rows, :] = jnp.where(allowed, s * (NOPE + ROPE) ** (-0.5), jnp.float32(-1e30))
    s = s_ref[...]
    raised = jnp.exp(s - jnp.max(s, axis=-1, keepdims=True))
    w = (raised / jnp.sum(raised, axis=-1, keepdims=True)).astype(BF)
    folded = dot(w, jnp.where(lands, 1.0, 0.0).astype(BF))
    for group in range(heads // per):
        out = folded[group * per * slots : (group * per + 1) * slots]
        for i in range(1, per):
            h = group * per + i
            out = jnp.where((lane >> 5) == i, folded[h * slots : (h + 1) * slots], out)
        out_ref[:, group * BLK : (group + 1) * BLK] = out.astype(BF)


def score_weights(counts, *arrays):
    slots, heads = arrays[2].shape[0], arrays[4].shape[1] // NOPE
    shape = (slots, heads * WIN)
    return pl.pallas_call(
        score_kernel,
        grid=(1,),
        out_shape=jax.ShapeDtypeStruct(shape, BF),
        in_specs=[pl.BlockSpec(memory_space=pltpu.SMEM)] + [whole(a.shape) for a in arrays],
        out_specs=whole(shape),
        scratch_shapes=[pltpu.VMEM((slots * heads, slots), F32)],
        cost_estimate=cost(4),
        name="score_weights",
    )(counts, *arrays)


def live_rows(goes_ref, own_ref, other_ref):
    row = iota((STEP, own_ref.shape[0]), 0) + pl.program_id(0) * STEP
    out = dot(jnp.where(goes_ref[0] == row, 1.0, 0.0).astype(BF), own_ref[...])
    out = out + dot(jnp.where(goes_ref[1] == row, 1.0, 0.0).astype(BF), other_ref[...])
    return out.astype(BF)


def values_kernel(goes_ref, own_ref, other_ref, up_ref, out_ref):
    out_ref[...] = dot(live_rows(goes_ref, own_ref, other_ref), up_ref[...]).astype(BF)


def live_values(goes, own, other, up):
    width = up.shape[1]
    return pl.pallas_call(
        values_kernel,
        grid=(LIVE // STEP,),
        out_shape=jax.ShapeDtypeStruct((LIVE, width), BF),
        in_specs=[whole(a.shape) for a in (goes, own, other, up)],
        out_specs=pl.BlockSpec((STEP, width), lambda b: (b, 0)),
        cost_estimate=cost(6),
        name="live_values",
    )(goes, own, other, up)


def mix_kernel(goes_ref, own_ref, other_ref, prev_ref, cur_ref, wo_ref, out_ref, att_ref, all_ref):
    b = pl.program_id(0)
    heads = cur_ref.shape[1] // VH
    r_at, l_at = iota((BLK, BLK), 0), iota((BLK, BLK), 1)
    gap = r_at - l_at
    near = (gap >= 0) & (gap < WIN)
    per = BLK // WIN
    masks = [jnp.where(near & ((l_at >> 5) == q), 1.0, 0.0).astype(BF) for q in range(per)]
    r_at, l_at = iota((WIN, BLK), 0), iota((WIN, BLK), 1)
    before = jnp.where((BLK + r_at - l_at) < WIN, 1.0, 0.0).astype(BF)
    blank = jnp.zeros((BLK, BLK), BF)
    packed = live_rows(goes_ref, own_ref, other_ref)
    for group in range(heads // per):
        one = packed[:, group * BLK : (group + 1) * BLK].astype(F32)
        turned = [one.astype(BF)]
        for q in range(1, per):
            turned.append(pltpu.roll(one, q * WIN, 1).astype(BF))
        for i in range(per):
            cols = slice((group * per + i) * VH, (group * per + i + 1) * VH)
            bands = []
            for rows in (slice(0, BLK), slice(BLK, STEP)):
                band = turned[(-i) % per][rows] * masks[0]
                for q in range(1, per):
                    band = band + turned[(q - i) % per][rows] * masks[q]
                bands.append(band)
            last = turned[(per - 1 - i) % per]
            corner = jnp.concatenate([last[BLK : BLK + WIN] * before, blank[WIN:]], axis=0)
            band = jnp.concatenate(
                [
                    jnp.concatenate([bands[0], blank], axis=1),
                    jnp.concatenate([corner, bands[1]], axis=1),
                ],
                axis=0,
            )
            att = dot(band, cur_ref[:, cols])
            old = dot(last[:WIN] * before, prev_ref[:, cols])
            att_ref[:WIN, cols] = (att[:WIN] + old).astype(BF)
            att_ref[WIN:, cols] = att[WIN:].astype(BF)
    part = nt(att_ref[...], wo_ref[...]).astype(BF)
    share = STEP // 8
    r_at, l_at = iota((STEP, STEP), 0), iota((STEP, STEP), 1)
    order = ((r_at & (share - 1)) * 8 + (r_at >> 5)) == l_at
    part = dot(jnp.where(order, 1.0, 0.0).astype(BF), part)
    rows = pl.ds(pl.multiple_of(b * share, share), share)
    for m in range(8):
        all_ref[m, rows, :] = part[m * share : (m + 1) * share]

    @pl.when(b == pl.num_programs(0) - 1)
    def _():
        for m in range(8):
            out_ref[m] = all_ref[m].T.astype(BF)


def mix_project(goes, own, other, values, wo):
    width = values.shape[1]
    n = wo.shape[0]
    shape = (8, n, LIVE // 8)
    return pl.pallas_call(
        mix_kernel,
        grid=(LIVE // STEP,),
        out_shape=jax.ShapeDtypeStruct(shape, BF),
        in_specs=[
            whole(goes.shape),
            whole(own.shape),
            whole(other.shape),
            pl.BlockSpec((BLK, width), lambda b: (jnp.maximum(b * (STEP // BLK) - 1, 0), 0)),
            pl.BlockSpec((STEP, width), lambda b: (b, 0)),
            whole(wo.shape),
        ],
        out_specs=whole(shape),
        scratch_shapes=[pltpu.VMEM((STEP, width), BF), pltpu.VMEM((8, LIVE // 8, n), F32)],
        cost_estimate=cost(9),
        name="mix_project",
    )(goes, own, other, values, values, wo)


def gate_up_kernel(own_ref, other_ref, gain_ref, gate_ref, up_ref, out_ref, x_ref):
    core = lax.axis_index("c")
    _, lows, blocks, k, chunk = own_ref.shape
    ff = gate_ref.shape[0]
    squares = jnp.zeros((1, blocks * chunk), F32)
    for ref, flip in ((own_ref, core), (other_ref, 1 - core)):
        for low in range(lows):
            rows = pl.ds(pl.multiple_of((low * 2 + flip) * k, 32), k)
            x = jnp.concatenate([ref[0, low, i] for i in range(blocks)], axis=1).astype(F32)
            squares = squares + jnp.sum(x * x, axis=0, keepdims=True)
            x_ref[rows, :] = (x * gain_ref[rows, :]).astype(BF)
    x = x_ref[...]
    gate = dot(gate_ref[...], x).astype(BF)
    up = dot(up_ref[...], x).astype(BF)
    row = iota((16, blocks * chunk), 0)
    high = squares.astype(BF).astype(F32)
    extra = jnp.where(row == 0, high, jnp.where(row == 1, squares - high, 0.0)).astype(BF)
    for i in range(blocks):
        cols = slice(i * chunk, (i + 1) * chunk)
        out_ref[i, :ff, :] = gate[:, cols]
        out_ref[i, ff : 2 * ff, :] = up[:, cols]
        out_ref[i, 2 * ff :, :] = extra[:, cols]


def gate_up(own, other, gain, gate_weight, up_weight):
    highs, lows, planes, k, chunk = own.shape
    ff, width = gate_weight.shape
    blocks = 2
    spec = pl.BlockSpec(
        (1, lows, blocks, k, chunk),
        lambda b: (b // (planes // blocks), 0, b % (planes // blocks), 0, 0),
    )
    return pl.pallas_call(
        gate_up_kernel,
        grid=(highs * planes // blocks,),
        out_shape=jax.ShapeDtypeStruct((highs * planes, 2 * ff + 16, chunk), BF),
        in_specs=[spec, spec, whole((width, 1)), whole((ff, width)), whole((ff, width))],
        out_specs=pl.BlockSpec((blocks, 2 * ff + 16, chunk), lambda b: (b, 0, 0)),
        scratch_shapes=[pltpu.VMEM((width, blocks * chunk), BF)],
        cost_estimate=cost(6),
        name="gate_up",
    )(own, other, gain, gate_weight, up_weight)


def exchange(x, axes):
    return lax.all_to_all(x, axes, split_axis=0, concat_axis=0, tiled=True)


def gather(x, axes):
    n = lax.axis_size(axes)
    return exchange(jnp.broadcast_to(x[None], (n,) + x.shape), axes)


def pick(x, index):
    return lax.dynamic_index_in_dim(x, index, 0, keepdims=False)


def on_device(
    query_nope,
    query_rope,
    latent,
    key_rope,
    key_up,
    value_up,
    output_weight,
    residual,
    norm_gain,
    gate_weight,
    up_weight,
    down_weight,
    rank_tokens,
    request_ids,
):
    slots = latent.shape[0]
    ranks = rank_tokens.shape[0]
    zh, y, c = (lax.axis_index(a) for a in DP)
    x_at, zl = (lax.axis_index(a) for a in HD)
    rank = (zh * 4 + y) * 2 + c
    chunk = LIVE // 8
    width = residual.shape[1]
    quarter = width // 4
    model = 8 * width

    every = jnp.arange(ranks, dtype=jnp.int32)

    def starts(which):
        return jnp.sum(jnp.where(every < which[..., None], rank_tokens, 0), axis=-1)

    def lengths(which):
        return jnp.sum(jnp.where(every == which[..., None], rank_tokens, 0), axis=-1)

    own_start, own_length = starts(rank), lengths(rank)
    slot = jnp.arange(slots, dtype=jnp.int32)

    share = slots // 4
    half = width // 2
    eight = jnp.arange(8, dtype=jnp.int32)
    spread = ((eight[:, None] - own_start) & 7) + 8 * eight[None, :]
    roll = (spread.reshape(slots, 1) == slot[None, :]).astype(BF)
    rows = dot(roll, residual).astype(BF).reshape(2, 4, 8, width)
    pad = ((0, 0),) * 3 + ((0, latent.shape[1] - half),)
    rows = jnp.stack([jnp.pad(rows[..., :half], pad), jnp.pad(rows[..., half:], pad)], axis=1)
    rows = rows.transpose(2, 0, 1, 3, 4).reshape(16, 8, latent.shape[1])
    latents = lax.dynamic_slice_in_dim(latent, x_at * share, share, 0)
    latents = jnp.broadcast_to(latents[None], (16,) + latents.shape)
    got = exchange(jnp.concatenate([latents, rows], axis=1), ("zh", "y"))

    weights = score_weights(
        rank_tokens, query_nope, query_rope, latent, key_rope, key_up, request_ids
    )
    weights = gather(gather(weights, "zh"), "y").reshape(-1, weights.shape[1])
    weights_other = shifted(weights, "c", 1)

    latents = got[:, :share].reshape(-1, latent.shape[1])
    latents = jnp.concatenate([latents] + [shifted(latents, "x", s) for s in (1, 2, 3)], axis=0)
    latents_other = shifted(latents, "c", 1)

    def by_core(a):
        a = a.reshape(4, 4, 2)
        return jnp.where(c == 0, jnp.stack([a[..., 0], a[..., 1]]), jnp.stack([a[..., 1], a[..., 0]]))

    first, count = by_core(starts(every)), by_core(rank_tokens)
    goes = jnp.swapaxes(first, 1, 2)[..., None] + slot
    goes = jnp.where(slot < jnp.swapaxes(count, 1, 2)[..., None], goes, -1).reshape(2, 1, -1)
    block = (x_at - jnp.arange(4, dtype=jnp.int32)) & 3
    own_slot = (block[:, None] * share + jnp.arange(share, dtype=jnp.int32)).reshape(1, 4, 1, 1, share)
    goes_latent = first[:, None, :, :, None] + own_slot
    goes_latent = jnp.where(own_slot < count[:, None, :, :, None], goes_latent, -1).reshape(2, 1, -1)
    values = live_values(goes_latent, latents, latents_other, value_up)

    mine = (y >> 1) * 4 + zh
    place = ((mine - first[..., None]) & 7) + 8 * eight
    come = jnp.where(place < count[..., None], (first[..., None] + place) >> 3, -1)
    come = (come.reshape(2, -1, 1) == jnp.arange(chunk, dtype=jnp.int32)).astype(BF)
    rows = got[:, share:].reshape(-1, latent.shape[1])
    left, right = rows[:, :quarter], rows[:, quarter:half]
    kept = jnp.where(c == 0, left, right)
    rows = shifted(jnp.where(c == 0, right, left), "c", 1)

    def tn(a, b):
        return lax.dot_general(a, b, (((0,), (0,)), ((), ())), preferred_element_type=F32)

    rows = tn(kept, come[0]) + tn(rows, come[1])

    weights_other, rows = lax.optimization_barrier((weights_other, rows))
    part = mix_project(goes, weights, weights_other, values, output_weight.T)
    projected = jnp.sum(exchange(part, HD).astype(F32), axis=0).astype(BF)
    sends = []
    for a in range(4):
        for b in range(4):
            for e in range(2):
                for f in range(4):
                    for g in range(2):
                        m = f * 2 + g
                        to = ((m & 3) * 4 + (m >> 2) * 2 + (b & 1)) * 2 + e
                        h = a * 2 + (b >> 1)
                        sends.append((((a * 4 + b) * 2 + e) * 8 + m, to * 8 + h))
    projected = lax.ppermute(projected, DP + HD, sends)
    mixed = (rows + projected.astype(F32)).astype(BF)

    full = gather(gather(mixed, "zh"), "y").reshape(2, 2, 4, quarter, chunk)
    full_other = shifted(full, "c", 1)
    ff = down_weight.shape[0]
    part = gate_up(full, full_other, norm_gain[:, None], gate_weight.T, up_weight.T)
    total = jnp.sum(exchange(part, HD).astype(F32), axis=0)
    scale = lax.rsqrt((total[2 * ff : 2 * ff + 1] + total[2 * ff + 1 : 2 * ff + 2]) / model + 1e-06)
    hidden = (jax.nn.silu(total[:ff] * scale) * (total[ff : 2 * ff] * scale)).astype(BF)
    hidden = gather(hidden, HD).reshape(4, 2, ff, chunk)

    def down(core):
        piece = lax.dynamic_index_in_dim(hidden, core, 1, keepdims=False)
        return lax.dot_general(
            piece, down_weight, (((1,), (0,)), ((), ())), preferred_element_type=F32
        )

    sent = shifted(down(1 - c).astype(BF), "c", 1)
    total = (down(c) + sent.astype(F32)).astype(BF)
    total = jnp.sum(exchange(total, "y").astype(F32), axis=0)
    m = y * 2 + c
    begin = starts(every)
    place = ((m - begin[:, None]) & 7) + 8 * eight[None, :]
    comes = jnp.where(place < rank_tokens[:, None], (begin[:, None] + place) >> 3, -1)
    expand = (comes.reshape(ranks * 8, 1) == jnp.arange(chunk, dtype=jnp.int32)).astype(BF)
    pair = [pick(a.reshape(2, 2, 4, quarter, chunk), m >> 2) for a in (full, full_other)]
    pair = [lax.dynamic_index_in_dim(a, m & 3, 1, keepdims=False) for a in pair]
    low = jnp.where(c == 0, pair[0], pair[1])
    high = jnp.where(c == 0, pair[1], pair[0])
    own = jnp.stack([low, high], axis=1).reshape(width, chunk)
    here = (jnp.arange(ranks * 8, dtype=jnp.int32) >> 6) == zh
    own = nt(jnp.where(here[:, None], expand, jnp.zeros_like(expand)), own)
    result = (dot(expand, total.astype(BF)) + own).astype(BF).reshape(ranks, 8, width)
    result = jnp.sum(exchange(result, DP).reshape(4, slots, width).astype(F32), axis=0).astype(BF)
    at = ((own_start + slot) & 7) * 8 + (slot >> 3)
    at = jnp.where(slot < own_length, at, -1)
    back = (at[:, None] == slot[None, :]).astype(BF)
    return dot(back, result).astype(BF)


def solution(mesh):
    mesh = Mesh(mesh.devices.reshape(4, 4, 2, 4, 2), DP + HD)
    in_specs = (
        P(DP, HD),
        P(DP, HD),
        P(DP, None),
        P(DP, None),
        P(None, HD),
        P(None, HD),
        P(HD, DP),
        P(DP, HD),
        P(HD),
        P(HD, DP),
        P(HD, DP),
        P(DP, HD),
        P(),
        P(DP, None),
    )
    return jax.shard_map(
        on_device, mesh=mesh, in_specs=in_specs, out_specs=P(DP, HD), check_vma=False
    )
```

```python
import jax
import jax.numpy as jnp
from jax import lax
from jax.experimental import pallas as pl
from jax.experimental.pallas import tpu as pltpu
from jax.sharding import Mesh, PartitionSpec as P

BF = jnp.bfloat16
F32 = jnp.float32
NOPE = 128
ROPE = 64
VH = 128
WIN = 32
LIVE = 1024
BLK = 128
STEP = 256
DP = ("zh", "y", "c")
HD = ("x", "zl")


def dot(a, b):
    return jnp.dot(a, b, preferred_element_type=F32)


def shifted(x, axis, shift):
    n = lax.axis_size(axis)
    return lax.ppermute(x, axis, [(i, (i + shift) % n) for i in range(n)])


def iota(shape, dim):
    return lax.broadcasted_iota(jnp.int32, shape, dim)


def nt(a, b):
    return lax.dot_general(a, b, (((1,), (1,)), ((), ())), preferred_element_type=F32)


def whole(shape):
    return pl.BlockSpec(shape, lambda *_: (0,) * len(shape), pipeline_mode=pl.Buffered(1))


def cost(us):
    return pl.CostEstimate(flops=us * 10**9, bytes_accessed=us * 3 * 10**6, transcendentals=0)


def rank_here():
    return (lax.axis_index("zh") * 4 + lax.axis_index("y")) * 2 + lax.axis_index("c")


def live_before(counts_ref):
    place = rank_here()
    return lax.fori_loop(
        0,
        counts_ref.shape[0],
        lambda i, a: a + jnp.where(i < place, counts_ref[i], 0),
        jnp.int32(0),
    )


def pack_kernel(counts_ref, lat_ref, res_ref, *refs):
    outs, rows_ref = refs[:4], refs[4]
    slots, width = res_ref.shape
    half, lanes = width // 2, lat_ref.shape[1]
    zh = lax.axis_index("zh")
    start = live_before(counts_ref)
    i_at, slot = iota((slots, slots), 0), iota((slots, slots), 1)
    roll = ((((i_at >> 3) - start) & 7) + 8 * (i_at & 7)) == slot
    rows_ref[...] = dot(jnp.where(roll, 1.0, 0.0).astype(BF), res_ref[...])
    fill = jnp.zeros((16, lanes - half), F32)
    for s in range(4):
        outs[s][:slots, :] = lat_ref[...]
        for high in range(2):
            m = ((zh + s) & 3) * 2 + high
            piece = rows_ref[pl.ds(pl.multiple_of(m * 8, 8), 8), :]
            piece = jnp.concatenate([piece[:, :half], piece[:, half:]], axis=0)
            piece = jnp.concatenate([piece, fill], axis=1)
            outs[s][slots + 16 * high : slots + 16 * (high + 1), :] = piece.astype(BF)


def pack(counts, latent, residual):
    slots, lanes = latent.shape
    shape = (slots + 32, lanes)
    return pl.pallas_call(
        pack_kernel,
        grid=(1,),
        out_shape=[jax.ShapeDtypeStruct(shape, BF)] * 4,
        in_specs=[
            pl.BlockSpec(memory_space=pltpu.SMEM),
            whole(latent.shape),
            whole(residual.shape),
        ],
        out_specs=[whole(shape)] * 4,
        scratch_shapes=[pltpu.VMEM(residual.shape, F32)],
        cost_estimate=cost(2),
        name="pack",
    )(counts, latent, residual)


def repack_kernel(*refs):
    ins, outs, rows_ref = refs[:4], refs[4:8], refs[8]
    slots = ins[0].shape[0] - 32
    y = lax.axis_index("y")
    for t in range(4):
        rows_ref[t] = ins[t][slots:, :].astype(F32)
    for s in range(4):
        at = pl.ds(pl.multiple_of(((y + s) & 3) * 8, 8), 8)
        for t in range(4):
            outs[s][t * slots : (t + 1) * slots, :] = ins[t][:slots, :]
        for t in (0, 2):
            pair = jnp.concatenate([rows_ref[t, at, :], rows_ref[t + 1, at, :]], axis=0)
            outs[s][4 * slots + 8 * t : 4 * slots + 8 * t + 16, :] = pair.astype(BF)


def repack(*pieces):
    rows, lanes = pieces[0].shape
    shape = (4 * (rows - 32) + 32, lanes)
    return pl.pallas_call(
        repack_kernel,
        grid=(1,),
        out_shape=[jax.ShapeDtypeStruct(shape, BF)] * 4,
        in_specs=[whole(pieces[0].shape)] * 4,
        out_specs=[whole(shape)] * 4,
        scratch_shapes=[pltpu.VMEM((4, 32, lanes), F32)],
        cost_estimate=cost(2),
        name="repack",
    )(*pieces)


def score_kernel(counts_ref, qn_ref, qr_ref, lat_ref, kr_ref, ku_ref, req_ref, out_ref, s_ref):
    slots = lat_ref.shape[0]
    heads = ku_ref.shape[1] // NOPE
    before = live_before(counts_ref)
    keys = dot(lat_ref[...], ku_ref[...]).astype(BF)
    key_rope = kr_ref[...]
    s_at, t_at = iota((slots, slots), 0), iota((slots, slots), 1)
    across = jnp.broadcast_to(req_ref[...], (slots, slots))
    down = jnp.sum(jnp.where(s_at == t_at, across, 0), axis=1, keepdims=True)
    allowed = (across == down) & (t_at <= s_at)
    t_row, lane = iota((slots, BLK), 0), iota((slots, BLK), 1)
    lands = ((before + t_row) & (WIN - 1)) == (lane & (WIN - 1))
    per = BLK // WIN
    for h in range(heads):
        rows = slice(h * slots, (h + 1) * slots)
        s = nt(qn_ref[:, h * NOPE : (h + 1) * NOPE], keys[:, h * NOPE : (h + 1) * NOPE])
        s = s + nt(qr_ref[:, h * ROPE : (h + 1) * ROPE], key_rope)
        s_ref[rows, :] = jnp.where(allowed, s * (NOPE + ROPE) ** (-0.5), jnp.float32(-1e30))
    s = s_ref[...]
    raised = jnp.exp(s - jnp.max(s, axis=-1, keepdims=True))
    w = (raised / jnp.sum(raised, axis=-1, keepdims=True)).astype(BF)
    folded = dot(w, jnp.where(lands, 1.0, 0.0).astype(BF))
    for group in range(heads // per):
        out = folded[group * per * slots : (group * per + 1) * slots]
        for i in range(1, per):
            h = group * per + i
            out = jnp.where((lane >> 5) == i, folded[h * slots : (h + 1) * slots], out)
        out_ref[:, group * BLK : (group + 1) * BLK] = out.astype(BF)


def score_weights(counts, *arrays):
    slots, heads = arrays[2].shape[0], arrays[4].shape[1] // NOPE
    shape = (slots, heads * WIN)
    return pl.pallas_call(
        score_kernel,
        grid=(1,),
        out_shape=jax.ShapeDtypeStruct(shape, BF),
        in_specs=[pl.BlockSpec(memory_space=pltpu.SMEM)] + [whole(a.shape) for a in arrays],
        out_specs=whole(shape),
        scratch_shapes=[pltpu.VMEM((slots * heads, slots), F32)],
        cost_estimate=cost(4),
        name="score_weights",
    )(counts, *arrays)


def live_rows(goes_ref, own_ref, other_ref):
    row = iota((STEP, own_ref.shape[0]), 0) + pl.program_id(0) * STEP
    out = dot(jnp.where(goes_ref[0] == row, 1.0, 0.0).astype(BF), own_ref[...])
    out = out + dot(jnp.where(goes_ref[1] == row, 1.0, 0.0).astype(BF), other_ref[...])
    return out.astype(BF)


def values_kernel(goes_ref, own_ref, other_ref, up_ref, out_ref):
    out_ref[...] = dot(live_rows(goes_ref, own_ref, other_ref), up_ref[...]).astype(BF)


def live_values(goes, own, other, up):
    width = up.shape[1]
    return pl.pallas_call(
        values_kernel,
        grid=(LIVE // STEP,),
        out_shape=jax.ShapeDtypeStruct((LIVE, width), BF),
        in_specs=[whole(a.shape) for a in (goes, own, other, up)],
        out_specs=pl.BlockSpec((STEP, width), lambda b: (b, 0)),
        cost_estimate=cost(6),
        name="live_values",
    )(goes, own, other, up)


def mix_kernel(goes_ref, own_ref, other_ref, prev_ref, cur_ref, wo_ref, out_ref, att_ref, all_ref):
    b = pl.program_id(0)
    heads = cur_ref.shape[1] // VH
    r_at, l_at = iota((BLK, BLK), 0), iota((BLK, BLK), 1)
    gap = r_at - l_at
    near = (gap >= 0) & (gap < WIN)
    per = BLK // WIN
    masks = [jnp.where(near & ((l_at >> 5) == q), 1.0, 0.0).astype(BF) for q in range(per)]
    r_at, l_at = iota((WIN, BLK), 0), iota((WIN, BLK), 1)
    before = jnp.where((BLK + r_at - l_at) < WIN, 1.0, 0.0).astype(BF)
    blank = jnp.zeros((BLK, BLK), BF)
    packed = live_rows(goes_ref, own_ref, other_ref)
    for group in range(heads // per):
        one = packed[:, group * BLK : (group + 1) * BLK].astype(F32)
        turned = [one.astype(BF)]
        for q in range(1, per):
            turned.append(pltpu.roll(one, q * WIN, 1).astype(BF))
        for i in range(per):
            cols = slice((group * per + i) * VH, (group * per + i + 1) * VH)
            bands = []
            for rows in (slice(0, BLK), slice(BLK, STEP)):
                band = turned[(-i) % per][rows] * masks[0]
                for q in range(1, per):
                    band = band + turned[(q - i) % per][rows] * masks[q]
                bands.append(band)
            last = turned[(per - 1 - i) % per]
            corner = jnp.concatenate([last[BLK : BLK + WIN] * before, blank[WIN:]], axis=0)
            band = jnp.concatenate(
                [
                    jnp.concatenate([bands[0], blank], axis=1),
                    jnp.concatenate([corner, bands[1]], axis=1),
                ],
                axis=0,
            )
            att = dot(band, cur_ref[:, cols])
            old = dot(last[:WIN] * before, prev_ref[:, cols])
            att_ref[:WIN, cols] = (att[:WIN] + old).astype(BF)
            att_ref[WIN:, cols] = att[WIN:].astype(BF)
    part = nt(att_ref[...], wo_ref[...]).astype(BF)
    share = STEP // 8
    r_at, l_at = iota((STEP, STEP), 0), iota((STEP, STEP), 1)
    order = ((r_at & (share - 1)) * 8 + (r_at >> 5)) == l_at
    part = dot(jnp.where(order, 1.0, 0.0).astype(BF), part)
    rows = pl.ds(pl.multiple_of(b * share, share), share)
    for m in range(8):
        all_ref[m, rows, :] = part[m * share : (m + 1) * share]

    @pl.when(b == pl.num_programs(0) - 1)
    def _():
        for m in range(8):
            out_ref[m] = all_ref[m].T.astype(BF)


def mix_project(goes, own, other, values, wo):
    width = values.shape[1]
    n = wo.shape[0]
    shape = (8, n, LIVE // 8)
    return pl.pallas_call(
        mix_kernel,
        grid=(LIVE // STEP,),
        out_shape=jax.ShapeDtypeStruct(shape, BF),
        in_specs=[
            whole(goes.shape),
            whole(own.shape),
            whole(other.shape),
            pl.BlockSpec((BLK, width), lambda b: (jnp.maximum(b * (STEP // BLK) - 1, 0), 0)),
            pl.BlockSpec((STEP, width), lambda b: (b, 0)),
            whole(wo.shape),
        ],
        out_specs=whole(shape),
        scratch_shapes=[pltpu.VMEM((STEP, width), BF), pltpu.VMEM((8, LIVE // 8, n), F32)],
        cost_estimate=cost(9),
        name="mix_project",
    )(goes, own, other, values, values, wo)


def gate_up_kernel(own_ref, other_ref, gain_ref, gate_ref, up_ref, out_ref, x_ref, gain_at):
    core = lax.axis_index("c")
    _, lows, blocks, k, chunk = own_ref.shape
    ff = gate_ref.shape[0]
    squares = jnp.zeros((1, blocks * chunk), F32)
    gain_at[...] = jnp.broadcast_to(gain_ref[...], (8, gain_ref.shape[1])).T
    for ref, flip in ((own_ref, core), (other_ref, 1 - core)):
        for low in range(lows):
            rows = pl.ds(pl.multiple_of((low * 2 + flip) * k, 32), k)
            x = jnp.concatenate([ref[0, low, i] for i in range(blocks)], axis=1).astype(F32)
            squares = squares + jnp.sum(x * x, axis=0, keepdims=True)
            x_ref[rows, :] = (x * gain_at[rows, :1]).astype(BF)
    x = x_ref[...]
    gate = dot(gate_ref[...], x).astype(BF)
    up = dot(up_ref[...], x).astype(BF)
    row = iota((16, blocks * chunk), 0)
    high = squares.astype(BF).astype(F32)
    extra = jnp.where(row == 0, high, jnp.where(row == 1, squares - high, 0.0)).astype(BF)
    for i in range(blocks):
        cols = slice(i * chunk, (i + 1) * chunk)
        out_ref[i, :ff, :] = gate[:, cols]
        out_ref[i, ff : 2 * ff, :] = up[:, cols]
        out_ref[i, 2 * ff :, :] = extra[:, cols]


def gate_up(own, other, gain, gate_weight, up_weight):
    highs, lows, planes, k, chunk = own.shape
    ff, width = gate_weight.shape
    blocks = 2
    spec = pl.BlockSpec(
        (1, lows, blocks, k, chunk),
        lambda b: (b // (planes // blocks), 0, b % (planes // blocks), 0, 0),
    )
    return pl.pallas_call(
        gate_up_kernel,
        grid=(highs * planes // blocks,),
        out_shape=jax.ShapeDtypeStruct((highs * planes, 2 * ff + 16, chunk), BF),
        in_specs=[spec, spec, whole((1, width)), whole((ff, width)), whole((ff, width))],
        out_specs=pl.BlockSpec((blocks, 2 * ff + 16, chunk), lambda b: (b, 0, 0)),
        scratch_shapes=[pltpu.VMEM((width, blocks * chunk), BF), pltpu.VMEM((width, 8), F32)],
        cost_estimate=cost(6),
        name="gate_up",
    )(own, other, gain, gate_weight, up_weight)


def exchange(x, axes):
    return lax.all_to_all(x, axes, split_axis=0, concat_axis=0, tiled=True)


def gather(x, axes):
    n = lax.axis_size(axes)
    return exchange(jnp.broadcast_to(x[None], (n,) + x.shape), axes)


def pick(x, index):
    return lax.dynamic_index_in_dim(x, index, 0, keepdims=False)


def on_device(
    query_nope,
    query_rope,
    latent,
    key_rope,
    key_up,
    value_up,
    output_weight,
    residual,
    norm_gain,
    gate_weight,
    up_weight,
    down_weight,
    rank_tokens,
    request_ids,
):
    slots = latent.shape[0]
    ranks = rank_tokens.shape[0]
    zh, y, c = (lax.axis_index(a) for a in DP)
    rank = (zh * 4 + y) * 2 + c
    chunk = LIVE // 8
    width = residual.shape[1]
    quarter = width // 4
    model = 8 * width

    every = jnp.arange(ranks, dtype=jnp.int32)

    def starts(which):
        return jnp.sum(jnp.where(every < which[..., None], rank_tokens, 0), axis=-1)

    def lengths(which):
        return jnp.sum(jnp.where(every == which[..., None], rank_tokens, 0), axis=-1)

    own_start, own_length = starts(rank), lengths(rank)
    slot = jnp.arange(slots, dtype=jnp.int32)

    pieces = pack(rank_tokens, latent, residual)
    pieces = [pieces[0]] + [shifted(pieces[s], "zh", s) for s in (1, 2, 3)]

    weights = score_weights(
        rank_tokens, query_nope, query_rope, latent, key_rope, key_up, request_ids
    )
    weights = gather(weights, "zh")
    pieces = repack(*pieces)
    pieces = [pieces[0]] + [shifted(pieces[s], "y", s) for s in (1, 2, 3)]
    got = jnp.concatenate(pieces, axis=0)
    got_other = shifted(got, "c", 1)
    weights = gather(weights, "y").reshape(-1, weights.shape[2])

    four = jnp.arange(4, dtype=jnp.int32)
    eight = jnp.arange(8, dtype=jnp.int32)
    core = jnp.stack([c, 1 - c])[:, None, None]
    ahead = (four[None, None, :] * 4 + four[None, :, None]) * 2 + core
    goes = jnp.where(slot < lengths(ahead)[..., None], starts(ahead)[..., None] + slot, -1)
    goes = goes.reshape(2, 1, -1)
    back = (((zh - four) & 3)[None, None, :] * 4 + ((y - four) & 3)[None, :, None]) * 2 + core
    back_start, back_count = starts(back)[..., None], lengths(back)[..., None]
    goes_back = jnp.where(slot < back_count, back_start + slot, -1).reshape(2, 4, -1)
    goes_back = jnp.pad(goes_back, ((0, 0), (0, 0), (0, 32)), constant_values=-1).reshape(2, 1, -1)
    values = live_values(goes_back, got, got_other, value_up)

    swap = []
    for a in range(4):
        for b in range(8):
            for e in range(4):
                for f in range(2):
                    to = (e * 8 + (f * 4 + (b & 3))) * 8 + a * 2 + (b >> 2)
                    swap.append(((a * 8 + b) * 8 + e * 2 + f, to))
    place = (((zh * 2 + (y >> 1)) - back_start) & 7) + 8 * eight
    come = jnp.where(place < back_count, (back_start + place) >> 3, -1)
    come = (come.reshape(2, -1, 1) == jnp.arange(chunk, dtype=jnp.int32)).astype(BF)

    def tn(a, b):
        return lax.dot_general(a, b, (((0,), (0,)), ((), ())), preferred_element_type=F32)

    rows = [a.reshape(4, -1, a.shape[1])[:, 4 * slots :].reshape(-1, a.shape[1]) for a in (got, got_other)]
    rows = tn(rows[0], come[0]) + tn(rows[1], come[1])
    rows = jnp.where(c == 0, rows[:quarter], rows[quarter : 2 * quarter]).astype(BF)
    rows = lax.ppermute(rows, DP + HD, swap)

    weights, values, rows = lax.optimization_barrier((weights, values, rows))
    weights_other = shifted(weights, "c", 1)
    part = mix_project(goes, weights, weights_other, values, output_weight.T)
    projected = jnp.sum(exchange(part, HD).astype(F32), axis=0)
    mixed = (rows.astype(F32) + projected).astype(BF)

    full = []
    for k in range(4):
        sends = []
        for a in range(4):
            for b in range(8):
                for e in range(4):
                    for f in range(2):
                        to = (((e + k) & 3) * 8 + (f * 4 + (b & 3))) * 8 + a * 2 + (b >> 2)
                        sends.append(((a * 8 + b) * 8 + e * 2 + f, to))
        full.append(lax.ppermute(mixed, DP + HD, sends))
    full = jnp.stack(full)

    full = gather(full, "y").reshape(2, 2, 4, quarter, chunk)
    full_other = shifted(full, "c", 1)
    ff = down_weight.shape[0]
    part = gate_up(full, full_other, norm_gain[None, :], gate_weight.T, up_weight.T)
    total = jnp.sum(exchange(part, HD).astype(F32), axis=0)
    scale = lax.rsqrt((total[2 * ff : 2 * ff + 1] + total[2 * ff + 1 : 2 * ff + 2]) / model + 1e-06)
    hidden = (jax.nn.silu(total[:ff] * scale) * (total[ff : 2 * ff] * scale)).astype(BF)
    hidden = gather(hidden, HD).reshape(4, 2, ff, chunk)

    def down(core):
        piece = lax.dynamic_index_in_dim(hidden, core, 1, keepdims=False)
        return lax.dot_general(
            piece, down_weight, (((1,), (0,)), ((), ())), preferred_element_type=F32
        )

    sent = shifted(down(1 - c).astype(BF), "c", 1)
    total = (down(c) + sent.astype(F32)).astype(BF)
    total = jnp.sum(exchange(total, "y").astype(F32), axis=0)
    spot = y * 2 + c
    begin = starts(every)
    m = ((zh - (spot & 3)) & 3) * 2 + (spot >> 2)
    place = ((m - begin[:, None]) & 7) + 8 * eight[None, :]
    comes = jnp.where(place < rank_tokens[:, None], (begin[:, None] + place) >> 3, -1)
    expand = (comes.reshape(ranks * 8, 1) == jnp.arange(chunk, dtype=jnp.int32)).astype(BF)
    pair = [pick(a.reshape(2, 2, 4, quarter, chunk), spot >> 2) for a in (full, full_other)]
    pair = [lax.dynamic_index_in_dim(a, spot & 3, 1, keepdims=False) for a in pair]
    low = jnp.where(c == 0, pair[0], pair[1])
    high = jnp.where(c == 0, pair[1], pair[0])
    own = jnp.stack([low, high], axis=1).reshape(width, chunk)
    here = (jnp.arange(ranks * 8, dtype=jnp.int32) >> 6) == zh
    own = nt(jnp.where(here[:, None], expand, jnp.zeros_like(expand)), own)
    result = (dot(expand, total.astype(BF)) + own).astype(BF).reshape(ranks, 8, width)
    result = exchange(result, DP).reshape(ranks * 8, width)
    source = jnp.arange(ranks, dtype=jnp.int32)
    chunk_of = (((source >> 3) - (source & 3)) & 3) * 2 + ((source >> 2) & 1)
    fits = chunk_of[None, :, None] == ((own_start + slot) & 7)[:, None, None]
    fits = fits & (eight[None, None, :] == (slot >> 3)[:, None, None])
    fits = fits & (slot < own_length)[:, None, None]
    return dot(fits.astype(BF).reshape(slots, ranks * 8), result).astype(BF)


def solution(mesh):
    mesh = Mesh(mesh.devices.reshape(4, 4, 2, 4, 2), DP + HD)
    in_specs = (
        P(DP, HD),
        P(DP, HD),
        P(DP, None),
        P(DP, None),
        P(None, HD),
        P(None, HD),
        P(HD, DP),
        P(DP, HD),
        P(HD),
        P(HD, DP),
        P(HD, DP),
        P(DP, HD),
        P(),
        P(DP, None),
    )
    return jax.shard_map(
        on_device, mesh=mesh, in_specs=in_specs, out_specs=P(DP, HD), check_vma=False
    )
```

```python
import jax
import jax.numpy as jnp
from jax import lax
from jax.experimental import pallas as pl
from jax.experimental.pallas import tpu as pltpu
from jax.sharding import Mesh, PartitionSpec as P

BF = jnp.bfloat16
F32 = jnp.float32
NOPE = 128
ROPE = 64
VH = 128
WIN = 32
LIVE = 1024
BLK = 128
STEP = 256
DP = ("zh", "y", "c")
HD = ("x", "zl")


def dot(a, b):
    return jnp.dot(a, b, preferred_element_type=F32)


def shifted(x, axis, shift):
    n = lax.axis_size(axis)
    return lax.ppermute(x, axis, [(i, (i + shift) % n) for i in range(n)])


def iota(shape, dim):
    return lax.broadcasted_iota(jnp.int32, shape, dim)


def nt(a, b):
    return lax.dot_general(a, b, (((1,), (1,)), ((), ())), preferred_element_type=F32)


def whole(shape):
    return pl.BlockSpec(shape, lambda *_: (0,) * len(shape), pipeline_mode=pl.Buffered(1))


def cost(us):
    return pl.CostEstimate(flops=us * 10**9, bytes_accessed=us * 3 * 10**6, transcendentals=0)


def rank_here():
    return (lax.axis_index("zh") * 4 + lax.axis_index("y")) * 2 + lax.axis_index("c")


def live_before(counts_ref):
    place = rank_here()
    return lax.fori_loop(
        0,
        counts_ref.shape[0],
        lambda i, a: a + jnp.where(i < place, counts_ref[i], 0),
        jnp.int32(0),
    )


def pack_kernel(counts_ref, lat_ref, res_ref, out_ref, rows_ref):
    slots, width = res_ref.shape
    half, lanes = width // 2, lat_ref.shape[1]
    start = live_before(counts_ref)
    i_at, slot = iota((slots, slots), 0), iota((slots, slots), 1)
    roll = ((((i_at >> 3) - start) & 7) + 8 * (i_at & 7)) == slot
    rows_ref[...] = dot(jnp.where(roll, 1.0, 0.0).astype(BF), res_ref[...])
    fill = jnp.zeros((16, lanes - half), F32)
    for s in range(4):
        out_ref[s, :slots, :] = lat_ref[...]
        for high in range(2):
            piece = rows_ref[(s * 2 + high) * 8 : (s * 2 + high + 1) * 8, :]
            piece = jnp.concatenate([piece[:, :half], piece[:, half:]], axis=0)
            piece = jnp.concatenate([piece, fill], axis=1)
            out_ref[s, slots + 16 * high : slots + 16 * (high + 1), :] = piece.astype(BF)


def pack(counts, latent, residual):
    slots, lanes = latent.shape
    shape = (4, slots + 32, lanes)
    return pl.pallas_call(
        pack_kernel,
        grid=(1,),
        out_shape=jax.ShapeDtypeStruct(shape, BF),
        in_specs=[
            pl.BlockSpec(memory_space=pltpu.SMEM),
            whole(latent.shape),
            whole(residual.shape),
        ],
        out_specs=whole(shape),
        scratch_shapes=[pltpu.VMEM(residual.shape, F32)],
        cost_estimate=cost(2),
        name="pack",
    )(counts, latent, residual)


def repack_kernel(in_ref, *refs):
    outs, rows_ref = refs[:4], refs[4]
    slots = in_ref.shape[1] - 32
    y = lax.axis_index("y")
    for t in range(4):
        rows_ref[t] = in_ref[t, slots:, :].astype(F32)
    for s in range(4):
        at = pl.ds(pl.multiple_of(((y + s) & 3) * 8, 8), 8)
        for t in range(4):
            outs[s][t * slots : (t + 1) * slots, :] = in_ref[t, :slots, :]
        for t in (0, 2):
            pair = jnp.concatenate([rows_ref[t, at, :], rows_ref[t + 1, at, :]], axis=0)
            outs[s][4 * slots + 8 * t : 4 * slots + 8 * t + 16, :] = pair.astype(BF)


def repack(packed):
    _, rows, lanes = packed.shape
    shape = (4 * (rows - 32) + 32, lanes)
    return pl.pallas_call(
        repack_kernel,
        grid=(1,),
        out_shape=[jax.ShapeDtypeStruct(shape, BF)] * 4,
        in_specs=[whole(packed.shape)],
        out_specs=[whole(shape)] * 4,
        scratch_shapes=[pltpu.VMEM((4, 32, lanes), F32)],
        cost_estimate=cost(2),
        name="repack",
    )(packed)


def score_kernel(counts_ref, qn_ref, qr_ref, lat_ref, kr_ref, ku_ref, req_ref, out_ref, s_ref):
    slots = lat_ref.shape[0]
    heads = ku_ref.shape[1] // NOPE
    before = live_before(counts_ref)
    keys = dot(lat_ref[...], ku_ref[...]).astype(BF)
    key_rope = kr_ref[...]
    s_at, t_at = iota((slots, slots), 0), iota((slots, slots), 1)
    across = jnp.broadcast_to(req_ref[...], (slots, slots))
    down = jnp.sum(jnp.where(s_at == t_at, across, 0), axis=1, keepdims=True)
    allowed = (across == down) & (t_at <= s_at)
    t_row, lane = iota((slots, BLK), 0), iota((slots, BLK), 1)
    lands = ((before + t_row) & (WIN - 1)) == (lane & (WIN - 1))
    per = BLK // WIN
    for h in range(heads):
        rows = slice(h * slots, (h + 1) * slots)
        s = nt(qn_ref[:, h * NOPE : (h + 1) * NOPE], keys[:, h * NOPE : (h + 1) * NOPE])
        s = s + nt(qr_ref[:, h * ROPE : (h + 1) * ROPE], key_rope)
        s_ref[rows, :] = jnp.where(allowed, s * (NOPE + ROPE) ** (-0.5), jnp.float32(-1e30))
    s = s_ref[...]
    raised = jnp.exp(s - jnp.max(s, axis=-1, keepdims=True))
    w = (raised / jnp.sum(raised, axis=-1, keepdims=True)).astype(BF)
    folded = dot(w, jnp.where(lands, 1.0, 0.0).astype(BF))
    for group in range(heads // per):
        out = folded[group * per * slots : (group * per + 1) * slots]
        for i in range(1, per):
            h = group * per + i
            out = jnp.where((lane >> 5) == i, folded[h * slots : (h + 1) * slots], out)
        for copy in range(out_ref.shape[0]):
            out_ref[copy, :, group * BLK : (group + 1) * BLK] = out.astype(BF)


def score_weights(counts, *arrays):
    slots, heads = arrays[2].shape[0], arrays[4].shape[1] // NOPE
    shape = (4, slots, heads * WIN)
    return pl.pallas_call(
        score_kernel,
        grid=(1,),
        out_shape=jax.ShapeDtypeStruct(shape, BF),
        in_specs=[pl.BlockSpec(memory_space=pltpu.SMEM)] + [whole(a.shape) for a in arrays],
        out_specs=whole(shape),
        scratch_shapes=[pltpu.VMEM((slots * heads, slots), F32)],
        cost_estimate=cost(4),
        name="score_weights",
    )(counts, *arrays)


def live_rows(goes_ref, slots_ref):
    row = iota((STEP, slots_ref.shape[0]), 0) + pl.program_id(0) * STEP
    return dot(jnp.where(goes_ref[...] == row, 1.0, 0.0).astype(BF), slots_ref[...]).astype(BF)


def values_kernel(goes_ref, slots_ref, up_ref, out_ref):
    out_ref[...] = dot(live_rows(goes_ref, slots_ref), up_ref[...]).astype(BF)


def live_values(goes, slots, up):
    width = up.shape[1]
    return pl.pallas_call(
        values_kernel,
        grid=(LIVE // STEP,),
        out_shape=jax.ShapeDtypeStruct((LIVE, width), BF),
        in_specs=[whole(a.shape) for a in (goes, slots, up)],
        out_specs=pl.BlockSpec((STEP, width), lambda b: (b, 0)),
        cost_estimate=cost(0),
        name="live_values",
    )(goes, slots, up)


def mix_kernel(goes_ref, slots_ref, prev_ref, cur_ref, *refs):
    att_ref, all_ref = refs[4:]
    b = pl.program_id(0)
    heads = cur_ref.shape[1] // VH
    r_at, l_at = iota((BLK, BLK), 0), iota((BLK, BLK), 1)
    gap = r_at - l_at
    near = (gap >= 0) & (gap < WIN)
    per = BLK // WIN
    masks = [jnp.where(near & ((l_at >> 5) == q), 1.0, 0.0).astype(BF) for q in range(per)]
    r_at, l_at = iota((WIN, BLK), 0), iota((WIN, BLK), 1)
    before = jnp.where((BLK + r_at - l_at) < WIN, 1.0, 0.0).astype(BF)
    blank = jnp.zeros((BLK - WIN, BLK), BF)
    packed = live_rows(goes_ref, slots_ref)
    for group in range(heads // per):
        one = packed[:, group * BLK : (group + 1) * BLK].astype(F32)
        turned = [one.astype(BF)]
        for q in range(1, per):
            turned.append(pltpu.roll(one, q * WIN, 1).astype(BF))
        for i in range(per):
            cols = slice((group * per + i) * VH, (group * per + i + 1) * VH)
            last = turned[(per - 1 - i) % per]
            olds = [prev_ref[:, cols], cur_ref[:BLK, cols]]
            for t in range(STEP // BLK):
                rows = slice(t * BLK, (t + 1) * BLK)
                band = turned[(-i) % per][rows] * masks[0]
                for q in range(1, per):
                    band = band + turned[(q - i) % per][rows] * masks[q]
                corner = jnp.concatenate([last[rows][:WIN] * before, blank], axis=0)
                att = dot(
                    jnp.concatenate([corner, band], axis=1),
                    jnp.concatenate([olds[t], cur_ref[rows, cols]], axis=0),
                )
                att_ref[rows, cols] = att.astype(BF)
    share = STEP // 8
    r_at, l_at = iota((STEP, STEP), 0), iota((STEP, STEP), 1)
    order = ((r_at & (share - 1)) * 8 + (r_at >> 5)) == l_at
    order = jnp.where(order, 1.0, 0.0).astype(BF)
    rows = pl.ds(pl.multiple_of(b * share, share), share)
    for which in range(2):
        part = dot(order, nt(att_ref[...], refs[which][...]).astype(BF))
        for m in range(8):
            all_ref[which, m, rows, :] = part[m * share : (m + 1) * share]

    @pl.when(b == pl.num_programs(0) - 1)
    def _():
        for which in range(2):
            for m in range(8):
                refs[2 + which][m] = all_ref[which, m].T.astype(BF)


def mix_project(goes, slots, values, wo, wo_other):
    width = values.shape[1]
    n = wo.shape[0]
    shape = (8, n, LIVE // 8)
    return pl.pallas_call(
        mix_kernel,
        grid=(LIVE // STEP,),
        out_shape=[jax.ShapeDtypeStruct(shape, BF)] * 2,
        in_specs=[
            whole(goes.shape),
            whole(slots.shape),
            pl.BlockSpec((BLK, width), lambda b: (jnp.maximum(b * (STEP // BLK) - 1, 0), 0)),
            pl.BlockSpec((STEP, width), lambda b: (b, 0)),
            whole(wo.shape),
            whole(wo.shape),
        ],
        out_specs=[whole(shape)] * 2,
        scratch_shapes=[pltpu.VMEM((STEP, width), BF), pltpu.VMEM((2, 8, LIVE // 8, n), F32)],
        cost_estimate=cost(9),
        name="mix_project",
    )(goes, slots, values, values, wo, wo_other)


def gate_up_kernel(own_ref, other_ref, gain_ref, gate_ref, up_ref, out_ref, x_ref, gain_at):
    core = lax.axis_index("c")
    _, lows, blocks, k, chunk = own_ref.shape
    ff = gate_ref.shape[0]
    squares = jnp.zeros((1, blocks * chunk), F32)
    gain_at[...] = jnp.broadcast_to(gain_ref[...], (8, gain_ref.shape[1])).T
    for ref, flip in ((own_ref, core), (other_ref, 1 - core)):
        for low in range(lows):
            rows = pl.ds(pl.multiple_of((low * 2 + flip) * k, 32), k)
            x = jnp.concatenate([ref[0, low, i] for i in range(blocks)], axis=1).astype(F32)
            squares = squares + jnp.sum(x * x, axis=0, keepdims=True)
            x_ref[rows, :] = (x * gain_at[rows, :1]).astype(BF)
    x = x_ref[...]
    gate = dot(gate_ref[...], x).astype(BF)
    up = dot(up_ref[...], x).astype(BF)
    row = iota((16, blocks * chunk), 0)
    high = squares.astype(BF).astype(F32)
    extra = jnp.where(row == 0, high, jnp.where(row == 1, squares - high, 0.0)).astype(BF)
    for i in range(blocks):
        cols = slice(i * chunk, (i + 1) * chunk)
        out_ref[i, :ff, :] = gate[:, cols]
        out_ref[i, ff : 2 * ff, :] = up[:, cols]
        out_ref[i, 2 * ff :, :] = extra[:, cols]


def gate_up(own, other, gain, gate_weight, up_weight):
    highs, lows, planes, k, chunk = own.shape
    ff, width = gate_weight.shape
    blocks = 2
    spec = pl.BlockSpec(
        (1, lows, blocks, k, chunk),
        lambda b: (b // (planes // blocks), 0, b % (planes // blocks), 0, 0),
    )
    return pl.pallas_call(
        gate_up_kernel,
        grid=(highs * planes // blocks,),
        out_shape=jax.ShapeDtypeStruct((highs * planes, 2 * ff + 16, chunk), BF),
        in_specs=[spec, spec, whole((1, width)), whole((ff, width)), whole((ff, width))],
        out_specs=pl.BlockSpec((blocks, 2 * ff + 16, chunk), lambda b: (b, 0, 0)),
        scratch_shapes=[pltpu.VMEM((width, blocks * chunk), BF), pltpu.VMEM((width, 8), F32)],
        cost_estimate=cost(6),
        name="gate_up",
    )(own, other, gain, gate_weight, up_weight)


def exchange(x, axes):
    return lax.all_to_all(x, axes, split_axis=0, concat_axis=0, tiled=True)


def gather(x, axes):
    n = lax.axis_size(axes)
    return exchange(jnp.broadcast_to(x[None], (n,) + x.shape), axes)


def pick(x, index):
    return lax.dynamic_index_in_dim(x, index, 0, keepdims=False)


def on_device(
    query_nope,
    query_rope,
    latent,
    key_rope,
    key_up,
    value_up,
    output_weight,
    residual,
    norm_gain,
    gate_weight,
    up_weight,
    down_weight,
    rank_tokens,
    request_ids,
):
    slots = latent.shape[0]
    ranks = rank_tokens.shape[0]
    zh, y, c = (lax.axis_index(a) for a in DP)
    rank = (zh * 4 + y) * 2 + c
    chunk = LIVE // 8
    width = residual.shape[1]
    quarter = width // 4
    model = 8 * width

    every = jnp.arange(ranks, dtype=jnp.int32)

    def starts(which):
        return jnp.sum(jnp.where(every < which[..., None], rank_tokens, 0), axis=-1)

    def lengths(which):
        return jnp.sum(jnp.where(every == which[..., None], rank_tokens, 0), axis=-1)

    own_start, own_length = starts(rank), lengths(rank)
    slot = jnp.arange(slots, dtype=jnp.int32)

    packed = exchange(pack(rank_tokens, latent, residual), "zh")

    weights = score_weights(
        rank_tokens, query_nope, query_rope, latent, key_rope, key_up, request_ids
    )
    weights, packed = lax.optimization_barrier((weights, packed))
    weights = exchange(weights, "zh")
    pieces = repack(packed)
    weights, _ = lax.optimization_barrier((weights, pieces))
    pieces = [pieces[0]] + [shifted(pieces[s], "y", s) for s in (1, 2, 3)]
    got = jnp.concatenate(pieces, axis=0)
    weights = gather(weights, "y").reshape(-1, weights.shape[2])

    four = jnp.arange(4, dtype=jnp.int32)
    eight = jnp.arange(8, dtype=jnp.int32)
    ahead = (four[None, :] * 4 + four[:, None]) * 2 + c
    goes = jnp.where(slot < lengths(ahead)[..., None], starts(ahead)[..., None] + slot, -1)
    goes = goes.reshape(1, -1)
    core = jnp.stack([c, 1 - c])[:, None, None]
    back = (four[None, None, :] * 4 + ((y - four) & 3)[None, :, None]) * 2 + core
    back_start, back_count = starts(back)[..., None], lengths(back)[..., None]
    goes_back = jnp.where(slot < back_count[0], back_start[0] + slot, -1).reshape(4, -1)
    goes_back = jnp.pad(goes_back, ((0, 0), (0, 32)), constant_values=-1).reshape(1, -1)
    values = live_values(goes_back, got, value_up)

    swap = []
    for a in range(4):
        for b in range(8):
            for e in range(4):
                for f in range(2):
                    to = (e * 8 + (f * 4 + (b & 3))) * 8 + a * 2 + (b >> 2)
                    swap.append(((a * 8 + b) * 8 + e * 2 + f, to))
    place = (((zh * 2 + (y >> 1)) - back_start) & 7) + 8 * eight
    come = jnp.where(place < back_count, (back_start + place) >> 3, -1)
    come = (come.reshape(2, -1, 1) == jnp.arange(chunk, dtype=jnp.int32)).astype(BF)

    def tn(a, b):
        return lax.dot_general(a, b, (((0,), (0,)), ((), ())), preferred_element_type=F32)

    rows = got.reshape(4, -1, got.shape[1])[:, 4 * slots :].reshape(-1, got.shape[1])
    rows = [rows, shifted(rows, "c", 1)]
    rows = tn(rows[0], come[0]) + tn(rows[1], come[1])
    rows = jnp.where(c == 0, rows[:quarter], rows[quarter : 2 * quarter]).astype(BF)
    rows, values = lax.optimization_barrier((rows, values))
    rows = lax.ppermute(rows, DP + HD, swap)

    wo = output_weight.T
    part, sent = mix_project(goes, weights, values, wo, shifted(wo, "c", 1))
    part = part + shifted(sent, "c", 1)
    projected = jnp.sum(exchange(part, HD).astype(F32), axis=0)
    mixed = (rows.astype(F32) + projected).astype(BF)

    full = []
    for k in range(4):
        sends = []
        for a in range(4):
            for b in range(8):
                for e in range(4):
                    for f in range(2):
                        to = (((e + k) & 3) * 8 + (f * 4 + (b & 3))) * 8 + a * 2 + (b >> 2)
                        sends.append(((a * 8 + b) * 8 + e * 2 + f, to))
        full.append(lax.ppermute(mixed, DP + HD, sends))
    full = jnp.stack(full)

    full = gather(full, "y").reshape(2, 2, 4, quarter, chunk)
    full_other = shifted(full, "c", 1)
    ff = down_weight.shape[0]
    part = gate_up(full, full_other, norm_gain[None, :], gate_weight.T, up_weight.T)
    total = jnp.sum(exchange(part, HD).astype(F32), axis=0)
    scale = lax.rsqrt((total[2 * ff : 2 * ff + 1] + total[2 * ff + 1 : 2 * ff + 2]) / model + 1e-06)
    hidden = (jax.nn.silu(total[:ff] * scale) * (total[ff : 2 * ff] * scale)).astype(BF)
    hidden = gather(hidden, HD).reshape(4, 2, ff, chunk)

    def down(core):
        piece = lax.dynamic_index_in_dim(hidden, core, 1, keepdims=False)
        return lax.dot_general(
            piece, down_weight, (((1,), (0,)), ((), ())), preferred_element_type=F32
        )

    sent = shifted(down(1 - c).astype(BF), "c", 1)
    total = (down(c) + sent.astype(F32)).astype(BF)
    total = jnp.sum(exchange(total, "y").astype(F32), axis=0)
    spot = y * 2 + c
    begin = starts(every)
    m = ((zh - (spot & 3)) & 3) * 2 + (spot >> 2)
    place = ((m - begin[:, None]) & 7) + 8 * eight[None, :]
    comes = jnp.where(place < rank_tokens[:, None], (begin[:, None] + place) >> 3, -1)
    expand = (comes.reshape(ranks * 8, 1) == jnp.arange(chunk, dtype=jnp.int32)).astype(BF)
    pair = [pick(a.reshape(2, 2, 4, quarter, chunk), spot >> 2) for a in (full, full_other)]
    pair = [lax.dynamic_index_in_dim(a, spot & 3, 1, keepdims=False) for a in pair]
    low = jnp.where(c == 0, pair[0], pair[1])
    high = jnp.where(c == 0, pair[1], pair[0])
    own = jnp.stack([low, high], axis=1).reshape(width, chunk)
    here = (jnp.arange(ranks * 8, dtype=jnp.int32) >> 6) == zh
    own = nt(jnp.where(here[:, None], expand, jnp.zeros_like(expand)), own)
    result = (dot(expand, total.astype(BF)) + own).astype(BF).reshape(ranks, 8, width)
    result = exchange(result, DP).reshape(ranks * 8, width)
    source = jnp.arange(ranks, dtype=jnp.int32)
    chunk_of = (((source >> 3) - (source & 3)) & 3) * 2 + ((source >> 2) & 1)
    fits = chunk_of[None, :, None] == ((own_start + slot) & 7)[:, None, None]
    fits = fits & (eight[None, None, :] == (slot >> 3)[:, None, None])
    fits = fits & (slot < own_length)[:, None, None]
    return dot(fits.astype(BF).reshape(slots, ranks * 8), result).astype(BF)


def solution(mesh):
    mesh = Mesh(mesh.devices.reshape(4, 4, 2, 4, 2), DP + HD)
    in_specs = (
        P(DP, HD),
        P(DP, HD),
        P(DP, None),
        P(DP, None),
        P(None, HD),
        P(None, HD),
        P(HD, DP),
        P(DP, HD),
        P(HD),
        P(HD, DP),
        P(HD, DP),
        P(DP, HD),
        P(),
        P(DP, None),
    )
    return jax.shard_map(
        on_device, mesh=mesh, in_specs=in_specs, out_specs=P(DP, HD), check_vma=False
    )
```

```python
import jax
import jax.numpy as jnp
from jax import lax
from jax.experimental import pallas as pl
from jax.experimental.pallas import tpu as pltpu
from jax.sharding import Mesh, PartitionSpec as P

BF = jnp.bfloat16
F32 = jnp.float32
NOPE = 128
ROPE = 64
VH = 128
WIN = 32
LIVE = 1024
BLK = 128
STEP = 256
DP = ("zh", "y", "c")
HD = ("x", "zl")


def dot(a, b):
    return jnp.dot(a, b, preferred_element_type=F32)


def shifted(x, axis, shift):
    n = lax.axis_size(axis)
    return lax.ppermute(x, axis, [(i, (i + shift) % n) for i in range(n)])


def iota(shape, dim):
    return lax.broadcasted_iota(jnp.int32, shape, dim)


def nt(a, b):
    return lax.dot_general(a, b, (((1,), (1,)), ((), ())), preferred_element_type=F32)


def whole(shape):
    return pl.BlockSpec(shape, lambda *_: (0,) * len(shape), pipeline_mode=pl.Buffered(1))


def cost(us):
    return pl.CostEstimate(flops=us * 10**9, bytes_accessed=us * 3 * 10**6, transcendentals=0)


def rank_here():
    return (lax.axis_index("zh") * 4 + lax.axis_index("y")) * 2 + lax.axis_index("c")


def live_before(counts_ref):
    place = rank_here()
    return lax.fori_loop(
        0,
        counts_ref.shape[0],
        lambda i, a: a + jnp.where(i < place, counts_ref[i], 0),
        jnp.int32(0),
    )


def pack_kernel(counts_ref, lat_ref, res_ref, *refs):
    outs, rows_ref = refs[:4], refs[4]
    slots, width = res_ref.shape
    half, lanes = width // 2, lat_ref.shape[1]
    zh = lax.axis_index("zh")
    start = live_before(counts_ref)
    i_at, slot = iota((slots, slots), 0), iota((slots, slots), 1)
    roll = ((((i_at >> 3) - start) & 7) + 8 * (i_at & 7)) == slot
    rows_ref[...] = dot(jnp.where(roll, 1.0, 0.0).astype(BF), res_ref[...])
    fill = jnp.zeros((16, lanes - half), F32)
    for s in range(4):
        outs[s][:slots, :] = lat_ref[...]
        for high in range(2):
            m = ((zh + s) & 3) * 2 + high
            piece = rows_ref[pl.ds(pl.multiple_of(m * 8, 8), 8), :]
            piece = jnp.concatenate([piece[:, :half], piece[:, half:]], axis=0)
            piece = jnp.concatenate([piece, fill], axis=1)
            outs[s][slots + 16 * high : slots + 16 * (high + 1), :] = piece.astype(BF)


def pack(counts, latent, residual):
    slots, lanes = latent.shape
    shape = (slots + 32, lanes)
    return pl.pallas_call(
        pack_kernel,
        grid=(1,),
        out_shape=[jax.ShapeDtypeStruct(shape, BF)] * 4,
        in_specs=[
            pl.BlockSpec(memory_space=pltpu.SMEM),
            whole(latent.shape),
            whole(residual.shape),
        ],
        out_specs=[whole(shape)] * 4,
        scratch_shapes=[pltpu.VMEM(residual.shape, F32)],
        cost_estimate=cost(2),
        name="pack",
    )(counts, latent, residual)


def repack_kernel(*refs):
    ins, outs, rows_ref = refs[:4], refs[4:8], refs[8]
    slots = ins[0].shape[0] - 32
    y = lax.axis_index("y")
    for t in range(4):
        rows_ref[t] = ins[t][slots:, :].astype(F32)
    for s in range(4):
        at = pl.ds(pl.multiple_of(((y + s) & 3) * 8, 8), 8)
        for t in range(4):
            outs[s][t * slots : (t + 1) * slots, :] = ins[t][:slots, :]
        for t in (0, 2):
            pair = jnp.concatenate([rows_ref[t, at, :], rows_ref[t + 1, at, :]], axis=0)
            outs[s][4 * slots + 8 * t : 4 * slots + 8 * t + 16, :] = pair.astype(BF)


def repack(*pieces):
    rows, lanes = pieces[0].shape
    shape = (4 * (rows - 32) + 32, lanes)
    return pl.pallas_call(
        repack_kernel,
        grid=(1,),
        out_shape=[jax.ShapeDtypeStruct(shape, BF)] * 4,
        in_specs=[whole(pieces[0].shape)] * 4,
        out_specs=[whole(shape)] * 4,
        scratch_shapes=[pltpu.VMEM((4, 32, lanes), F32)],
        cost_estimate=cost(2),
        name="repack",
    )(*pieces)


def score_kernel(counts_ref, qn_ref, qr_ref, lat_ref, kr_ref, ku_ref, req_ref, out_ref, s_ref):
    slots = lat_ref.shape[0]
    heads = ku_ref.shape[1] // NOPE
    before = live_before(counts_ref)
    keys = dot(lat_ref[...], ku_ref[...]).astype(BF)
    key_rope = kr_ref[...]
    s_at, t_at = iota((slots, slots), 0), iota((slots, slots), 1)
    across = jnp.broadcast_to(req_ref[...], (slots, slots))
    down = jnp.sum(jnp.where(s_at == t_at, across, 0), axis=1, keepdims=True)
    allowed = (across == down) & (t_at <= s_at)
    t_row, lane = iota((slots, BLK), 0), iota((slots, BLK), 1)
    lands = ((before + t_row) & (WIN - 1)) == (lane & (WIN - 1))
    per = BLK // WIN
    for h in range(heads):
        rows = slice(h * slots, (h + 1) * slots)
        s = nt(qn_ref[:, h * NOPE : (h + 1) * NOPE], keys[:, h * NOPE : (h + 1) * NOPE])
        s = s + nt(qr_ref[:, h * ROPE : (h + 1) * ROPE], key_rope)
        s_ref[rows, :] = jnp.where(allowed, s * (NOPE + ROPE) ** (-0.5), jnp.float32(-1e30))
    s = s_ref[...]
    raised = jnp.exp(s - jnp.max(s, axis=-1, keepdims=True))
    w = (raised / jnp.sum(raised, axis=-1, keepdims=True)).astype(BF)
    folded = dot(w, jnp.where(lands, 1.0, 0.0).astype(BF))
    for group in range(heads // per):
        out = folded[group * per * slots : (group * per + 1) * slots]
        for i in range(1, per):
            h = group * per + i
            out = jnp.where((lane >> 5) == i, folded[h * slots : (h + 1) * slots], out)
        for copy in range(out_ref.shape[0]):
            out_ref[copy, :, group * BLK : (group + 1) * BLK] = out.astype(BF)


def score_weights(counts, *arrays):
    slots, heads = arrays[2].shape[0], arrays[4].shape[1] // NOPE
    shape = (4, slots, heads * WIN)
    return pl.pallas_call(
        score_kernel,
        grid=(1,),
        out_shape=jax.ShapeDtypeStruct(shape, BF),
        in_specs=[pl.BlockSpec(memory_space=pltpu.SMEM)] + [whole(a.shape) for a in arrays],
        out_specs=whole(shape),
        scratch_shapes=[pltpu.VMEM((slots * heads, slots), F32)],
        cost_estimate=cost(4),
        name="score_weights",
    )(counts, *arrays)


def live_rows(goes_ref, own_ref, other_ref):
    row = iota((STEP, own_ref.shape[0]), 0) + pl.program_id(0) * STEP
    out = dot(jnp.where(goes_ref[0] == row, 1.0, 0.0).astype(BF), own_ref[...])
    out = out + dot(jnp.where(goes_ref[1] == row, 1.0, 0.0).astype(BF), other_ref[...])
    return out.astype(BF)


def values_kernel(goes_ref, own_ref, other_ref, up_ref, out_ref):
    out_ref[...] = dot(live_rows(goes_ref, own_ref, other_ref), up_ref[...]).astype(BF)


def live_values(goes, own, other, up):
    width = up.shape[1]
    return pl.pallas_call(
        values_kernel,
        grid=(LIVE // STEP,),
        out_shape=jax.ShapeDtypeStruct((LIVE, width), BF),
        in_specs=[whole(a.shape) for a in (goes, own, other, up)],
        out_specs=pl.BlockSpec((STEP, width), lambda b: (b, 0)),
        cost_estimate=cost(0),
        name="live_values",
    )(goes, own, other, up)


def mix_kernel(goes_ref, own_ref, other_ref, prev_ref, cur_ref, wo_ref, out_ref, att_ref, all_ref):
    b = pl.program_id(0)
    heads = cur_ref.shape[1] // VH
    r_at, l_at = iota((BLK, BLK), 0), iota((BLK, BLK), 1)
    gap = r_at - l_at
    near = (gap >= 0) & (gap < WIN)
    per = BLK // WIN
    masks = [jnp.where(near & ((l_at >> 5) == q), 1.0, 0.0).astype(BF) for q in range(per)]
    r_at, l_at = iota((WIN, BLK), 0), iota((WIN, BLK), 1)
    before = jnp.where((BLK + r_at - l_at) < WIN, 1.0, 0.0).astype(BF)
    blank = jnp.zeros((BLK - WIN, BLK), BF)
    packed = live_rows(goes_ref, own_ref, other_ref)
    for group in range(heads // per):
        one = packed[:, group * BLK : (group + 1) * BLK].astype(F32)
        turned = [one.astype(BF)]
        for q in range(1, per):
            turned.append(pltpu.roll(one, q * WIN, 1).astype(BF))
        for i in range(per):
            cols = slice((group * per + i) * VH, (group * per + i + 1) * VH)
            last = turned[(per - 1 - i) % per]
            olds = [prev_ref[:, cols], cur_ref[:BLK, cols]]
            for t in range(STEP // BLK):
                rows = slice(t * BLK, (t + 1) * BLK)
                band = turned[(-i) % per][rows] * masks[0]
                for q in range(1, per):
                    band = band + turned[(q - i) % per][rows] * masks[q]
                corner = jnp.concatenate([last[rows][:WIN] * before, blank], axis=0)
                att = dot(
                    jnp.concatenate([corner, band], axis=1),
                    jnp.concatenate([olds[t], cur_ref[rows, cols]], axis=0),
                )
                att_ref[rows, cols] = att.astype(BF)
    part = nt(att_ref[...], wo_ref[...]).astype(BF)
    share = STEP // 8
    r_at, l_at = iota((STEP, STEP), 0), iota((STEP, STEP), 1)
    order = ((r_at & (share - 1)) * 8 + (r_at >> 5)) == l_at
    part = dot(jnp.where(order, 1.0, 0.0).astype(BF), part)
    rows = pl.ds(pl.multiple_of(b * share, share), share)
    for m in range(8):
        all_ref[m, rows, :] = part[m * share : (m + 1) * share]

    @pl.when(b == pl.num_programs(0) - 1)
    def _():
        for m in range(8):
            out_ref[m] = all_ref[m].T.astype(BF)


def mix_project(goes, own, other, values, wo):
    width = values.shape[1]
    n = wo.shape[0]
    shape = (8, n, LIVE // 8)
    return pl.pallas_call(
        mix_kernel,
        grid=(LIVE // STEP,),
        out_shape=jax.ShapeDtypeStruct(shape, BF),
        in_specs=[
            whole(goes.shape),
            whole(own.shape),
            whole(other.shape),
            pl.BlockSpec((BLK, width), lambda b: (jnp.maximum(b * (STEP // BLK) - 1, 0), 0)),
            pl.BlockSpec((STEP, width), lambda b: (b, 0)),
            whole(wo.shape),
        ],
        out_specs=whole(shape),
        scratch_shapes=[pltpu.VMEM((STEP, width), BF), pltpu.VMEM((8, LIVE // 8, n), F32)],
        cost_estimate=cost(9),
        name="mix_project",
    )(goes, own, other, values, values, wo)


def gate_up_kernel(own_ref, other_ref, gain_ref, gate_ref, up_ref, out_ref, x_ref, gain_at):
    core, y = lax.axis_index("c"), lax.axis_index("y")
    b = pl.program_id(0)
    blocks = out_ref.shape[0]
    _, planes, k, chunk = own_ref.shape
    ff = gate_ref.shape[0]
    steps = planes // blocks
    high, first = b // steps, (b % steps) * blocks
    squares = jnp.zeros((1, blocks * chunk), F32)
    gain_at[...] = jnp.broadcast_to(gain_ref[...], (8, gain_ref.shape[1])).T
    for ref, flip in ((own_ref, core), (other_ref, 1 - core)):
        for low in range(2):
            rows = pl.ds(pl.multiple_of((low * 2 + flip) * k, 32), k)
            s = (y - high * 2 - low) & 3
            x = jnp.concatenate([ref[s, first + i] for i in range(blocks)], axis=1).astype(F32)
            squares = squares + jnp.sum(x * x, axis=0, keepdims=True)
            x_ref[rows, :] = (x * gain_at[rows, :1]).astype(BF)
    x = x_ref[...]
    gate = dot(gate_ref[...], x).astype(BF)
    up = dot(up_ref[...], x).astype(BF)
    row = iota((16, blocks * chunk), 0)
    high = squares.astype(BF).astype(F32)
    extra = jnp.where(row == 0, high, jnp.where(row == 1, squares - high, 0.0)).astype(BF)
    for i in range(blocks):
        cols = slice(i * chunk, (i + 1) * chunk)
        out_ref[i, :ff, :] = gate[:, cols]
        out_ref[i, ff : 2 * ff, :] = up[:, cols]
        out_ref[i, 2 * ff :, :] = extra[:, cols]


def gate_up(own, other, gain, gate_weight, up_weight):
    _, planes, k, chunk = own.shape
    ff, width = gate_weight.shape
    blocks = 2
    return pl.pallas_call(
        gate_up_kernel,
        grid=(2 * planes // blocks,),
        out_shape=jax.ShapeDtypeStruct((2 * planes, 2 * ff + 16, chunk), BF),
        in_specs=[
            whole(own.shape),
            whole(own.shape),
            whole((1, width)),
            whole((ff, width)),
            whole((ff, width)),
        ],
        out_specs=pl.BlockSpec((blocks, 2 * ff + 16, chunk), lambda b: (b, 0, 0)),
        scratch_shapes=[pltpu.VMEM((width, blocks * chunk), BF), pltpu.VMEM((width, 8), F32)],
        cost_estimate=cost(6),
        name="gate_up",
    )(own, other, gain, gate_weight, up_weight)


def exchange(x, axes):
    return lax.all_to_all(x, axes, split_axis=0, concat_axis=0, tiled=True)


def gather(x, axes):
    n = lax.axis_size(axes)
    return exchange(jnp.broadcast_to(x[None], (n,) + x.shape), axes)


def pick(x, index):
    return lax.dynamic_index_in_dim(x, index, 0, keepdims=False)


def on_device(
    query_nope,
    query_rope,
    latent,
    key_rope,
    key_up,
    value_up,
    output_weight,
    residual,
    norm_gain,
    gate_weight,
    up_weight,
    down_weight,
    rank_tokens,
    request_ids,
):
    slots = latent.shape[0]
    ranks = rank_tokens.shape[0]
    zh, y, c = (lax.axis_index(a) for a in DP)
    rank = (zh * 4 + y) * 2 + c
    chunk = LIVE // 8
    width = residual.shape[1]
    quarter = width // 4
    model = 8 * width

    every = jnp.arange(ranks, dtype=jnp.int32)

    def starts(which):
        return jnp.sum(jnp.where(every < which[..., None], rank_tokens, 0), axis=-1)

    def lengths(which):
        return jnp.sum(jnp.where(every == which[..., None], rank_tokens, 0), axis=-1)

    own_start, own_length = starts(rank), lengths(rank)
    slot = jnp.arange(slots, dtype=jnp.int32)

    pieces = pack(rank_tokens, latent, residual)
    pieces = [pieces[0]] + [shifted(pieces[s], "zh", s) for s in (1, 2, 3)]

    weights = score_weights(
        rank_tokens, query_nope, query_rope, latent, key_rope, key_up, request_ids
    )
    weights = exchange(weights, "zh")
    pieces = repack(*pieces)
    weights, gain, _ = lax.optimization_barrier((weights, norm_gain[None, :], pieces))
    weights = jnp.broadcast_to(weights[None], (4,) + weights.shape)
    pieces = [pieces[0]] + [shifted(pieces[s], "y", s) for s in (1, 2, 3)]
    pieces, weights = lax.optimization_barrier((pieces, weights))
    got = jnp.concatenate(pieces, axis=0)
    got_other = shifted(got, "c", 1)
    weights = exchange(weights, "y").reshape(-1, weights.shape[3])

    four = jnp.arange(4, dtype=jnp.int32)
    eight = jnp.arange(8, dtype=jnp.int32)
    core = jnp.stack([c, 1 - c])[:, None, None]
    ahead = (four[None, None, :] * 4 + four[None, :, None]) * 2 + core
    goes = jnp.where(slot < lengths(ahead)[..., None], starts(ahead)[..., None] + slot, -1)
    goes = goes.reshape(2, 1, -1)
    back = (((zh - four) & 3)[None, None, :] * 4 + ((y - four) & 3)[None, :, None]) * 2 + core
    back_start, back_count = starts(back)[..., None], lengths(back)[..., None]
    goes_back = jnp.where(slot < back_count, back_start + slot, -1).reshape(2, 4, -1)
    goes_back = jnp.pad(goes_back, ((0, 0), (0, 0), (0, 32)), constant_values=-1).reshape(2, 1, -1)
    values = live_values(goes_back, got, got_other, value_up)

    swap = []
    for a in range(4):
        for b in range(8):
            for e in range(4):
                for f in range(2):
                    to = (e * 8 + (f * 4 + (b & 3))) * 8 + a * 2 + (b >> 2)
                    swap.append(((a * 8 + b) * 8 + e * 2 + f, to))
    place = (((zh * 2 + (y >> 1)) - back_start) & 7) + 8 * eight
    come = jnp.where(place < back_count, (back_start + place) >> 3, -1)
    come = (come.reshape(2, -1, 1) == jnp.arange(chunk, dtype=jnp.int32)).astype(BF)

    def tn(a, b):
        return lax.dot_general(a, b, (((0,), (0,)), ((), ())), preferred_element_type=F32)

    rows = [a.reshape(4, -1, a.shape[1])[:, 4 * slots :].reshape(-1, a.shape[1]) for a in (got, got_other)]
    rows = tn(rows[0], come[0]) + tn(rows[1], come[1])
    rows = jnp.where(c == 0, rows[:quarter], rows[quarter : 2 * quarter]).astype(BF)
    rows, values = lax.optimization_barrier((rows, values))
    rows = lax.ppermute(rows, DP + HD, swap)

    weights, values = lax.optimization_barrier((weights, values))
    weights_other = shifted(weights, "c", 1)
    part = mix_project(goes, weights, weights_other, values, output_weight.T)
    projected = jnp.sum(exchange(part, HD).astype(F32), axis=0)
    mixed = (rows.astype(F32) + projected).astype(BF)

    full = []
    for k in range(4):
        sends = []
        for a in range(4):
            for b in range(8):
                for e in range(4):
                    for f in range(2):
                        to = (((e + k) & 3) * 8 + (f * 4 + (b & 3))) * 8 + a * 2 + (b >> 2)
                        sends.append(((a * 8 + b) * 8 + e * 2 + f, to))
        full.append(lax.ppermute(mixed, DP + HD, sends))
    full = jnp.stack(full)

    full = jnp.stack([full] + [shifted(full, "y", s) for s in (1, 2, 3)])
    full_other = shifted(full, "c", 1)
    ff = down_weight.shape[0]
    part = gate_up(full, full_other, gain, gate_weight.T, up_weight.T)
    total = jnp.sum(exchange(part, HD).astype(F32), axis=0)
    scale = lax.rsqrt((total[2 * ff : 2 * ff + 1] + total[2 * ff + 1 : 2 * ff + 2]) / model + 1e-06)
    hidden = (jax.nn.silu(total[:ff] * scale) * (total[ff : 2 * ff] * scale)).astype(BF)
    hidden = gather(hidden, HD).reshape(4, 2, ff, chunk)

    def down(core):
        piece = lax.dynamic_index_in_dim(hidden, core, 1, keepdims=False)
        return lax.dot_general(
            piece, down_weight, (((1,), (0,)), ((), ())), preferred_element_type=F32
        )

    sent = shifted(down(1 - c).astype(BF), "c", 1)
    total = down(c) + sent.astype(F32)
    pieces = [pick(total, (y + s) & 3) for s in range(4)]
    total = pieces[0]
    for s in (1, 2, 3):
        total = total + shifted(pieces[s].astype(BF), "y", s).astype(F32)
    spot = y * 2 + c
    begin = starts(every)
    m = ((zh - (spot & 3)) & 3) * 2 + (spot >> 2)
    place = ((m - begin[:, None]) & 7) + 8 * eight[None, :]
    comes = jnp.where(place < rank_tokens[:, None], (begin[:, None] + place) >> 3, -1)
    expand = (comes.reshape(ranks * 8, 1) == jnp.arange(chunk, dtype=jnp.int32)).astype(BF)
    at = [(y - (spot >> 2) * 2 - low) & 3 for low in range(2)]
    pair = [jnp.stack([pick(pick(a, s), spot & 3) for s in at]) for a in (full, full_other)]
    low = jnp.where(c == 0, pair[0], pair[1])
    high = jnp.where(c == 0, pair[1], pair[0])
    own = jnp.stack([low, high], axis=1).reshape(width, chunk)
    here = (jnp.arange(ranks * 8, dtype=jnp.int32) >> 6) == zh
    own = nt(jnp.where(here[:, None], expand, jnp.zeros_like(expand)), own)
    result = (dot(expand, total.astype(BF)) + own).astype(BF).reshape(ranks, 8, width)
    result = exchange(result, DP).reshape(ranks * 8, width)
    source = jnp.arange(ranks, dtype=jnp.int32)
    chunk_of = (((source >> 3) - (source & 3)) & 3) * 2 + ((source >> 2) & 1)
    fits = chunk_of[None, :, None] == ((own_start + slot) & 7)[:, None, None]
    fits = fits & (eight[None, None, :] == (slot >> 3)[:, None, None])
    fits = fits & (slot < own_length)[:, None, None]
    return dot(fits.astype(BF).reshape(slots, ranks * 8), result).astype(BF)


def solution(mesh):
    mesh = Mesh(mesh.devices.reshape(4, 4, 2, 4, 2), DP + HD)
    in_specs = (
        P(DP, HD),
        P(DP, HD),
        P(DP, None),
        P(DP, None),
        P(None, HD),
        P(None, HD),
        P(HD, DP),
        P(DP, HD),
        P(HD),
        P(HD, DP),
        P(HD, DP),
        P(DP, HD),
        P(),
        P(DP, None),
    )
    return jax.shard_map(
        on_device, mesh=mesh, in_specs=in_specs, out_specs=P(DP, HD), check_vma=False
    )
```

```python
import functools

import jax
import jax.numpy as jnp
from jax import lax
from jax.experimental import pallas as pl
from jax.experimental.pallas import tpu as pltpu
from jax.sharding import Mesh, PartitionSpec as P

BF = jnp.bfloat16
F32 = jnp.float32
NOPE = 128
ROPE = 64
VH = 128
WIN = 32
LIVE = 1024
BLK = 128
STEP = 256
DP = ("zh", "y", "c")
HD = ("x", "zl")


def dot(a, b):
    return jnp.dot(a, b, preferred_element_type=F32)


def shifted(x, axis, shift):
    n = lax.axis_size(axis)
    return lax.ppermute(x, axis, [(i, (i + shift) % n) for i in range(n)])


def iota(shape, dim):
    return lax.broadcasted_iota(jnp.int32, shape, dim)


def nt(a, b):
    return lax.dot_general(a, b, (((1,), (1,)), ((), ())), preferred_element_type=F32)


def whole(shape):
    return pl.BlockSpec(shape, lambda *_: (0,) * len(shape), pipeline_mode=pl.Buffered(1))


def cost(us):
    return pl.CostEstimate(flops=us * 10**9, bytes_accessed=us * 3 * 10**6, transcendentals=0)


def rank_here():
    return (lax.axis_index("zh") * 4 + lax.axis_index("y")) * 2 + lax.axis_index("c")


def live_before(counts_ref):
    place = rank_here()
    return lax.fori_loop(
        0,
        counts_ref.shape[0],
        lambda i, a: a + jnp.where(i < place, counts_ref[i], 0),
        jnp.int32(0),
    )


def pack_kernel(counts_ref, lat_ref, res_ref, *refs):
    outs, rows_ref = refs[:4], refs[4]
    slots, width = res_ref.shape
    half, lanes = width // 2, lat_ref.shape[1]
    zh = lax.axis_index("zh")
    start = live_before(counts_ref)
    i_at, slot = iota((slots, slots), 0), iota((slots, slots), 1)
    roll = ((((i_at >> 3) - start) & 7) + 8 * (i_at & 7)) == slot
    rows_ref[...] = dot(jnp.where(roll, 1.0, 0.0).astype(BF), res_ref[...])
    fill = jnp.zeros((16, lanes - half), F32)
    for s in range(4):
        outs[s][:slots, :] = lat_ref[...]
        for high in range(2):
            m = ((zh + s) & 3) * 2 + high
            piece = rows_ref[pl.ds(pl.multiple_of(m * 8, 8), 8), :]
            piece = jnp.concatenate([piece[:, :half], piece[:, half:]], axis=0)
            piece = jnp.concatenate([piece, fill], axis=1)
            outs[s][slots + 16 * high : slots + 16 * (high + 1), :] = piece.astype(BF)


def pack(counts, latent, residual):
    slots, lanes = latent.shape
    shape = (slots + 32, lanes)
    return pl.pallas_call(
        pack_kernel,
        grid=(1,),
        out_shape=[jax.ShapeDtypeStruct(shape, BF)] * 4,
        in_specs=[
            pl.BlockSpec(memory_space=pltpu.SMEM),
            whole(latent.shape),
            whole(residual.shape),
        ],
        out_specs=[whole(shape)] * 4,
        scratch_shapes=[pltpu.VMEM(residual.shape, F32)],
        cost_estimate=cost(2),
        name="pack",
    )(counts, latent, residual)


def repack_kernel(*refs):
    ins, outs, rows_ref = refs[:4], refs[4:8], refs[8]
    slots = ins[0].shape[0] - 32
    y = lax.axis_index("y")
    for t in range(4):
        rows_ref[t] = ins[t][slots:, :].astype(F32)
    for s in range(4):
        at = pl.ds(pl.multiple_of(((y + s) & 3) * 8, 8), 8)
        for t in range(4):
            outs[s][t * slots : (t + 1) * slots, :] = ins[t][:slots, :]
        for t in (0, 2):
            pair = jnp.concatenate([rows_ref[t, at, :], rows_ref[t + 1, at, :]], axis=0)
            outs[s][4 * slots + 8 * t : 4 * slots + 8 * t + 16, :] = pair.astype(BF)


def repack(*pieces):
    rows, lanes = pieces[0].shape
    shape = (4 * (rows - 32) + 32, lanes)
    return pl.pallas_call(
        repack_kernel,
        grid=(1,),
        out_shape=[jax.ShapeDtypeStruct(shape, BF)] * 4,
        in_specs=[whole(pieces[0].shape)] * 4,
        out_specs=[whole(shape)] * 4,
        scratch_shapes=[pltpu.VMEM((4, 32, lanes), F32)],
        cost_estimate=cost(2),
        name="repack",
    )(*pieces)


def score_kernel(counts_ref, qn_ref, qr_ref, lat_ref, kr_ref, ku_ref, req_ref, out_ref, s_ref):
    slots = lat_ref.shape[0]
    heads = ku_ref.shape[1] // NOPE
    before = live_before(counts_ref)
    keys = dot(lat_ref[...], ku_ref[...]).astype(BF)
    key_rope = kr_ref[...]
    s_at, t_at = iota((slots, slots), 0), iota((slots, slots), 1)
    across = jnp.broadcast_to(req_ref[...], (slots, slots))
    down = jnp.sum(jnp.where(s_at == t_at, across, 0), axis=1, keepdims=True)
    allowed = (across == down) & (t_at <= s_at)
    t_row, lane = iota((slots, BLK), 0), iota((slots, BLK), 1)
    lands = ((before + t_row) & (WIN - 1)) == (lane & (WIN - 1))
    per = BLK // WIN
    for h in range(heads):
        rows = slice(h * slots, (h + 1) * slots)
        s = nt(qn_ref[:, h * NOPE : (h + 1) * NOPE], keys[:, h * NOPE : (h + 1) * NOPE])
        s = s + nt(qr_ref[:, h * ROPE : (h + 1) * ROPE], key_rope)
        s_ref[rows, :] = jnp.where(allowed, s * (NOPE + ROPE) ** (-0.5), jnp.float32(-1e30))
    s = s_ref[...]
    raised = jnp.exp(s - jnp.max(s, axis=-1, keepdims=True))
    w = (raised / jnp.sum(raised, axis=-1, keepdims=True)).astype(BF)
    folded = dot(w, jnp.where(lands, 1.0, 0.0).astype(BF))
    for group in range(heads // per):
        out = folded[group * per * slots : (group * per + 1) * slots]
        for i in range(1, per):
            h = group * per + i
            out = jnp.where((lane >> 5) == i, folded[h * slots : (h + 1) * slots], out)
        for copy in range(out_ref.shape[0]):
            out_ref[copy, :, group * BLK : (group + 1) * BLK] = out.astype(BF)


def score_weights(counts, *arrays):
    slots, heads = arrays[2].shape[0], arrays[4].shape[1] // NOPE
    shape = (4, slots, heads * WIN)
    return pl.pallas_call(
        score_kernel,
        grid=(1,),
        out_shape=jax.ShapeDtypeStruct(shape, BF),
        in_specs=[pl.BlockSpec(memory_space=pltpu.SMEM)] + [whole(a.shape) for a in arrays],
        out_specs=whole(shape),
        scratch_shapes=[pltpu.VMEM((slots * heads, slots), F32)],
        cost_estimate=cost(4),
        name="score_weights",
    )(counts, *arrays)


def live_rows(goes_ref, own_ref, other_ref):
    row = iota((STEP, own_ref.shape[0]), 0) + pl.program_id(0) * STEP
    out = dot(jnp.where(goes_ref[0] == row, 1.0, 0.0).astype(BF), own_ref[...])
    out = out + dot(jnp.where(goes_ref[1] == row, 1.0, 0.0).astype(BF), other_ref[...])
    return out.astype(BF)


def values_kernel(goes_ref, own_ref, other_ref, up_ref, out_ref):
    out_ref[...] = dot(live_rows(goes_ref, own_ref, other_ref), up_ref[...]).astype(BF)


def live_values(goes, own, other, up):
    width = up.shape[1]
    return pl.pallas_call(
        values_kernel,
        grid=(LIVE // STEP,),
        out_shape=jax.ShapeDtypeStruct((LIVE, width), BF),
        in_specs=[whole(a.shape) for a in (goes, own, other, up)],
        out_specs=pl.BlockSpec((STEP, width), lambda b: (b, 0)),
        cost_estimate=cost(0),
        compiler_params=pltpu.CompilerParams(vmem_limit_bytes=24 * 2**20),
        name="live_values",
    )(goes, own, other, up)


def mix_kernel(goes_ref, own_ref, other_ref, prev_ref, cur_ref, wo_ref, out_ref, att_ref, all_ref):
    b = pl.program_id(0)
    heads = cur_ref.shape[1] // VH
    r_at, l_at = iota((BLK, BLK), 0), iota((BLK, BLK), 1)
    gap = r_at - l_at
    near = (gap >= 0) & (gap < WIN)
    per = BLK // WIN
    masks = [jnp.where(near & ((l_at >> 5) == q), 1.0, 0.0).astype(BF) for q in range(per)]
    r_at, l_at = iota((WIN, BLK), 0), iota((WIN, BLK), 1)
    before = jnp.where((BLK + r_at - l_at) < WIN, 1.0, 0.0).astype(BF)
    blank = jnp.zeros((BLK - WIN, BLK), BF)
    packed = live_rows(goes_ref, own_ref, other_ref)
    for group in range(heads // per):
        one = packed[:, group * BLK : (group + 1) * BLK].astype(F32)
        turned = [one.astype(BF)]
        for q in range(1, per):
            turned.append(pltpu.roll(one, q * WIN, 1).astype(BF))
        for i in range(per):
            cols = slice((group * per + i) * VH, (group * per + i + 1) * VH)
            last = turned[(per - 1 - i) % per]
            olds = [prev_ref[:, cols], cur_ref[:BLK, cols]]
            for t in range(STEP // BLK):
                rows = slice(t * BLK, (t + 1) * BLK)
                band = turned[(-i) % per][rows] * masks[0]
                for q in range(1, per):
                    band = band + turned[(q - i) % per][rows] * masks[q]
                corner = jnp.concatenate([last[rows][:WIN] * before, blank], axis=0)
                att = dot(
                    jnp.concatenate([corner, band], axis=1),
                    jnp.concatenate([olds[t], cur_ref[rows, cols]], axis=0),
                )
                att_ref[rows, cols] = att.astype(BF)
    part = nt(att_ref[...], wo_ref[...]).astype(BF)
    share = STEP // 8
    r_at, l_at = iota((STEP, STEP), 0), iota((STEP, STEP), 1)
    order = ((r_at & (share - 1)) * 8 + (r_at >> 5)) == l_at
    part = dot(jnp.where(order, 1.0, 0.0).astype(BF), part)
    rows = pl.ds(pl.multiple_of(b * share, share), share)
    for m in range(8):
        all_ref[m, rows, :] = part[m * share : (m + 1) * share]

    @pl.when(b == pl.num_programs(0) - 1)
    def _():
        for m in range(8):
            out_ref[m] = all_ref[m].T.astype(BF)


def mix_project(goes, own, other, values, wo):
    width = values.shape[1]
    n = wo.shape[0]
    shape = (8, n, LIVE // 8)
    return pl.pallas_call(
        mix_kernel,
        grid=(LIVE // STEP,),
        out_shape=jax.ShapeDtypeStruct(shape, BF),
        in_specs=[
            whole(goes.shape),
            whole(own.shape),
            whole(other.shape),
            pl.BlockSpec((BLK, width), lambda b: (jnp.maximum(b * (STEP // BLK) - 1, 0), 0)),
            pl.BlockSpec((STEP, width), lambda b: (b, 0)),
            whole(wo.shape),
        ],
        out_specs=whole(shape),
        scratch_shapes=[pltpu.VMEM((STEP, width), BF), pltpu.VMEM((8, LIVE // 8, n), F32)],
        cost_estimate=cost(9),
        compiler_params=pltpu.CompilerParams(vmem_limit_bytes=50 * 2**20),
        name="mix_project",
    )(goes, own, other, values, values, wo)


def gate_up_kernel(steps, own_ref, other_ref, gain_ref, gate_ref, up_ref, *refs):
    outs, x_ref = refs[:-1], refs[-1]
    core, y = lax.axis_index("c"), lax.axis_index("y")
    x_at, zl = lax.axis_index("x"), lax.axis_index("zl")
    k, chunk = own_ref.shape[2:]
    ff = gate_ref.shape[0]
    gain = jnp.broadcast_to(gain_ref[...], (8, gain_ref.shape[1])).T
    x_ref[:, :8] = gain.astype(F32)
    squares = []
    scaled = []
    for dx, dz in steps:
        spot = ((x_at + dx) & 3) * 2 + (zl ^ dz)
        total = jnp.zeros((1, chunk), F32)
        for low in range(2):
            s = (y - (spot >> 2) * 2 - low) & 3
            one, two = own_ref[s, spot & 3], other_ref[s, spot & 3]
            for half in range(2):
                x = jnp.where(core == half, one, two).astype(F32)
                total = total + jnp.sum(x * x, axis=0, keepdims=True)
                rows = slice((low * 2 + half) * k, (low * 2 + half + 1) * k)
                scaled.append((x * x_ref[rows, :1]).astype(BF))
        squares.append(total)
    columns = [
        jnp.concatenate(scaled[4 * i : 4 * i + 4], axis=0) for i in range(len(steps))
    ]
    x = jnp.concatenate(columns, axis=1)
    gate = dot(gate_ref[...], x).astype(BF)
    up = dot(up_ref[...], x).astype(BF)
    row = iota((16, chunk), 0)
    for i, out_ref in enumerate(outs):
        cols = slice(i * chunk, (i + 1) * chunk)
        high = squares[i].astype(BF).astype(F32)
        extra = jnp.where(row == 0, high, jnp.where(row == 1, squares[i] - high, 0.0))
        out_ref[:ff, :] = gate[:, cols]
        out_ref[ff : 2 * ff, :] = up[:, cols]
        out_ref[2 * ff :, :] = extra.astype(BF)


def gate_up(steps, own, other, gain, gate_weight, up_weight):
    k, chunk = own.shape[2:]
    ff, width = gate_weight.shape
    shape = (2 * ff + 16, chunk)
    arrays = (own, other, gain, gate_weight, up_weight)
    return pl.pallas_call(
        functools.partial(gate_up_kernel, steps),
        grid=(1,),
        out_shape=[jax.ShapeDtypeStruct(shape, BF)] * len(steps),
        in_specs=[whole(a.shape) for a in arrays],
        out_specs=[whole(shape)] * len(steps),
        scratch_shapes=[pltpu.VMEM((width, BLK), F32)],
        cost_estimate=cost(4),
        compiler_params=pltpu.CompilerParams(vmem_limit_bytes=24 * 2**20),
        name="gate_up",
    )(*arrays)


def exchange(x, axes):
    return lax.all_to_all(x, axes, split_axis=0, concat_axis=0, tiled=True)


def gather(x, axes):
    n = lax.axis_size(axes)
    return exchange(jnp.broadcast_to(x[None], (n,) + x.shape), axes)


def pick(x, index):
    return lax.dynamic_index_in_dim(x, index, 0, keepdims=False)


def on_device(
    query_nope,
    query_rope,
    latent,
    key_rope,
    key_up,
    value_up,
    output_weight,
    residual,
    norm_gain,
    gate_weight,
    up_weight,
    down_weight,
    rank_tokens,
    request_ids,
):
    slots = latent.shape[0]
    ranks = rank_tokens.shape[0]
    zh, y, c = (lax.axis_index(a) for a in DP)
    rank = (zh * 4 + y) * 2 + c
    chunk = LIVE // 8
    width = residual.shape[1]
    quarter = width // 4
    model = 8 * width

    every = jnp.arange(ranks, dtype=jnp.int32)

    def starts(which):
        return jnp.sum(jnp.where(every < which[..., None], rank_tokens, 0), axis=-1)

    def lengths(which):
        return jnp.sum(jnp.where(every == which[..., None], rank_tokens, 0), axis=-1)

    own_start, own_length = starts(rank), lengths(rank)
    slot = jnp.arange(slots, dtype=jnp.int32)

    pieces = pack(rank_tokens, latent, residual)
    pieces = [pieces[0]] + [shifted(pieces[s], "zh", s) for s in (1, 2, 3)]

    weights = score_weights(
        rank_tokens, query_nope, query_rope, latent, key_rope, key_up, request_ids
    )
    weights = exchange(weights, "zh")
    pieces = repack(*pieces)
    weights, gain, _ = lax.optimization_barrier((weights, norm_gain[None, :], pieces))
    weights = jnp.broadcast_to(weights[None], (4,) + weights.shape)
    pieces = [pieces[0]] + [shifted(pieces[s], "y", s) for s in (1, 2, 3)]
    pieces, weights = lax.optimization_barrier((pieces, weights))
    got = jnp.concatenate(pieces, axis=0)
    got_other = shifted(got, "c", 1)
    weights = exchange(weights, "y").reshape(-1, weights.shape[3])

    four = jnp.arange(4, dtype=jnp.int32)
    eight = jnp.arange(8, dtype=jnp.int32)
    core = jnp.stack([c, 1 - c])[:, None, None]
    ahead = (four[None, None, :] * 4 + four[None, :, None]) * 2 + core
    goes = jnp.where(slot < lengths(ahead)[..., None], starts(ahead)[..., None] + slot, -1)
    goes = goes.reshape(2, 1, -1)
    back = (((zh - four) & 3)[None, None, :] * 4 + ((y - four) & 3)[None, :, None]) * 2 + core
    back_start, back_count = starts(back)[..., None], lengths(back)[..., None]
    goes_back = jnp.where(slot < back_count, back_start + slot, -1).reshape(2, 4, -1)
    goes_back = jnp.pad(goes_back, ((0, 0), (0, 0), (0, 32)), constant_values=-1).reshape(2, 1, -1)
    values = live_values(goes_back, got, got_other, value_up)

    swap = []
    for a in range(4):
        for b in range(8):
            for e in range(4):
                for f in range(2):
                    to = (e * 8 + (f * 4 + (b & 3))) * 8 + a * 2 + (b >> 2)
                    swap.append(((a * 8 + b) * 8 + e * 2 + f, to))
    place = (((zh * 2 + (y >> 1)) - back_start) & 7) + 8 * eight
    come = jnp.where(place < back_count, (back_start + place) >> 3, -1)
    come = (come.reshape(2, -1, 1) == jnp.arange(chunk, dtype=jnp.int32)).astype(BF)

    def tn(a, b):
        return lax.dot_general(a, b, (((0,), (0,)), ((), ())), preferred_element_type=F32)

    rows = [a.reshape(4, -1, a.shape[1])[:, 4 * slots :].reshape(-1, a.shape[1]) for a in (got, got_other)]
    rows = tn(rows[0], come[0]) + tn(rows[1], come[1])
    rows = jnp.where(c == 0, rows[:quarter], rows[quarter : 2 * quarter]).astype(BF)
    rows, values = lax.optimization_barrier((rows, values))
    rows = lax.ppermute(rows, DP + HD, swap)

    weights, values = lax.optimization_barrier((weights, values))
    weights_other = shifted(weights, "c", 1)
    part = mix_project(goes, weights, weights_other, values, output_weight.T)
    projected = jnp.sum(exchange(part, HD).astype(F32), axis=0)
    mixed = (rows.astype(F32) + projected).astype(BF)

    full = []
    for k in range(4):
        sends = []
        for a in range(4):
            for b in range(8):
                for e in range(4):
                    for f in range(2):
                        to = (((e + k) & 3) * 8 + (f * 4 + (b & 3))) * 8 + a * 2 + (b >> 2)
                        sends.append(((a * 8 + b) * 8 + e * 2 + f, to))
        full.append(lax.ppermute(mixed, DP + HD, sends))
    full = jnp.stack(full)

    full = jnp.stack([full] + [shifted(full, "y", s) for s in (1, 2, 3)])
    full_other = shifted(full, "c", 1)
    ff = down_weight.shape[0]
    arrays = (full, full_other, gain, gate_weight.T, up_weight.T)
    near = [(0, 0), (1, 0), (3, 0), (2, 0)]
    far = [(0, 1), (1, 1), (3, 1), (2, 1)]
    parts = list(zip(near, gate_up(near, *arrays))) + list(zip(far, gate_up(far, *arrays)))
    total = parts[0][1].astype(F32)
    for (dx, dz), part in parts[1:]:
        sends = [(i, ((i // 2 + dx) % 4) * 2 + ((i % 2) ^ dz)) for i in range(8)]
        total = total + lax.ppermute(part, HD, sends).astype(F32)
    scale = lax.rsqrt((total[2 * ff : 2 * ff + 1] + total[2 * ff + 1 : 2 * ff + 2]) / model + 1e-06)
    hidden = (jax.nn.silu(total[:ff] * scale) * (total[ff : 2 * ff] * scale)).astype(BF)
    hidden = gather(hidden, HD).reshape(4, 2, ff, chunk)

    def down(core):
        piece = lax.dynamic_index_in_dim(hidden, core, 1, keepdims=False)
        return lax.dot_general(
            piece, down_weight, (((1,), (0,)), ((), ())), preferred_element_type=F32
        )

    sent = shifted(down(1 - c).astype(BF), "c", 1)
    total = down(c) + sent.astype(F32)
    pieces = [pick(total, (y + s) & 3) for s in range(4)]
    total = pieces[0]
    for s in (1, 2, 3):
        total = total + shifted(pieces[s].astype(BF), "y", s).astype(F32)
    spot = y * 2 + c
    begin = starts(every)
    m = ((zh - (spot & 3)) & 3) * 2 + (spot >> 2)
    place = ((m - begin[:, None]) & 7) + 8 * eight[None, :]
    comes = jnp.where(place < rank_tokens[:, None], (begin[:, None] + place) >> 3, -1)
    expand = (comes.reshape(ranks * 8, 1) == jnp.arange(chunk, dtype=jnp.int32)).astype(BF)
    at = [(y - (spot >> 2) * 2 - low) & 3 for low in range(2)]
    pair = [jnp.stack([pick(pick(a, s), spot & 3) for s in at]) for a in (full, full_other)]
    low = jnp.where(c == 0, pair[0], pair[1])
    high = jnp.where(c == 0, pair[1], pair[0])
    own = jnp.stack([low, high], axis=1).reshape(width, chunk)
    here = (jnp.arange(ranks * 8, dtype=jnp.int32) >> 6) == zh
    own = nt(jnp.where(here[:, None], expand, jnp.zeros_like(expand)), own)
    result = (dot(expand, total.astype(BF)) + own).astype(BF).reshape(ranks, 8, width)
    result = exchange(result, DP).reshape(ranks * 8, width)
    source = jnp.arange(ranks, dtype=jnp.int32)
    chunk_of = (((source >> 3) - (source & 3)) & 3) * 2 + ((source >> 2) & 1)
    fits = chunk_of[None, :, None] == ((own_start + slot) & 7)[:, None, None]
    fits = fits & (eight[None, None, :] == (slot >> 3)[:, None, None])
    fits = fits & (slot < own_length)[:, None, None]
    return dot(fits.astype(BF).reshape(slots, ranks * 8), result).astype(BF)


def solution(mesh):
    mesh = Mesh(mesh.devices.reshape(4, 4, 2, 4, 2), DP + HD)
    in_specs = (
        P(DP, HD),
        P(DP, HD),
        P(DP, None),
        P(DP, None),
        P(None, HD),
        P(None, HD),
        P(HD, DP),
        P(DP, HD),
        P(HD),
        P(HD, DP),
        P(HD, DP),
        P(DP, HD),
        P(),
        P(DP, None),
    )
    return jax.shard_map(
        on_device, mesh=mesh, in_specs=in_specs, out_specs=P(DP, HD), check_vma=False
    )
```

```python
import functools

import jax
import jax.numpy as jnp
from jax import lax
from jax.experimental import pallas as pl
from jax.experimental.pallas import tpu as pltpu
from jax.sharding import Mesh, PartitionSpec as P

BF = jnp.bfloat16
F32 = jnp.float32
NOPE = 128
ROPE = 64
VH = 128
WIN = 32
LIVE = 1024
BLK = 128
STEP = 256
DP = ("zh", "y", "c")
HD = ("x", "zl")


def dot(a, b):
    return jnp.dot(a, b, preferred_element_type=F32)


def shifted(x, axis, shift):
    n = lax.axis_size(axis)
    return lax.ppermute(x, axis, [(i, (i + shift) % n) for i in range(n)])


def iota(shape, dim):
    return lax.broadcasted_iota(jnp.int32, shape, dim)


def nt(a, b):
    return lax.dot_general(a, b, (((1,), (1,)), ((), ())), preferred_element_type=F32)


def whole(shape):
    return pl.BlockSpec(shape, lambda *_: (0,) * len(shape), pipeline_mode=pl.Buffered(1))


def cost(us):
    return pl.CostEstimate(flops=us * 10**9, bytes_accessed=us * 3 * 10**6, transcendentals=0)


def rank_here():
    return (lax.axis_index("zh") * 4 + lax.axis_index("y")) * 2 + lax.axis_index("c")


def live_before(counts_ref):
    place = rank_here()
    return lax.fori_loop(
        0,
        counts_ref.shape[0],
        lambda i, a: a + jnp.where(i < place, counts_ref[i], 0),
        jnp.int32(0),
    )


def pack_kernel(counts_ref, lat_ref, res_ref, *refs):
    outs, rows_ref = refs[:4], refs[4]
    slots, width = res_ref.shape
    half, lanes = width // 2, lat_ref.shape[1]
    zh = lax.axis_index("zh")
    start = live_before(counts_ref)
    i_at, slot = iota((slots, slots), 0), iota((slots, slots), 1)
    roll = ((((i_at >> 3) - start) & 7) + 8 * (i_at & 7)) == slot
    rows_ref[...] = dot(jnp.where(roll, 1.0, 0.0).astype(BF), res_ref[...])
    fill = jnp.zeros((16, lanes - half), F32)
    for s in range(4):
        outs[s][:slots, :] = lat_ref[...]
        for high in range(2):
            m = ((zh + s) & 3) * 2 + high
            piece = rows_ref[pl.ds(pl.multiple_of(m * 8, 8), 8), :]
            piece = jnp.concatenate([piece[:, :half], piece[:, half:]], axis=0)
            piece = jnp.concatenate([piece, fill], axis=1)
            outs[s][slots + 16 * high : slots + 16 * (high + 1), :] = piece.astype(BF)


def pack(counts, latent, residual):
    slots, lanes = latent.shape
    shape = (slots + 32, lanes)
    return pl.pallas_call(
        pack_kernel,
        grid=(1,),
        out_shape=[jax.ShapeDtypeStruct(shape, BF)] * 4,
        in_specs=[
            pl.BlockSpec(memory_space=pltpu.SMEM),
            whole(latent.shape),
            whole(residual.shape),
        ],
        out_specs=[whole(shape)] * 4,
        scratch_shapes=[pltpu.VMEM(residual.shape, F32)],
        cost_estimate=cost(2),
        name="pack",
    )(counts, latent, residual)


def repack_kernel(*refs):
    ins, outs, rows_ref = refs[:4], refs[4:8], refs[8]
    slots = ins[0].shape[0] - 32
    y = lax.axis_index("y")
    for t in range(4):
        rows_ref[t] = ins[t][slots:, :].astype(F32)
    for s in range(4):
        at = pl.ds(pl.multiple_of(((y + s) & 3) * 8, 8), 8)
        for t in range(4):
            outs[s][t * slots : (t + 1) * slots, :] = ins[t][:slots, :]
        for t in (0, 2):
            pair = jnp.concatenate([rows_ref[t, at, :], rows_ref[t + 1, at, :]], axis=0)
            outs[s][4 * slots + 8 * t : 4 * slots + 8 * t + 16, :] = pair.astype(BF)


def repack(*pieces):
    rows, lanes = pieces[0].shape
    shape = (4 * (rows - 32) + 32, lanes)
    return pl.pallas_call(
        repack_kernel,
        grid=(1,),
        out_shape=[jax.ShapeDtypeStruct(shape, BF)] * 4,
        in_specs=[whole(pieces[0].shape)] * 4,
        out_specs=[whole(shape)] * 4,
        scratch_shapes=[pltpu.VMEM((4, 32, lanes), F32)],
        cost_estimate=cost(2),
        name="repack",
    )(*pieces)


def score_kernel(counts_ref, qn_ref, qr_ref, lat_ref, kr_ref, ku_ref, req_ref, out_ref, s_ref):
    slots = lat_ref.shape[0]
    heads = ku_ref.shape[1] // NOPE
    before = live_before(counts_ref)
    keys = dot(lat_ref[...], ku_ref[...]).astype(BF)
    key_rope = kr_ref[...]
    s_at, t_at = iota((slots, slots), 0), iota((slots, slots), 1)
    across = jnp.broadcast_to(req_ref[...], (slots, slots))
    down = jnp.sum(jnp.where(s_at == t_at, across, 0), axis=1, keepdims=True)
    allowed = (across == down) & (t_at <= s_at)
    t_row, lane = iota((slots, BLK), 0), iota((slots, BLK), 1)
    lands = ((before + t_row) & (WIN - 1)) == (lane & (WIN - 1))
    per = BLK // WIN
    for h in range(heads):
        rows = slice(h * slots, (h + 1) * slots)
        s = nt(qn_ref[:, h * NOPE : (h + 1) * NOPE], keys[:, h * NOPE : (h + 1) * NOPE])
        s = s + nt(qr_ref[:, h * ROPE : (h + 1) * ROPE], key_rope)
        s_ref[rows, :] = jnp.where(allowed, s * (NOPE + ROPE) ** (-0.5), jnp.float32(-1e30))
    s = s_ref[...]
    raised = jnp.exp(s - jnp.max(s, axis=-1, keepdims=True))
    w = (raised / jnp.sum(raised, axis=-1, keepdims=True)).astype(BF)
    folded = dot(w, jnp.where(lands, 1.0, 0.0).astype(BF))
    for group in range(heads // per):
        out = folded[group * per * slots : (group * per + 1) * slots]
        for i in range(1, per):
            h = group * per + i
            out = jnp.where((lane >> 5) == i, folded[h * slots : (h + 1) * slots], out)
        for copy in range(out_ref.shape[0]):
            out_ref[copy, :, group * BLK : (group + 1) * BLK] = out.astype(BF)


def score_weights(counts, *arrays):
    slots, heads = arrays[2].shape[0], arrays[4].shape[1] // NOPE
    shape = (4, slots, heads * WIN)
    return pl.pallas_call(
        score_kernel,
        grid=(1,),
        out_shape=jax.ShapeDtypeStruct(shape, BF),
        in_specs=[pl.BlockSpec(memory_space=pltpu.SMEM)] + [whole(a.shape) for a in arrays],
        out_specs=whole(shape),
        scratch_shapes=[pltpu.VMEM((slots * heads, slots), F32)],
        cost_estimate=cost(4),
        compiler_params=pltpu.CompilerParams(vmem_limit_bytes=16 * 2**20),
        name="score_weights",
    )(counts, *arrays)


def live_rows(goes_ref, own_ref, other_ref):
    row = iota((STEP, own_ref.shape[0]), 0) + pl.program_id(0) * STEP
    out = dot(jnp.where(goes_ref[0] == row, 1.0, 0.0).astype(BF), own_ref[...])
    out = out + dot(jnp.where(goes_ref[1] == row, 1.0, 0.0).astype(BF), other_ref[...])
    return out.astype(BF)


def values_kernel(goes_ref, own_ref, other_ref, up_ref, out_ref):
    out_ref[...] = dot(live_rows(goes_ref, own_ref, other_ref), up_ref[...]).astype(BF)


def live_values(goes, own, other, up):
    width = up.shape[1]
    return pl.pallas_call(
        values_kernel,
        grid=(LIVE // STEP,),
        out_shape=jax.ShapeDtypeStruct((LIVE, width), BF),
        in_specs=[whole(a.shape) for a in (goes, own, other, up)],
        out_specs=pl.BlockSpec((STEP, width), lambda b: (b, 0)),
        cost_estimate=cost(0),
        compiler_params=pltpu.CompilerParams(vmem_limit_bytes=24 * 2**20),
        name="live_values",
    )(goes, own, other, up)


def mix_kernel(goes_ref, own_ref, other_ref, prev_ref, cur_ref, wo_ref, out_ref, att_ref, all_ref):
    b = pl.program_id(0)
    heads = cur_ref.shape[1] // VH
    r_at, l_at = iota((BLK, BLK), 0), iota((BLK, BLK), 1)
    gap = r_at - l_at
    near = (gap >= 0) & (gap < WIN)
    per = BLK // WIN
    masks = [jnp.where(near & ((l_at >> 5) == q), 1.0, 0.0).astype(BF) for q in range(per)]
    r_at, l_at = iota((WIN, BLK), 0), iota((WIN, BLK), 1)
    before = jnp.where((BLK + r_at - l_at) < WIN, 1.0, 0.0).astype(BF)
    blank = jnp.zeros((BLK - WIN, BLK), BF)
    packed = live_rows(goes_ref, own_ref, other_ref)
    for group in range(heads // per):
        one = packed[:, group * BLK : (group + 1) * BLK].astype(F32)
        turned = [one.astype(BF)]
        for q in range(1, per):
            turned.append(pltpu.roll(one, q * WIN, 1).astype(BF))
        for i in range(per):
            cols = slice((group * per + i) * VH, (group * per + i + 1) * VH)
            last = turned[(per - 1 - i) % per]
            olds = [prev_ref[:, cols], cur_ref[:BLK, cols]]
            for t in range(STEP // BLK):
                rows = slice(t * BLK, (t + 1) * BLK)
                band = turned[(-i) % per][rows] * masks[0]
                for q in range(1, per):
                    band = band + turned[(q - i) % per][rows] * masks[q]
                corner = jnp.concatenate([last[rows][:WIN] * before, blank], axis=0)
                att = dot(
                    jnp.concatenate([corner, band], axis=1),
                    jnp.concatenate([olds[t], cur_ref[rows, cols]], axis=0),
                )
                att_ref[rows, cols] = att.astype(BF)
    part = nt(att_ref[...], wo_ref[...]).astype(BF)
    share = STEP // 8
    r_at, l_at = iota((STEP, STEP), 0), iota((STEP, STEP), 1)
    order = ((r_at & (share - 1)) * 8 + (r_at >> 5)) == l_at
    part = dot(jnp.where(order, 1.0, 0.0).astype(BF), part)
    rows = pl.ds(pl.multiple_of(b * share, share), share)
    for m in range(8):
        all_ref[m, rows, :] = part[m * share : (m + 1) * share]

    @pl.when(b == pl.num_programs(0) - 1)
    def _():
        for m in range(8):
            out_ref[m] = all_ref[m].T.astype(BF)


def mix_project(goes, own, other, values, wo):
    width = values.shape[1]
    n = wo.shape[0]
    shape = (8, n, LIVE // 8)
    return pl.pallas_call(
        mix_kernel,
        grid=(LIVE // STEP,),
        out_shape=jax.ShapeDtypeStruct(shape, BF),
        in_specs=[
            whole(goes.shape),
            whole(own.shape),
            whole(other.shape),
            pl.BlockSpec((BLK, width), lambda b: (jnp.maximum(b * (STEP // BLK) - 1, 0), 0)),
            pl.BlockSpec((STEP, width), lambda b: (b, 0)),
            whole(wo.shape),
        ],
        out_specs=whole(shape),
        scratch_shapes=[pltpu.VMEM((STEP, width), BF), pltpu.VMEM((8, LIVE // 8, n), F32)],
        cost_estimate=cost(9),
        compiler_params=pltpu.CompilerParams(vmem_limit_bytes=50 * 2**20),
        name="mix_project",
    )(goes, own, other, values, values, wo)


def gate_up_kernel(steps, own_ref, other_ref, gain_ref, gate_ref, up_ref, *refs):
    outs, x_ref = refs[:-1], refs[-1]
    core, y = lax.axis_index("c"), lax.axis_index("y")
    x_at, zl = lax.axis_index("x"), lax.axis_index("zl")
    k, chunk = own_ref.shape[2:]
    ff = gate_ref.shape[0]
    gain = jnp.broadcast_to(gain_ref[...], (8, gain_ref.shape[1])).T
    x_ref[:, :8] = gain.astype(F32)
    squares = []
    scaled = []
    for dx, dz in steps:
        spot = ((x_at + dx) & 3) * 2 + (zl ^ dz)
        total = jnp.zeros((1, chunk), F32)
        for low in range(2):
            s = (y - (spot >> 2) * 2 - low) & 3
            one, two = own_ref[s, spot & 3], other_ref[s, spot & 3]
            for half in range(2):
                x = jnp.where(core == half, one, two).astype(F32)
                total = total + jnp.sum(x * x, axis=0, keepdims=True)
                rows = slice((low * 2 + half) * k, (low * 2 + half + 1) * k)
                scaled.append((x * x_ref[rows, :1]).astype(BF))
        squares.append(total)
    columns = [
        jnp.concatenate(scaled[4 * i : 4 * i + 4], axis=0) for i in range(len(steps))
    ]
    x = jnp.concatenate(columns, axis=1)
    gate = dot(gate_ref[...], x).astype(BF)
    up = dot(up_ref[...], x).astype(BF)
    row = iota((16, chunk), 0)
    for i, out_ref in enumerate(outs):
        cols = slice(i * chunk, (i + 1) * chunk)
        high = squares[i].astype(BF).astype(F32)
        extra = jnp.where(row == 0, high, jnp.where(row == 1, squares[i] - high, 0.0))
        out_ref[:ff, :] = gate[:, cols]
        out_ref[ff : 2 * ff, :] = up[:, cols]
        out_ref[2 * ff :, :] = extra.astype(BF)


def gate_up(steps, own, other, gain, gate_weight, up_weight):
    k, chunk = own.shape[2:]
    ff, width = gate_weight.shape
    shape = (2 * ff + 16, chunk)
    arrays = (own, other, gain, gate_weight, up_weight)
    return pl.pallas_call(
        functools.partial(gate_up_kernel, steps),
        grid=(1,),
        out_shape=[jax.ShapeDtypeStruct(shape, BF)] * len(steps),
        in_specs=[whole(a.shape) for a in arrays],
        out_specs=[whole(shape)] * len(steps),
        scratch_shapes=[pltpu.VMEM((width, BLK), F32)],
        cost_estimate=cost(4),
        compiler_params=pltpu.CompilerParams(vmem_limit_bytes=24 * 2**20),
        name="gate_up",
    )(*arrays)


def exchange(x, axes):
    return lax.all_to_all(x, axes, split_axis=0, concat_axis=0, tiled=True)


def gather(x, axes):
    n = lax.axis_size(axes)
    return exchange(jnp.broadcast_to(x[None], (n,) + x.shape), axes)


def pick(x, index):
    return lax.dynamic_index_in_dim(x, index, 0, keepdims=False)


def on_device(
    query_nope,
    query_rope,
    latent,
    key_rope,
    key_up,
    value_up,
    output_weight,
    residual,
    norm_gain,
    gate_weight,
    up_weight,
    down_weight,
    rank_tokens,
    request_ids,
):
    slots = latent.shape[0]
    ranks = rank_tokens.shape[0]
    zh, y, c = (lax.axis_index(a) for a in DP)
    rank = (zh * 4 + y) * 2 + c
    chunk = LIVE // 8
    width = residual.shape[1]
    quarter = width // 4
    model = 8 * width

    every = jnp.arange(ranks, dtype=jnp.int32)

    def starts(which):
        return jnp.sum(jnp.where(every < which[..., None], rank_tokens, 0), axis=-1)

    def lengths(which):
        return jnp.sum(jnp.where(every == which[..., None], rank_tokens, 0), axis=-1)

    own_start, own_length = starts(rank), lengths(rank)
    slot = jnp.arange(slots, dtype=jnp.int32)

    pieces = pack(rank_tokens, latent, residual)
    pieces = [pieces[0]] + [shifted(pieces[s], "zh", s) for s in (1, 2, 3)]

    weights = score_weights(
        rank_tokens, query_nope, query_rope, latent, key_rope, key_up, request_ids
    )
    weights = exchange(weights, "zh")
    pieces = repack(*pieces)
    weights, gain, _ = lax.optimization_barrier((weights, norm_gain[None, :], pieces))
    weights = jnp.broadcast_to(weights[None], (4,) + weights.shape)
    pieces = [pieces[0]] + [shifted(pieces[s], "y", s) for s in (1, 2, 3)]
    pieces, weights = lax.optimization_barrier((pieces, weights))
    got = jnp.concatenate(pieces, axis=0)
    got_other = shifted(got, "c", 1)
    weights = exchange(weights, "y").reshape(-1, weights.shape[3])

    four = jnp.arange(4, dtype=jnp.int32)
    eight = jnp.arange(8, dtype=jnp.int32)
    core = jnp.stack([c, 1 - c])[:, None, None]
    ahead = (four[None, None, :] * 4 + four[None, :, None]) * 2 + core
    goes = jnp.where(slot < lengths(ahead)[..., None], starts(ahead)[..., None] + slot, -1)
    goes = goes.reshape(2, 1, -1)
    back = (((zh - four) & 3)[None, None, :] * 4 + ((y - four) & 3)[None, :, None]) * 2 + core
    back_start, back_count = starts(back)[..., None], lengths(back)[..., None]
    goes_back = jnp.where(slot < back_count, back_start + slot, -1).reshape(2, 4, -1)
    goes_back = jnp.pad(goes_back, ((0, 0), (0, 0), (0, 32)), constant_values=-1).reshape(2, 1, -1)
    values = live_values(goes_back, got, got_other, value_up)

    swap = []
    for a in range(4):
        for b in range(8):
            for e in range(4):
                for f in range(2):
                    to = (e * 8 + (f * 4 + (b & 3))) * 8 + a * 2 + (b >> 2)
                    swap.append(((a * 8 + b) * 8 + e * 2 + f, to))
    place = (((zh * 2 + (y >> 1)) - back_start) & 7) + 8 * eight
    come = jnp.where(place < back_count, (back_start + place) >> 3, -1)
    come = (come.reshape(2, -1, 1) == jnp.arange(chunk, dtype=jnp.int32)).astype(BF)

    def tn(a, b):
        return lax.dot_general(a, b, (((0,), (0,)), ((), ())), preferred_element_type=F32)

    rows = [a.reshape(4, -1, a.shape[1])[:, 4 * slots :].reshape(-1, a.shape[1]) for a in (got, got_other)]
    rows = tn(rows[0], come[0]) + tn(rows[1], come[1])
    rows = jnp.where(c == 0, rows[:quarter], rows[quarter : 2 * quarter]).astype(BF)
    rows, values = lax.optimization_barrier((rows, values))
    rows = lax.ppermute(rows, DP + HD, swap)

    weights, values, rows = lax.optimization_barrier((weights, values, rows))
    weights_other = shifted(weights, "c", 1)
    part = mix_project(goes, weights, weights_other, values, output_weight.T)
    projected = jnp.sum(exchange(part, HD).astype(F32), axis=0)
    mixed = (rows.astype(F32) + projected).astype(BF)

    full = jnp.stack([mixed] + [shifted(mixed, "x", k) for k in (1, 2, 3)])
    full = lax.ppermute(full, DP + HD, swap)

    full = jnp.stack([full] + [shifted(full, "y", s) for s in (1, 2, 3)])
    full_other = shifted(full, "c", 1)
    ff = down_weight.shape[0]
    arrays = (full, full_other, gain, gate_weight.T, up_weight.T)
    near = [(0, 0), (1, 0), (3, 0), (2, 0)]
    far = [(0, 1), (1, 1), (3, 1), (2, 1)]
    parts = list(zip(near, gate_up(near, *arrays))) + list(zip(far, gate_up(far, *arrays)))
    total = parts[0][1].astype(F32)
    for (dx, dz), part in parts[1:]:
        sends = [(i, ((i // 2 + dx) % 4) * 2 + ((i % 2) ^ dz)) for i in range(8)]
        total = total + lax.ppermute(part, HD, sends).astype(F32)
    scale = lax.rsqrt((total[2 * ff : 2 * ff + 1] + total[2 * ff + 1 : 2 * ff + 2]) / model + 1e-06)
    hidden = (jax.nn.silu(total[:ff] * scale) * (total[ff : 2 * ff] * scale)).astype(BF)
    hidden = gather(hidden, HD).reshape(4, 2, ff, chunk)

    def down(core):
        piece = lax.dynamic_index_in_dim(hidden, core, 1, keepdims=False)
        return lax.dot_general(
            piece, down_weight, (((1,), (0,)), ((), ())), preferred_element_type=F32
        )

    sent = shifted(down(1 - c).astype(BF), "c", 1)
    total = down(c) + sent.astype(F32)
    pieces = [pick(total, (y + s) & 3) for s in range(4)]
    total = pieces[0]
    for s in (1, 2, 3):
        total = total + shifted(pieces[s].astype(BF), "y", s).astype(F32)
    spot = y * 2 + c
    begin = starts(every)
    m = ((zh - (spot & 3)) & 3) * 2 + (spot >> 2)
    place = ((m - begin[:, None]) & 7) + 8 * eight[None, :]
    comes = jnp.where(place < rank_tokens[:, None], (begin[:, None] + place) >> 3, -1)
    expand = (comes.reshape(ranks * 8, 1) == jnp.arange(chunk, dtype=jnp.int32)).astype(BF)
    at = [(y - (spot >> 2) * 2 - low) & 3 for low in range(2)]
    pair = [jnp.stack([pick(pick(a, s), spot & 3) for s in at]) for a in (full, full_other)]
    low = jnp.where(c == 0, pair[0], pair[1])
    high = jnp.where(c == 0, pair[1], pair[0])
    own = jnp.stack([low, high], axis=1).reshape(width, chunk)
    here = (jnp.arange(ranks * 8, dtype=jnp.int32) >> 6) == zh
    own = nt(jnp.where(here[:, None], expand, jnp.zeros_like(expand)), own)
    result = (dot(expand, total.astype(BF)) + own).astype(BF).reshape(ranks, 8, width)
    result = exchange(result, DP).reshape(ranks * 8, width)
    source = jnp.arange(ranks, dtype=jnp.int32)
    chunk_of = (((source >> 3) - (source & 3)) & 3) * 2 + ((source >> 2) & 1)
    fits = chunk_of[None, :, None] == ((own_start + slot) & 7)[:, None, None]
    fits = fits & (eight[None, None, :] == (slot >> 3)[:, None, None])
    fits = fits & (slot < own_length)[:, None, None]
    return dot(fits.astype(BF).reshape(slots, ranks * 8), result).astype(BF)


def solution(mesh):
    mesh = Mesh(mesh.devices.reshape(4, 4, 2, 4, 2), DP + HD)
    in_specs = (
        P(DP, HD),
        P(DP, HD),
        P(DP, None),
        P(DP, None),
        P(None, HD),
        P(None, HD),
        P(HD, DP),
        P(DP, HD),
        P(HD),
        P(HD, DP),
        P(HD, DP),
        P(DP, HD),
        P(),
        P(DP, None),
    )
    return jax.shard_map(
        on_device, mesh=mesh, in_specs=in_specs, out_specs=P(DP, HD), check_vma=False
    )
```

```python
import functools

import jax
import jax.numpy as jnp
from jax import lax
from jax.experimental import pallas as pl
from jax.experimental.pallas import tpu as pltpu
from jax.sharding import Mesh, PartitionSpec as P

BF = jnp.bfloat16
F32 = jnp.float32
NOPE = 128
ROPE = 64
VH = 128
WIN = 32
LIVE = 1024
BLK = 128
STEP = 256
DP = ("zh", "y", "c")
HD = ("x", "zl")


def dot(a, b):
    return jnp.dot(a, b, preferred_element_type=F32)


def shifted(x, axis, shift):
    n = lax.axis_size(axis)
    return lax.ppermute(x, axis, [(i, (i + shift) % n) for i in range(n)])


def iota(shape, dim):
    return lax.broadcasted_iota(jnp.int32, shape, dim)


def nt(a, b):
    return lax.dot_general(a, b, (((1,), (1,)), ((), ())), preferred_element_type=F32)


def whole(shape):
    return pl.BlockSpec(shape, lambda *_: (0,) * len(shape), pipeline_mode=pl.Buffered(1))


def cost(us):
    return pl.CostEstimate(flops=us * 10**9, bytes_accessed=us * 3 * 10**6, transcendentals=0)


def rank_here():
    return (lax.axis_index("zh") * 4 + lax.axis_index("y")) * 2 + lax.axis_index("c")


def live_before(counts_ref):
    place = rank_here()
    return lax.fori_loop(
        0,
        counts_ref.shape[0],
        lambda i, a: a + jnp.where(i < place, counts_ref[i], 0),
        jnp.int32(0),
    )


def score_kernel(counts_ref, qn_ref, qr_ref, lat_ref, kr_ref, ku_ref, req_ref, out_ref, s_ref):
    slots = lat_ref.shape[0]
    heads = ku_ref.shape[1] // NOPE
    before = live_before(counts_ref)
    keys = dot(lat_ref[...], ku_ref[...]).astype(BF)
    key_rope = kr_ref[...]
    s_at, t_at = iota((slots, slots), 0), iota((slots, slots), 1)
    across = jnp.broadcast_to(req_ref[...], (slots, slots))
    down = jnp.sum(jnp.where(s_at == t_at, across, 0), axis=1, keepdims=True)
    allowed = (across == down) & (t_at <= s_at)
    t_row, lane = iota((slots, BLK), 0), iota((slots, BLK), 1)
    lands = ((before + t_row) & (WIN - 1)) == (lane & (WIN - 1))
    per = BLK // WIN
    for h in range(heads):
        rows = slice(h * slots, (h + 1) * slots)
        s = nt(qn_ref[:, h * NOPE : (h + 1) * NOPE], keys[:, h * NOPE : (h + 1) * NOPE])
        s = s + nt(qr_ref[:, h * ROPE : (h + 1) * ROPE], key_rope)
        s_ref[rows, :] = jnp.where(allowed, s * (NOPE + ROPE) ** (-0.5), jnp.float32(-1e30))
    s = s_ref[...]
    raised = jnp.exp(s - jnp.max(s, axis=-1, keepdims=True))
    w = (raised / jnp.sum(raised, axis=-1, keepdims=True)).astype(BF)
    folded = dot(w, jnp.where(lands, 1.0, 0.0).astype(BF))
    for group in range(heads // per):
        out = folded[group * per * slots : (group * per + 1) * slots]
        for i in range(1, per):
            h = group * per + i
            out = jnp.where((lane >> 5) == i, folded[h * slots : (h + 1) * slots], out)
        for copy in range(out_ref.shape[0]):
            out_ref[copy, :, group * BLK : (group + 1) * BLK] = out.astype(BF)


def score_weights(counts, *arrays):
    slots, heads = arrays[2].shape[0], arrays[4].shape[1] // NOPE
    shape = (4, slots, heads * WIN)
    return pl.pallas_call(
        score_kernel,
        grid=(1,),
        out_shape=jax.ShapeDtypeStruct(shape, BF),
        in_specs=[pl.BlockSpec(memory_space=pltpu.SMEM)] + [whole(a.shape) for a in arrays],
        out_specs=whole(shape),
        scratch_shapes=[pltpu.VMEM((slots * heads, slots), F32)],
        cost_estimate=cost(4),
        name="score_weights",
    )(counts, *arrays)


def live_rows(goes_ref, own_ref, other_ref):
    row = iota((STEP, own_ref.shape[0]), 0) + pl.program_id(0) * STEP
    out = dot(jnp.where(goes_ref[0] == row, 1.0, 0.0).astype(BF), own_ref[...])
    out = out + dot(jnp.where(goes_ref[1] == row, 1.0, 0.0).astype(BF), other_ref[...])
    return out.astype(BF)


def values_kernel(goes_ref, slots_ref, up_ref, out_ref):
    row = iota((STEP, slots_ref.shape[0]), 0) + pl.program_id(0) * STEP
    live = dot(jnp.where(goes_ref[...] == row, 1.0, 0.0).astype(BF), slots_ref[...])
    out_ref[...] = dot(live.astype(BF), up_ref[...]).astype(BF)


def live_values(goes, slots, up):
    width = up.shape[1]
    return pl.pallas_call(
        values_kernel,
        grid=(LIVE // STEP,),
        out_shape=jax.ShapeDtypeStruct((LIVE, width), BF),
        in_specs=[whole(a.shape) for a in (goes, slots, up)],
        out_specs=pl.BlockSpec((STEP, width), lambda b: (b, 0)),
        cost_estimate=cost(0),
        compiler_params=pltpu.CompilerParams(vmem_limit_bytes=24 * 2**20),
        name="live_values",
    )(goes, slots, up)


def mix_kernel(goes_ref, own_ref, other_ref, prev_ref, cur_ref, wo_ref, out_ref, att_ref, all_ref):
    b = pl.program_id(0)
    heads = cur_ref.shape[1] // VH
    r_at, l_at = iota((BLK, BLK), 0), iota((BLK, BLK), 1)
    gap = r_at - l_at
    near = (gap >= 0) & (gap < WIN)
    per = BLK // WIN
    masks = [jnp.where(near & ((l_at >> 5) == q), 1.0, 0.0).astype(BF) for q in range(per)]
    r_at, l_at = iota((WIN, BLK), 0), iota((WIN, BLK), 1)
    before = jnp.where((BLK + r_at - l_at) < WIN, 1.0, 0.0).astype(BF)
    blank = jnp.zeros((BLK - WIN, BLK), BF)
    packed = live_rows(goes_ref, own_ref, other_ref)
    for group in range(heads // per):
        one = packed[:, group * BLK : (group + 1) * BLK].astype(F32)
        turned = [one.astype(BF)]
        for q in range(1, per):
            turned.append(pltpu.roll(one, q * WIN, 1).astype(BF))
        for i in range(per):
            cols = slice((group * per + i) * VH, (group * per + i + 1) * VH)
            last = turned[(per - 1 - i) % per]
            olds = [prev_ref[:, cols], cur_ref[:BLK, cols]]
            for t in range(STEP // BLK):
                rows = slice(t * BLK, (t + 1) * BLK)
                band = turned[(-i) % per][rows] * masks[0]
                for q in range(1, per):
                    band = band + turned[(q - i) % per][rows] * masks[q]
                corner = jnp.concatenate([last[rows][:WIN] * before, blank], axis=0)
                att = dot(
                    jnp.concatenate([corner, band], axis=1),
                    jnp.concatenate([olds[t], cur_ref[rows, cols]], axis=0),
                )
                att_ref[rows, cols] = att.astype(BF)
    part = nt(att_ref[...], wo_ref[...]).astype(BF)
    share = STEP // 8
    r_at, l_at = iota((STEP, STEP), 0), iota((STEP, STEP), 1)
    order = ((r_at & (share - 1)) * 8 + (r_at >> 5)) == l_at
    part = dot(jnp.where(order, 1.0, 0.0).astype(BF), part)
    rows = pl.ds(pl.multiple_of(b * share, share), share)
    for m in range(8):
        all_ref[m, rows, :] = part[m * share : (m + 1) * share]

    @pl.when(b == pl.num_programs(0) - 1)
    def _():
        for m in range(8):
            out_ref[m] = all_ref[m].T.astype(BF)


def mix_project(goes, own, other, values, wo):
    width = values.shape[1]
    n = wo.shape[0]
    shape = (8, n, LIVE // 8)
    return pl.pallas_call(
        mix_kernel,
        grid=(LIVE // STEP,),
        out_shape=jax.ShapeDtypeStruct(shape, BF),
        in_specs=[
            whole(goes.shape),
            whole(own.shape),
            whole(other.shape),
            pl.BlockSpec((BLK, width), lambda b: (jnp.maximum(b * (STEP // BLK) - 1, 0), 0)),
            pl.BlockSpec((STEP, width), lambda b: (b, 0)),
            whole(wo.shape),
        ],
        out_specs=whole(shape),
        scratch_shapes=[pltpu.VMEM((STEP, width), BF), pltpu.VMEM((8, LIVE // 8, n), F32)],
        cost_estimate=cost(9),
        compiler_params=pltpu.CompilerParams(vmem_limit_bytes=50 * 2**20),
        name="mix_project",
    )(goes, own, other, values, values, wo)


def gate_up_kernel(steps, own_ref, other_ref, gain_ref, gate_ref, up_ref, *refs):
    outs, x_ref = refs[:-1], refs[-1]
    core, y = lax.axis_index("c"), lax.axis_index("y")
    x_at, zl = lax.axis_index("x"), lax.axis_index("zl")
    k, chunk = own_ref.shape[2:]
    ff = gate_ref.shape[0]
    gain = jnp.broadcast_to(gain_ref[...], (8, gain_ref.shape[1])).T
    x_ref[:, :8] = gain.astype(F32)
    squares = []
    scaled = []
    for dx, dz in steps:
        spot = ((x_at + dx) & 3) * 2 + (zl ^ dz)
        total = jnp.zeros((1, chunk), F32)
        for low in range(2):
            s = (y - (spot >> 2) * 2 - low) & 3
            one, two = own_ref[s, spot & 3], other_ref[s, spot & 3]
            for half in range(2):
                x = jnp.where(core == half, one, two).astype(F32)
                total = total + jnp.sum(x * x, axis=0, keepdims=True)
                rows = slice((low * 2 + half) * k, (low * 2 + half + 1) * k)
                scaled.append((x * x_ref[rows, :1]).astype(BF))
        squares.append(total)
    columns = [
        jnp.concatenate(scaled[4 * i : 4 * i + 4], axis=0) for i in range(len(steps))
    ]
    x = jnp.concatenate(columns, axis=1)
    gate = dot(gate_ref[...], x).astype(BF)
    up = dot(up_ref[...], x).astype(BF)
    row = iota((16, chunk), 0)
    for i, out_ref in enumerate(outs):
        cols = slice(i * chunk, (i + 1) * chunk)
        high = squares[i].astype(BF).astype(F32)
        extra = jnp.where(row == 0, high, jnp.where(row == 1, squares[i] - high, 0.0))
        out_ref[:ff, :] = gate[:, cols]
        out_ref[ff : 2 * ff, :] = up[:, cols]
        out_ref[2 * ff :, :] = extra.astype(BF)


def gate_up(steps, own, other, gain, gate_weight, up_weight):
    k, chunk = own.shape[2:]
    ff, width = gate_weight.shape
    shape = (2 * ff + 16, chunk)
    arrays = (own, other, gain, gate_weight, up_weight)
    return pl.pallas_call(
        functools.partial(gate_up_kernel, steps),
        grid=(1,),
        out_shape=[jax.ShapeDtypeStruct(shape, BF)] * len(steps),
        in_specs=[whole(a.shape) for a in arrays],
        out_specs=[whole(shape)] * len(steps),
        scratch_shapes=[pltpu.VMEM((width, BLK), F32)],
        cost_estimate=cost(4),
        compiler_params=pltpu.CompilerParams(vmem_limit_bytes=24 * 2**20),
        name="gate_up",
    )(*arrays)


def exchange(x, axes):
    return lax.all_to_all(x, axes, split_axis=0, concat_axis=0, tiled=True)


def gather(x, axes):
    n = lax.axis_size(axes)
    return exchange(jnp.broadcast_to(x[None], (n,) + x.shape), axes)


def pick(x, index):
    return lax.dynamic_index_in_dim(x, index, 0, keepdims=False)


def on_device(
    query_nope,
    query_rope,
    latent,
    key_rope,
    key_up,
    value_up,
    output_weight,
    residual,
    norm_gain,
    gate_weight,
    up_weight,
    down_weight,
    rank_tokens,
    request_ids,
):
    slots = latent.shape[0]
    ranks = rank_tokens.shape[0]
    zh, y, c = (lax.axis_index(a) for a in DP)
    rank = (zh * 4 + y) * 2 + c
    chunk = LIVE // 8
    width = residual.shape[1]
    quarter = width // 4
    model = 8 * width

    every = jnp.arange(ranks, dtype=jnp.int32)

    def starts(which):
        return jnp.sum(jnp.where(every < which[..., None], rank_tokens, 0), axis=-1)

    def lengths(which):
        return jnp.sum(jnp.where(every == which[..., None], rank_tokens, 0), axis=-1)

    own_start, own_length = starts(rank), lengths(rank)
    slot = jnp.arange(slots, dtype=jnp.int32)

    latents = lax.all_gather(latent, DP, axis=0, tiled=True)
    begin = starts(every)
    slots_go = jnp.where(slot < rank_tokens[:, None], begin[:, None] + slot, -1)
    values = live_values(slots_go.reshape(1, -1), latents, value_up)

    eight = jnp.arange(8, dtype=jnp.int32)
    spread = ((eight[:, None] - own_start) & 7) + 8 * eight
    roll = (spread.reshape(slots, 1) == slot).astype(BF)
    rows = dot(roll, residual).astype(BF).reshape(8, 8, 4, quarter)
    rows = exchange(rows.transpose(0, 2, 1, 3).reshape(ranks, 8, quarter), DP)

    weights = score_weights(
        rank_tokens, query_nope, query_rope, latent, key_rope, key_up, request_ids
    )
    weights = exchange(weights, "zh")

    swap = []
    for a in range(4):
        for b in range(8):
            for e in range(4):
                for f in range(2):
                    to = (e * 8 + (f * 4 + (b & 3))) * 8 + a * 2 + (b >> 2)
                    swap.append(((a * 8 + b) * 8 + e * 2 + f, to))
    place = (((zh * 2 + (y >> 1)) - begin[:, None]) & 7) + 8 * eight
    come = jnp.where(place < rank_tokens[:, None], (begin[:, None] + place) >> 3, -1)
    come = (come.reshape(-1, 1) == jnp.arange(chunk, dtype=jnp.int32)).astype(BF)
    rows = lax.dot_general(
        rows.reshape(ranks * 8, quarter), come, (((0,), (0,)), ((), ())), preferred_element_type=F32
    )
    rows = lax.ppermute(rows.astype(BF), DP + HD, swap)
    weights, gain, _ = lax.optimization_barrier((weights, norm_gain[None, :], rows))
    weights = gather(weights, "y").reshape(-1, weights.shape[2])
    weights_other = shifted(weights, "c", 1)

    goes = slots_go.reshape(4, 4, 2, slots).transpose(2, 1, 0, 3)
    goes = jnp.where(c == 0, goes, goes[::-1]).reshape(2, 1, -1)

    part = mix_project(goes, weights, weights_other, values, output_weight.T)
    projected = jnp.sum(exchange(part, HD).astype(F32), axis=0)
    mixed = (rows.astype(F32) + projected).astype(BF)

    full = []
    for k in range(4):
        sends = []
        for a in range(4):
            for b in range(8):
                for e in range(4):
                    for f in range(2):
                        to = (((e + k) & 3) * 8 + (f * 4 + (b & 3))) * 8 + a * 2 + (b >> 2)
                        sends.append(((a * 8 + b) * 8 + e * 2 + f, to))
        full.append(lax.ppermute(mixed, DP + HD, sends))
    full = jnp.stack(full)

    full = jnp.stack([full] + [shifted(full, "y", s) for s in (1, 2, 3)])
    full_other = shifted(full, "c", 1)
    ff = down_weight.shape[0]
    arrays = (full, full_other, gain, gate_weight.T, up_weight.T)
    near = [(0, 0), (1, 0), (3, 0), (2, 0)]
    far = [(0, 1), (1, 1), (3, 1), (2, 1)]
    parts = list(zip(near, gate_up(near, *arrays))) + list(zip(far, gate_up(far, *arrays)))
    total = parts[0][1].astype(F32)
    for (dx, dz), part in parts[1:]:
        sends = [(i, ((i // 2 + dx) % 4) * 2 + ((i % 2) ^ dz)) for i in range(8)]
        total = total + lax.ppermute(part, HD, sends).astype(F32)
    scale = lax.rsqrt((total[2 * ff : 2 * ff + 1] + total[2 * ff + 1 : 2 * ff + 2]) / model + 1e-06)
    hidden = (jax.nn.silu(total[:ff] * scale) * (total[ff : 2 * ff] * scale)).astype(BF)
    hidden = gather(hidden, HD).reshape(4, 2, ff, chunk)

    def down(core):
        piece = lax.dynamic_index_in_dim(hidden, core, 1, keepdims=False)
        return lax.dot_general(
            piece, down_weight, (((1,), (0,)), ((), ())), preferred_element_type=F32
        )

    sent = shifted(down(1 - c).astype(BF), "c", 1)
    total = down(c) + sent.astype(F32)
    pieces = [pick(total, (y + s) & 3) for s in range(4)]
    total = pieces[0]
    for s in (1, 2, 3):
        total = total + shifted(pieces[s].astype(BF), "y", s).astype(F32)
    spot = y * 2 + c
    m = ((zh - (spot & 3)) & 3) * 2 + (spot >> 2)
    place = ((m - begin[:, None]) & 7) + 8 * eight[None, :]
    comes = jnp.where(place < rank_tokens[:, None], (begin[:, None] + place) >> 3, -1)
    expand = (comes.reshape(ranks * 8, 1) == jnp.arange(chunk, dtype=jnp.int32)).astype(BF)
    at = [(y - (spot >> 2) * 2 - low) & 3 for low in range(2)]
    pair = [jnp.stack([pick(pick(a, s), spot & 3) for s in at]) for a in (full, full_other)]
    low = jnp.where(c == 0, pair[0], pair[1])
    high = jnp.where(c == 0, pair[1], pair[0])
    own = jnp.stack([low, high], axis=1).reshape(width, chunk)
    here = (jnp.arange(ranks * 8, dtype=jnp.int32) >> 6) == zh
    own = nt(jnp.where(here[:, None], expand, jnp.zeros_like(expand)), own)
    result = (dot(expand, total.astype(BF)) + own).astype(BF).reshape(ranks, 8, width)
    result = exchange(result, DP).reshape(ranks * 8, width)
    source = jnp.arange(ranks, dtype=jnp.int32)
    chunk_of = (((source >> 3) - (source & 3)) & 3) * 2 + ((source >> 2) & 1)
    fits = chunk_of[None, :, None] == ((own_start + slot) & 7)[:, None, None]
    fits = fits & (eight[None, None, :] == (slot >> 3)[:, None, None])
    fits = fits & (slot < own_length)[:, None, None]
    return dot(fits.astype(BF).reshape(slots, ranks * 8), result).astype(BF)


def solution(mesh):
    mesh = Mesh(mesh.devices.reshape(4, 4, 2, 4, 2), DP + HD)
    in_specs = (
        P(DP, HD),
        P(DP, HD),
        P(DP, None),
        P(DP, None),
        P(None, HD),
        P(None, HD),
        P(HD, DP),
        P(DP, HD),
        P(HD),
        P(HD, DP),
        P(HD, DP),
        P(DP, HD),
        P(),
        P(DP, None),
    )
    return jax.shard_map(
        on_device, mesh=mesh, in_specs=in_specs, out_specs=P(DP, HD), check_vma=False
    )
```

```python
import functools

import jax
import jax.numpy as jnp
from jax import lax
from jax.experimental import pallas as pl
from jax.experimental.pallas import tpu as pltpu
from jax.sharding import Mesh, PartitionSpec as P

BF = jnp.bfloat16
F32 = jnp.float32
NOPE = 128
ROPE = 64
VH = 128
WIN = 32
LIVE = 1024
BLK = 128
STEP = 256
DP = ("zh", "y", "c")
HD = ("x", "zl")


def dot(a, b):
    return jnp.dot(a, b, preferred_element_type=F32)


def shifted(x, axis, shift):
    n = lax.axis_size(axis)
    return lax.ppermute(x, axis, [(i, (i + shift) % n) for i in range(n)])


def iota(shape, dim):
    return lax.broadcasted_iota(jnp.int32, shape, dim)


def nt(a, b):
    return lax.dot_general(a, b, (((1,), (1,)), ((), ())), preferred_element_type=F32)


def whole(shape):
    return pl.BlockSpec(shape, lambda *_: (0,) * len(shape), pipeline_mode=pl.Buffered(1))


def cost(us):
    return pl.CostEstimate(flops=us * 10**9, bytes_accessed=us * 3 * 10**6, transcendentals=0)


def rank_here():
    return (lax.axis_index("zh") * 4 + lax.axis_index("y")) * 2 + lax.axis_index("c")


def live_before(counts_ref):
    place = rank_here()
    return lax.fori_loop(
        0,
        counts_ref.shape[0],
        lambda i, a: a + jnp.where(i < place, counts_ref[i], 0),
        jnp.int32(0),
    )


def pack_kernel(counts_ref, lat_ref, res_ref, *refs):
    outs, rows_ref = refs[:4], refs[4]
    slots, width = res_ref.shape
    half, lanes = width // 2, lat_ref.shape[1]
    zh = lax.axis_index("zh")
    start = live_before(counts_ref)
    i_at, slot = iota((slots, slots), 0), iota((slots, slots), 1)
    roll = ((((i_at >> 3) - start) & 7) + 8 * (i_at & 7)) == slot
    rows_ref[...] = dot(jnp.where(roll, 1.0, 0.0).astype(BF), res_ref[...])
    fill = jnp.zeros((16, lanes - half), F32)
    for s in range(4):
        outs[s][:slots, :] = lat_ref[...]
        for high in range(2):
            m = ((zh + s) & 3) * 2 + high
            piece = rows_ref[pl.ds(pl.multiple_of(m * 8, 8), 8), :]
            piece = jnp.concatenate([piece[:, :half], piece[:, half:]], axis=0)
            piece = jnp.concatenate([piece, fill], axis=1)
            outs[s][slots + 16 * high : slots + 16 * (high + 1), :] = piece.astype(BF)


def pack(counts, latent, residual):
    slots, lanes = latent.shape
    shape = (slots + 32, lanes)
    return pl.pallas_call(
        pack_kernel,
        grid=(1,),
        out_shape=[jax.ShapeDtypeStruct(shape, BF)] * 4,
        in_specs=[
            pl.BlockSpec(memory_space=pltpu.SMEM),
            whole(latent.shape),
            whole(residual.shape),
        ],
        out_specs=[whole(shape)] * 4,
        scratch_shapes=[pltpu.VMEM(residual.shape, F32)],
        cost_estimate=cost(2),
        name="pack",
    )(counts, latent, residual)


def repack_kernel(*refs):
    ins, outs, rows_ref = refs[:4], refs[4:8], refs[8]
    slots = ins[0].shape[0] - 32
    y = lax.axis_index("y")
    for t in range(4):
        rows_ref[t] = ins[t][slots:, :].astype(F32)
    for s in range(4):
        at = pl.ds(pl.multiple_of(((y + s) & 3) * 8, 8), 8)
        for t in range(4):
            outs[s][t * slots : (t + 1) * slots, :] = ins[t][:slots, :]
        for t in (0, 2):
            pair = jnp.concatenate([rows_ref[t, at, :], rows_ref[t + 1, at, :]], axis=0)
            outs[s][4 * slots + 8 * t : 4 * slots + 8 * t + 16, :] = pair.astype(BF)


def repack(*pieces):
    rows, lanes = pieces[0].shape
    shape = (4 * (rows - 32) + 32, lanes)
    return pl.pallas_call(
        repack_kernel,
        grid=(1,),
        out_shape=[jax.ShapeDtypeStruct(shape, BF)] * 4,
        in_specs=[whole(pieces[0].shape)] * 4,
        out_specs=[whole(shape)] * 4,
        scratch_shapes=[pltpu.VMEM((4, 32, lanes), F32)],
        cost_estimate=cost(2),
        name="repack",
    )(*pieces)


def score_kernel(counts_ref, qn_ref, qr_ref, lat_ref, kr_ref, ku_ref, req_ref, out_ref, s_ref):
    slots = lat_ref.shape[0]
    heads = ku_ref.shape[1] // NOPE
    before = live_before(counts_ref)
    keys = dot(lat_ref[...], ku_ref[...]).astype(BF)
    key_rope = kr_ref[...]
    s_at, t_at = iota((slots, slots), 0), iota((slots, slots), 1)
    across = jnp.broadcast_to(req_ref[...], (slots, slots))
    down = jnp.sum(jnp.where(s_at == t_at, across, 0), axis=1, keepdims=True)
    allowed = (across == down) & (t_at <= s_at)
    t_row, lane = iota((slots, BLK), 0), iota((slots, BLK), 1)
    lands = ((before + t_row) & (WIN - 1)) == (lane & (WIN - 1))
    per = BLK // WIN
    for h in range(heads):
        rows = slice(h * slots, (h + 1) * slots)
        s = nt(qn_ref[:, h * NOPE : (h + 1) * NOPE], keys[:, h * NOPE : (h + 1) * NOPE])
        s = s + nt(qr_ref[:, h * ROPE : (h + 1) * ROPE], key_rope)
        s_ref[rows, :] = jnp.where(allowed, s * (NOPE + ROPE) ** (-0.5), jnp.float32(-1e30))
    s = s_ref[...]
    raised = jnp.exp(s - jnp.max(s, axis=-1, keepdims=True))
    w = (raised / jnp.sum(raised, axis=-1, keepdims=True)).astype(BF)
    folded = dot(w, jnp.where(lands, 1.0, 0.0).astype(BF))
    for group in range(heads // per):
        out = folded[group * per * slots : (group * per + 1) * slots]
        for i in range(1, per):
            h = group * per + i
            out = jnp.where((lane >> 5) == i, folded[h * slots : (h + 1) * slots], out)
        for copy in range(out_ref.shape[0]):
            out_ref[copy, :, group * BLK : (group + 1) * BLK] = out.astype(BF)


def score_weights(counts, *arrays):
    slots, heads = arrays[2].shape[0], arrays[4].shape[1] // NOPE
    shape = (4, slots, heads * WIN)
    return pl.pallas_call(
        score_kernel,
        grid=(1,),
        out_shape=jax.ShapeDtypeStruct(shape, BF),
        in_specs=[pl.BlockSpec(memory_space=pltpu.SMEM)] + [whole(a.shape) for a in arrays],
        out_specs=whole(shape),
        scratch_shapes=[pltpu.VMEM((slots * heads, slots), F32)],
        cost_estimate=cost(4),
        name="score_weights",
    )(counts, *arrays)


def live_rows(goes_ref, own_ref, other_ref):
    row = iota((STEP, own_ref.shape[0]), 0) + pl.program_id(0) * STEP
    out = dot(jnp.where(goes_ref[0] == row, 1.0, 0.0).astype(BF), own_ref[...])
    out = out + dot(jnp.where(goes_ref[1] == row, 1.0, 0.0).astype(BF), other_ref[...])
    return out.astype(BF)


def values_kernel(goes_ref, own_ref, other_ref, up_ref, out_ref):
    out_ref[...] = dot(live_rows(goes_ref, own_ref, other_ref), up_ref[...]).astype(BF)


def live_values(goes, own, other, up):
    width = up.shape[1]
    return pl.pallas_call(
        values_kernel,
        grid=(LIVE // STEP,),
        out_shape=jax.ShapeDtypeStruct((LIVE, width), BF),
        in_specs=[whole(a.shape) for a in (goes, own, other, up)],
        out_specs=pl.BlockSpec((STEP, width), lambda b: (b, 0)),
        cost_estimate=cost(0),
        compiler_params=pltpu.CompilerParams(vmem_limit_bytes=24 * 2**20),
        name="live_values",
    )(goes, own, other, up)


def mix_kernel(goes_ref, own_ref, other_ref, prev_ref, cur_ref, wo_ref, out_ref, att_ref, all_ref):
    b = pl.program_id(0)
    heads = cur_ref.shape[1] // VH
    r_at, l_at = iota((BLK, BLK), 0), iota((BLK, BLK), 1)
    gap = r_at - l_at
    near = (gap >= 0) & (gap < WIN)
    per = BLK // WIN
    masks = [jnp.where(near & ((l_at >> 5) == q), 1.0, 0.0).astype(BF) for q in range(per)]
    r_at, l_at = iota((WIN, BLK), 0), iota((WIN, BLK), 1)
    before = jnp.where((BLK + r_at - l_at) < WIN, 1.0, 0.0).astype(BF)
    blank = jnp.zeros((BLK - WIN, BLK), BF)
    packed = live_rows(goes_ref, own_ref, other_ref)
    for group in range(heads // per):
        one = packed[:, group * BLK : (group + 1) * BLK].astype(F32)
        turned = [one.astype(BF)]
        for q in range(1, per):
            turned.append(pltpu.roll(one, q * WIN, 1).astype(BF))
        for i in range(per):
            cols = slice((group * per + i) * VH, (group * per + i + 1) * VH)
            last = turned[(per - 1 - i) % per]
            olds = [prev_ref[:, cols], cur_ref[:BLK, cols]]
            for t in range(STEP // BLK):
                rows = slice(t * BLK, (t + 1) * BLK)
                band = turned[(-i) % per][rows] * masks[0]
                for q in range(1, per):
                    band = band + turned[(q - i) % per][rows] * masks[q]
                corner = jnp.concatenate([last[rows][:WIN] * before, blank], axis=0)
                att = dot(
                    jnp.concatenate([corner, band], axis=1),
                    jnp.concatenate([olds[t], cur_ref[rows, cols]], axis=0),
                )
                att_ref[rows, cols] = att.astype(BF)
    part = nt(att_ref[...], wo_ref[...]).astype(BF)
    share = STEP // 8
    r_at, l_at = iota((STEP, STEP), 0), iota((STEP, STEP), 1)
    order = ((r_at & (share - 1)) * 8 + (r_at >> 5)) == l_at
    part = dot(jnp.where(order, 1.0, 0.0).astype(BF), part)
    rows = pl.ds(pl.multiple_of(b * share, share), share)
    for m in range(8):
        all_ref[m, rows, :] = part[m * share : (m + 1) * share]

    @pl.when(b == pl.num_programs(0) - 1)
    def _():
        for m in range(8):
            out_ref[m] = all_ref[m].T.astype(BF)


def mix_project(goes, own, other, values, wo):
    width = values.shape[1]
    n = wo.shape[0]
    shape = (8, n, LIVE // 8)
    return pl.pallas_call(
        mix_kernel,
        grid=(LIVE // STEP,),
        out_shape=jax.ShapeDtypeStruct(shape, BF),
        in_specs=[
            whole(goes.shape),
            whole(own.shape),
            whole(other.shape),
            pl.BlockSpec((BLK, width), lambda b: (jnp.maximum(b * (STEP // BLK) - 1, 0), 0)),
            pl.BlockSpec((STEP, width), lambda b: (b, 0)),
            whole(wo.shape),
        ],
        out_specs=whole(shape),
        scratch_shapes=[pltpu.VMEM((STEP, width), BF), pltpu.VMEM((8, LIVE // 8, n), F32)],
        cost_estimate=cost(9),
        compiler_params=pltpu.CompilerParams(vmem_limit_bytes=50 * 2**20),
        name="mix_project",
    )(goes, own, other, values, values, wo)


def gate_up_kernel(steps, own_ref, other_ref, gain_ref, gate_ref, up_ref, *refs):
    outs, x_ref = refs[:-1], refs[-1]
    core, y = lax.axis_index("c"), lax.axis_index("y")
    x_at, zl = lax.axis_index("x"), lax.axis_index("zl")
    k, chunk = own_ref.shape[2:]
    ff = gate_ref.shape[0]
    gain = jnp.broadcast_to(gain_ref[...], (8, gain_ref.shape[1])).T
    x_ref[:, :8] = gain.astype(F32)
    squares = []
    scaled = []
    for dx, dz in steps:
        spot = ((x_at + dx) & 3) * 2 + (zl ^ dz)
        total = jnp.zeros((1, chunk), F32)
        for low in range(2):
            s = (y - (spot >> 2) * 2 - low) & 3
            one, two = own_ref[s, spot & 3], other_ref[s, spot & 3]
            for half in range(2):
                x = jnp.where(core == half, one, two).astype(F32)
                total = total + jnp.sum(x * x, axis=0, keepdims=True)
                rows = slice((low * 2 + half) * k, (low * 2 + half + 1) * k)
                scaled.append((x * x_ref[rows, :1]).astype(BF))
        squares.append(total)
    columns = [
        jnp.concatenate(scaled[4 * i : 4 * i + 4], axis=0) for i in range(len(steps))
    ]
    x = jnp.concatenate(columns, axis=1)
    gate = dot(gate_ref[...], x).astype(BF)
    up = dot(up_ref[...], x).astype(BF)
    row = iota((16, chunk), 0)
    for i, out_ref in enumerate(outs):
        cols = slice(i * chunk, (i + 1) * chunk)
        high = squares[i].astype(BF).astype(F32)
        extra = jnp.where(row == 0, high, jnp.where(row == 1, squares[i] - high, 0.0))
        out_ref[:ff, :] = gate[:, cols]
        out_ref[ff : 2 * ff, :] = up[:, cols]
        out_ref[2 * ff :, :] = extra.astype(BF)


def gate_up(steps, own, other, gain, gate_weight, up_weight):
    k, chunk = own.shape[2:]
    ff, width = gate_weight.shape
    shape = (2 * ff + 16, chunk)
    arrays = (own, other, gain, gate_weight, up_weight)
    return pl.pallas_call(
        functools.partial(gate_up_kernel, steps),
        grid=(1,),
        out_shape=[jax.ShapeDtypeStruct(shape, BF)] * len(steps),
        in_specs=[whole(a.shape) for a in arrays],
        out_specs=[whole(shape)] * len(steps),
        scratch_shapes=[pltpu.VMEM((width, BLK), F32)],
        cost_estimate=cost(4),
        compiler_params=pltpu.CompilerParams(vmem_limit_bytes=24 * 2**20),
        name="gate_up",
    )(*arrays)


def down_kernel(flip, *refs):
    pieces, (w_ref, out_ref) = refs[:8], refs[8:]
    swapped = lax.axis_index("zl") ^ lax.axis_index("c") ^ flip
    x = jnp.concatenate(
        [
            jnp.where(swapped == 0, pieces[2 * dx][...], pieces[2 * dx + 1][...])
            for dx in range(4)
        ],
        axis=1,
    )
    out = lax.dot_general(
        x, w_ref[...], (((0,), (0,)), ((), ())), preferred_element_type=F32
    )
    out_ref[...] = out.reshape(out_ref.shape).astype(out_ref.dtype)


def down(flip, pieces, weight, kind):
    shape = (4, pieces[0].shape[1], weight.shape[1])
    return pl.pallas_call(
        functools.partial(down_kernel, flip),
        grid=(1,),
        out_shape=jax.ShapeDtypeStruct(shape, kind),
        in_specs=[whole(p.shape) for p in pieces] + [whole(weight.shape)],
        out_specs=whole(shape),
        compiler_params=pltpu.CompilerParams(vmem_limit_bytes=24 * 2**20),
        cost_estimate=cost(2),
        name="down",
    )(*pieces, weight)


def sent_along_hd(x, dx, dz):
    return lax.ppermute(x, HD, [(i, ((i // 2 + dx) % 4) * 2 + ((i % 2) ^ dz)) for i in range(8)])


def exchange(x, axes):
    return lax.all_to_all(x, axes, split_axis=0, concat_axis=0, tiled=True)


def gather(x, axes):
    n = lax.axis_size(axes)
    return exchange(jnp.broadcast_to(x[None], (n,) + x.shape), axes)


def pick(x, index):
    return lax.dynamic_index_in_dim(x, index, 0, keepdims=False)


def on_device(
    query_nope,
    query_rope,
    latent,
    key_rope,
    key_up,
    value_up,
    output_weight,
    residual,
    norm_gain,
    gate_weight,
    up_weight,
    down_weight,
    rank_tokens,
    request_ids,
):
    slots = latent.shape[0]
    ranks = rank_tokens.shape[0]
    zh, y, c = (lax.axis_index(a) for a in DP)
    rank = (zh * 4 + y) * 2 + c
    chunk = LIVE // 8
    width = residual.shape[1]
    quarter = width // 4
    model = 8 * width

    every = jnp.arange(ranks, dtype=jnp.int32)

    def starts(which):
        return jnp.sum(jnp.where(every < which[..., None], rank_tokens, 0), axis=-1)

    def lengths(which):
        return jnp.sum(jnp.where(every == which[..., None], rank_tokens, 0), axis=-1)

    own_start, own_length = starts(rank), lengths(rank)
    slot = jnp.arange(slots, dtype=jnp.int32)

    pieces = pack(rank_tokens, latent, residual)
    pieces = [pieces[0]] + [shifted(pieces[s], "zh", s) for s in (1, 2, 3)]

    weights = score_weights(
        rank_tokens, query_nope, query_rope, latent, key_rope, key_up, request_ids
    )
    weights = exchange(weights, "zh")
    pieces = repack(*pieces)
    weights, gain, _ = lax.optimization_barrier((weights, norm_gain[None, :], pieces))
    weights = jnp.broadcast_to(weights[None], (4,) + weights.shape)
    pieces = [pieces[0]] + [shifted(pieces[s], "y", s) for s in (1, 2, 3)]
    pieces, weights = lax.optimization_barrier((pieces, weights))
    got = jnp.concatenate(pieces, axis=0)
    got_other = shifted(got, "c", 1)
    weights = exchange(weights, "y").reshape(-1, weights.shape[3])

    four = jnp.arange(4, dtype=jnp.int32)
    eight = jnp.arange(8, dtype=jnp.int32)
    core = jnp.stack([c, 1 - c])[:, None, None]
    ahead = (four[None, None, :] * 4 + four[None, :, None]) * 2 + core
    goes = jnp.where(slot < lengths(ahead)[..., None], starts(ahead)[..., None] + slot, -1)
    goes = goes.reshape(2, 1, -1)
    back = (((zh - four) & 3)[None, None, :] * 4 + ((y - four) & 3)[None, :, None]) * 2 + core
    back_start, back_count = starts(back)[..., None], lengths(back)[..., None]
    goes_back = jnp.where(slot < back_count, back_start + slot, -1).reshape(2, 4, -1)
    goes_back = jnp.pad(goes_back, ((0, 0), (0, 0), (0, 32)), constant_values=-1).reshape(2, 1, -1)
    values = live_values(goes_back, got, got_other, value_up)

    swap = []
    for a in range(4):
        for b in range(8):
            for e in range(4):
                for f in range(2):
                    to = (e * 8 + (f * 4 + (b & 3))) * 8 + a * 2 + (b >> 2)
                    swap.append(((a * 8 + b) * 8 + e * 2 + f, to))
    place = (((zh * 2 + (y >> 1)) - back_start) & 7) + 8 * eight
    come = jnp.where(place < back_count, (back_start + place) >> 3, -1)
    come = (come.reshape(2, -1, 1) == jnp.arange(chunk, dtype=jnp.int32)).astype(BF)

    def tn(a, b):
        return lax.dot_general(a, b, (((0,), (0,)), ((), ())), preferred_element_type=F32)

    rows = [a.reshape(4, -1, a.shape[1])[:, 4 * slots :].reshape(-1, a.shape[1]) for a in (got, got_other)]
    rows = tn(rows[0], come[0]) + tn(rows[1], come[1])
    rows = jnp.where(c == 0, rows[:quarter], rows[quarter : 2 * quarter]).astype(BF)
    rows, values = lax.optimization_barrier((rows, values))
    rows = lax.ppermute(rows, DP + HD, swap)

    weights, values = lax.optimization_barrier((weights, values))
    weights_other = shifted(weights, "c", 1)
    part = mix_project(goes, weights, weights_other, values, output_weight.T)
    projected = jnp.sum(exchange(part, HD).astype(F32), axis=0)
    mixed = (rows.astype(F32) + projected).astype(BF)

    full = []
    for k in range(4):
        sends = []
        for a in range(4):
            for b in range(8):
                for e in range(4):
                    for f in range(2):
                        to = (((e + k) & 3) * 8 + (f * 4 + (b & 3))) * 8 + a * 2 + (b >> 2)
                        sends.append(((a * 8 + b) * 8 + e * 2 + f, to))
        full.append(lax.ppermute(mixed, DP + HD, sends))
    full = jnp.stack(full)

    full = jnp.stack([full] + [shifted(full, "y", s) for s in (1, 2, 3)])
    full_other = shifted(full, "c", 1)
    ff = down_weight.shape[0]
    arrays = (full, full_other, gain, gate_weight.T, up_weight.T)
    late = [(0, 0), (2, 1), (3, 1), (2, 0)]
    soon = [(1, 1), (3, 0), (1, 0), (0, 1)]
    parts = list(zip(late, gate_up(late, *arrays))) + list(zip(soon, gate_up(soon, *arrays)))
    total = parts[0][1].astype(F32)
    for (dx, dz), part in parts[1:]:
        total = total + sent_along_hd(part, dx, dz).astype(F32)
    scale = lax.rsqrt((total[2 * ff : 2 * ff + 1] + total[2 * ff + 1 : 2 * ff + 2]) / model + 1e-06)
    hidden = (jax.nn.silu(total[:ff] * scale) * (total[ff : 2 * ff] * scale)).astype(BF)
    hidden = [
        hidden if r == 0 else sent_along_hd(hidden, r // 2, r % 2) for r in range(8)
    ]

    sent = shifted(down(1, hidden, down_weight, BF), "c", 1)
    total = down(0, hidden, down_weight, F32) + sent.astype(F32)
    turn = lax.axis_index("x") - y
    pieces = [pick(total, (turn - s) & 3) for s in range(4)]
    total = pieces[0]
    for s in (1, 2, 3):
        total = total + shifted(pieces[s].astype(BF), "y", s).astype(F32)
    spot = y * 2 + c
    begin = starts(every)
    m = ((zh - (spot & 3)) & 3) * 2 + (spot >> 2)
    place = ((m - begin[:, None]) & 7) + 8 * eight[None, :]
    comes = jnp.where(place < rank_tokens[:, None], (begin[:, None] + place) >> 3, -1)
    expand = (comes.reshape(ranks * 8, 1) == jnp.arange(chunk, dtype=jnp.int32)).astype(BF)
    at = [(y - (spot >> 2) * 2 - low) & 3 for low in range(2)]
    pair = [jnp.stack([pick(pick(a, s), spot & 3) for s in at]) for a in (full, full_other)]
    low = jnp.where(c == 0, pair[0], pair[1])
    high = jnp.where(c == 0, pair[1], pair[0])
    own = jnp.stack([low, high], axis=1).reshape(width, chunk)
    here = (jnp.arange(ranks * 8, dtype=jnp.int32) >> 6) == zh
    own = nt(jnp.where(here[:, None], expand, jnp.zeros_like(expand)), own)
    result = (dot(expand, total.astype(BF)) + own).astype(BF).reshape(ranks, 8, width)
    result = exchange(result, DP).reshape(ranks * 8, width)
    source = jnp.arange(ranks, dtype=jnp.int32)
    chunk_of = (((source >> 3) - (source & 3)) & 3) * 2 + ((source >> 2) & 1)
    fits = chunk_of[None, :, None] == ((own_start + slot) & 7)[:, None, None]
    fits = fits & (eight[None, None, :] == (slot >> 3)[:, None, None])
    fits = fits & (slot < own_length)[:, None, None]
    return dot(fits.astype(BF).reshape(slots, ranks * 8), result).astype(BF)


def solution(mesh):
    mesh = Mesh(mesh.devices.reshape(4, 4, 2, 4, 2), DP + HD)
    in_specs = (
        P(DP, HD),
        P(DP, HD),
        P(DP, None),
        P(DP, None),
        P(None, HD),
        P(None, HD),
        P(HD, DP),
        P(DP, HD),
        P(HD),
        P(HD, DP),
        P(HD, DP),
        P(DP, HD),
        P(),
        P(DP, None),
    )
    return jax.shard_map(
        on_device, mesh=mesh, in_specs=in_specs, out_specs=P(DP, HD), check_vma=False
    )
```

```python
import functools

import jax
import jax.numpy as jnp
from jax import lax
from jax.experimental import pallas as pl
from jax.experimental.pallas import tpu as pltpu
from jax.sharding import Mesh, PartitionSpec as P

BF = jnp.bfloat16
F32 = jnp.float32
NOPE = 128
ROPE = 64
VH = 128
WIN = 32
LIVE = 1024
BLK = 128
STEP = 256
DP = ("zh", "y", "c")
HD = ("x", "zl")


def dot(a, b):
    return jnp.dot(a, b, preferred_element_type=F32)


def shifted(x, axis, shift):
    n = lax.axis_size(axis)
    return lax.ppermute(x, axis, [(i, (i + shift) % n) for i in range(n)])


def iota(shape, dim):
    return lax.broadcasted_iota(jnp.int32, shape, dim)


def nt(a, b):
    return lax.dot_general(a, b, (((1,), (1,)), ((), ())), preferred_element_type=F32)


def whole(shape):
    return pl.BlockSpec(shape, lambda *_: (0,) * len(shape), pipeline_mode=pl.Buffered(1))


def cost(us):
    return pl.CostEstimate(flops=us * 10**9, bytes_accessed=us * 3 * 10**6, transcendentals=0)


def rank_here():
    return (lax.axis_index("zh") * 4 + lax.axis_index("y")) * 2 + lax.axis_index("c")


def live_before(counts_ref):
    place = rank_here()
    return lax.fori_loop(
        0,
        counts_ref.shape[0],
        lambda i, a: a + jnp.where(i < place, counts_ref[i], 0),
        jnp.int32(0),
    )


def pack_kernel(counts_ref, lat_ref, res_ref, *refs):
    outs, rows_ref = refs[:4], refs[4]
    slots, width = res_ref.shape
    half, lanes = width // 2, lat_ref.shape[1]
    zh = lax.axis_index("zh")
    start = live_before(counts_ref)
    i_at, slot = iota((slots, slots), 0), iota((slots, slots), 1)
    roll = ((((i_at >> 3) - start) & 7) + 8 * (i_at & 7)) == slot
    rows_ref[...] = dot(jnp.where(roll, 1.0, 0.0).astype(BF), res_ref[...])
    fill = jnp.zeros((16, lanes - half), F32)
    for s in range(4):
        outs[s][:slots, :] = lat_ref[...]
        for high in range(2):
            m = ((zh + s) & 3) * 2 + high
            piece = rows_ref[pl.ds(pl.multiple_of(m * 8, 8), 8), :]
            piece = jnp.concatenate([piece[:, :half], piece[:, half:]], axis=0)
            piece = jnp.concatenate([piece, fill], axis=1)
            outs[s][slots + 16 * high : slots + 16 * (high + 1), :] = piece.astype(BF)


def pack(counts, latent, residual):
    slots, lanes = latent.shape
    shape = (slots + 32, lanes)
    return pl.pallas_call(
        pack_kernel,
        grid=(1,),
        out_shape=[jax.ShapeDtypeStruct(shape, BF)] * 4,
        in_specs=[
            pl.BlockSpec(memory_space=pltpu.SMEM),
            whole(latent.shape),
            whole(residual.shape),
        ],
        out_specs=[whole(shape)] * 4,
        scratch_shapes=[pltpu.VMEM(residual.shape, F32)],
        cost_estimate=cost(2),
        name="pack",
    )(counts, latent, residual)


def repack_kernel(*refs):
    ins, outs, rows_ref = refs[:4], refs[4:8], refs[8]
    slots = ins[0].shape[0] - 32
    y = lax.axis_index("y")
    for t in range(4):
        rows_ref[t] = ins[t][slots:, :].astype(F32)
    for s in range(4):
        at = pl.ds(pl.multiple_of(((y + s) & 3) * 8, 8), 8)
        for t in range(4):
            outs[s][t * slots : (t + 1) * slots, :] = ins[t][:slots, :]
        for t in (0, 2):
            pair = jnp.concatenate([rows_ref[t, at, :], rows_ref[t + 1, at, :]], axis=0)
            outs[s][4 * slots + 8 * t : 4 * slots + 8 * t + 16, :] = pair.astype(BF)


def repack(*pieces):
    rows, lanes = pieces[0].shape
    shape = (4 * (rows - 32) + 32, lanes)
    return pl.pallas_call(
        repack_kernel,
        grid=(1,),
        out_shape=[jax.ShapeDtypeStruct(shape, BF)] * 4,
        in_specs=[whole(pieces[0].shape)] * 4,
        out_specs=[whole(shape)] * 4,
        scratch_shapes=[pltpu.VMEM((4, 32, lanes), F32)],
        cost_estimate=cost(2),
        name="repack",
    )(*pieces)


def score_kernel(counts_ref, qn_ref, qr_ref, lat_ref, kr_ref, ku_ref, req_ref, out_ref, s_ref):
    slots = lat_ref.shape[0]
    heads = ku_ref.shape[1] // NOPE
    before = live_before(counts_ref)
    keys = dot(lat_ref[...], ku_ref[...]).astype(BF)
    key_rope = kr_ref[...]
    s_at, t_at = iota((slots, slots), 0), iota((slots, slots), 1)
    across = jnp.broadcast_to(req_ref[...], (slots, slots))
    down = jnp.sum(jnp.where(s_at == t_at, across, 0), axis=1, keepdims=True)
    allowed = (across == down) & (t_at <= s_at)
    t_row, lane = iota((slots, BLK), 0), iota((slots, BLK), 1)
    lands = ((before + t_row) & (WIN - 1)) == (lane & (WIN - 1))
    per = BLK // WIN
    for h in range(heads):
        rows = slice(h * slots, (h + 1) * slots)
        s = nt(qn_ref[:, h * NOPE : (h + 1) * NOPE], keys[:, h * NOPE : (h + 1) * NOPE])
        s = s + nt(qr_ref[:, h * ROPE : (h + 1) * ROPE], key_rope)
        s_ref[rows, :] = jnp.where(allowed, s * (NOPE + ROPE) ** (-0.5), jnp.float32(-1e30))
    s = s_ref[...]
    raised = jnp.exp(s - jnp.max(s, axis=-1, keepdims=True))
    w = (raised / jnp.sum(raised, axis=-1, keepdims=True)).astype(BF)
    folded = dot(w, jnp.where(lands, 1.0, 0.0).astype(BF))
    for group in range(heads // per):
        out = folded[group * per * slots : (group * per + 1) * slots]
        for i in range(1, per):
            h = group * per + i
            out = jnp.where((lane >> 5) == i, folded[h * slots : (h + 1) * slots], out)
        for copy in range(out_ref.shape[0]):
            out_ref[copy, :, group * BLK : (group + 1) * BLK] = out.astype(BF)


def score_weights(counts, *arrays):
    slots, heads = arrays[2].shape[0], arrays[4].shape[1] // NOPE
    shape = (4, slots, heads * WIN)
    return pl.pallas_call(
        score_kernel,
        grid=(1,),
        out_shape=jax.ShapeDtypeStruct(shape, BF),
        in_specs=[pl.BlockSpec(memory_space=pltpu.SMEM)] + [whole(a.shape) for a in arrays],
        out_specs=whole(shape),
        scratch_shapes=[pltpu.VMEM((slots * heads, slots), F32)],
        cost_estimate=cost(4),
        name="score_weights",
    )(counts, *arrays)


def live_rows(goes_ref, own_ref, other_ref):
    row = iota((STEP, own_ref.shape[0]), 0) + pl.program_id(0) * STEP
    out = dot(jnp.where(goes_ref[0] == row, 1.0, 0.0).astype(BF), own_ref[...])
    out = out + dot(jnp.where(goes_ref[1] == row, 1.0, 0.0).astype(BF), other_ref[...])
    return out.astype(BF)


def values_kernel(goes_ref, own_ref, other_ref, up_ref, out_ref):
    out_ref[...] = dot(live_rows(goes_ref, own_ref, other_ref), up_ref[...]).astype(BF)


def live_values(goes, own, other, up):
    width = up.shape[1]
    return pl.pallas_call(
        values_kernel,
        grid=(LIVE // STEP,),
        out_shape=jax.ShapeDtypeStruct((LIVE, width), BF),
        in_specs=[whole(a.shape) for a in (goes, own, other, up)],
        out_specs=pl.BlockSpec((STEP, width), lambda b: (b, 0)),
        cost_estimate=cost(0),
        compiler_params=pltpu.CompilerParams(vmem_limit_bytes=24 * 2**20),
        name="live_values",
    )(goes, own, other, up)


def mix_kernel(goes_ref, own_ref, other_ref, prev_ref, cur_ref, wo_ref, out_ref, att_ref, all_ref):
    b = pl.program_id(0)
    heads = cur_ref.shape[1] // VH
    r_at, l_at = iota((BLK, BLK), 0), iota((BLK, BLK), 1)
    gap = r_at - l_at
    near = (gap >= 0) & (gap < WIN)
    per = BLK // WIN
    masks = [jnp.where(near & ((l_at >> 5) == q), 1.0, 0.0).astype(BF) for q in range(per)]
    r_at, l_at = iota((WIN, BLK), 0), iota((WIN, BLK), 1)
    before = jnp.where((BLK + r_at - l_at) < WIN, 1.0, 0.0).astype(BF)
    blank = jnp.zeros((BLK - WIN, BLK), BF)
    packed = live_rows(goes_ref, own_ref, other_ref)
    for group in range(heads // per):
        one = packed[:, group * BLK : (group + 1) * BLK].astype(F32)
        turned = [one.astype(BF)]
        for q in range(1, per):
            turned.append(pltpu.roll(one, q * WIN, 1).astype(BF))
        for i in range(per):
            cols = slice((group * per + i) * VH, (group * per + i + 1) * VH)
            last = turned[(per - 1 - i) % per]
            olds = [prev_ref[:, cols], cur_ref[:BLK, cols]]
            for t in range(STEP // BLK):
                rows = slice(t * BLK, (t + 1) * BLK)
                band = turned[(-i) % per][rows] * masks[0]
                for q in range(1, per):
                    band = band + turned[(q - i) % per][rows] * masks[q]
                corner = jnp.concatenate([last[rows][:WIN] * before, blank], axis=0)
                att = dot(
                    jnp.concatenate([corner, band], axis=1),
                    jnp.concatenate([olds[t], cur_ref[rows, cols]], axis=0),
                )
                att_ref[rows, cols] = att.astype(BF)
    part = nt(att_ref[...], wo_ref[...]).astype(BF)
    share = STEP // 8
    r_at, l_at = iota((STEP, STEP), 0), iota((STEP, STEP), 1)
    order = ((r_at & (share - 1)) * 8 + (r_at >> 5)) == l_at
    part = dot(jnp.where(order, 1.0, 0.0).astype(BF), part)
    rows = pl.ds(pl.multiple_of(b * share, share), share)
    for m in range(8):
        all_ref[m, rows, :] = part[m * share : (m + 1) * share]

    @pl.when(b == pl.num_programs(0) - 1)
    def _():
        for m in range(8):
            out_ref[m] = all_ref[m].T.astype(BF)


def mix_project(goes, own, other, values, wo):
    width = values.shape[1]
    n = wo.shape[0]
    shape = (8, n, LIVE // 8)
    return pl.pallas_call(
        mix_kernel,
        grid=(LIVE // STEP,),
        out_shape=jax.ShapeDtypeStruct(shape, BF),
        in_specs=[
            whole(goes.shape),
            whole(own.shape),
            whole(other.shape),
            pl.BlockSpec((BLK, width), lambda b: (jnp.maximum(b * (STEP // BLK) - 1, 0), 0)),
            pl.BlockSpec((STEP, width), lambda b: (b, 0)),
            whole(wo.shape),
        ],
        out_specs=whole(shape),
        scratch_shapes=[pltpu.VMEM((STEP, width), BF), pltpu.VMEM((8, LIVE // 8, n), F32)],
        cost_estimate=cost(9),
        compiler_params=pltpu.CompilerParams(vmem_limit_bytes=50 * 2**20),
        name="mix_project",
    )(goes, own, other, values, values, wo)


def gate_up_kernel(steps, own_ref, other_ref, gain_ref, gate_ref, up_ref, *refs):
    outs, x_ref = refs[:-1], refs[-1]
    core, y = lax.axis_index("c"), lax.axis_index("y")
    x_at, zl = lax.axis_index("x"), lax.axis_index("zl")
    k, chunk = own_ref.shape[2:]
    ff = gate_ref.shape[0]
    gain = jnp.broadcast_to(gain_ref[...], (8, gain_ref.shape[1])).T
    x_ref[:, :8] = gain.astype(F32)
    squares = []
    scaled = []
    for dx, dz in steps:
        spot = ((x_at + dx) & 3) * 2 + (zl ^ dz)
        total = jnp.zeros((1, chunk), F32)
        for low in range(2):
            s = (y - (spot >> 2) * 2 - low) & 3
            one, two = own_ref[s, spot & 3], other_ref[s, spot & 3]
            for half in range(2):
                x = jnp.where(core == half, one, two).astype(F32)
                total = total + jnp.sum(x * x, axis=0, keepdims=True)
                rows = slice((low * 2 + half) * k, (low * 2 + half + 1) * k)
                scaled.append((x * x_ref[rows, :1]).astype(BF))
        squares.append(total)
    columns = [
        jnp.concatenate(scaled[4 * i : 4 * i + 4], axis=0) for i in range(len(steps))
    ]
    x = jnp.concatenate(columns, axis=1)
    gate = dot(gate_ref[...], x).astype(BF)
    up = dot(up_ref[...], x).astype(BF)
    row = iota((16, chunk), 0)
    for i, out_ref in enumerate(outs):
        cols = slice(i * chunk, (i + 1) * chunk)
        high = squares[i].astype(BF).astype(F32)
        extra = jnp.where(row == 0, high, jnp.where(row == 1, squares[i] - high, 0.0))
        out_ref[:ff, :] = gate[:, cols]
        out_ref[ff : 2 * ff, :] = up[:, cols]
        out_ref[2 * ff :, :] = extra.astype(BF)


def gate_up(steps, own, other, gain, gate_weight, up_weight):
    k, chunk = own.shape[2:]
    ff, width = gate_weight.shape
    shape = (2 * ff + 16, chunk)
    arrays = (own, other, gain, gate_weight, up_weight)
    return pl.pallas_call(
        functools.partial(gate_up_kernel, steps),
        grid=(1,),
        out_shape=[jax.ShapeDtypeStruct(shape, BF)] * len(steps),
        in_specs=[whole(a.shape) for a in arrays],
        out_specs=[whole(shape)] * len(steps),
        scratch_shapes=[pltpu.VMEM((width, BLK), F32)],
        cost_estimate=cost(4),
        compiler_params=pltpu.CompilerParams(vmem_limit_bytes=24 * 2**20),
        name="gate_up",
    )(*arrays)


def down_kernel(flip, *refs):
    pieces, (w_ref, out_ref) = refs[:8], refs[8:]
    swapped = lax.axis_index("zl") ^ lax.axis_index("c") ^ flip
    x = jnp.concatenate(
        [
            jnp.where(swapped == 0, pieces[4 + dx][...], pieces[dx][...])
            for dx in range(4)
        ],
        axis=1,
    )
    out = lax.dot_general(
        x, w_ref[...], (((0,), (0,)), ((), ())), preferred_element_type=F32
    )
    out_ref[...] = out.reshape(out_ref.shape).astype(out_ref.dtype)


def down(flip, pieces, weight, kind):
    shape = (4, pieces[0].shape[1], weight.shape[1])
    return pl.pallas_call(
        functools.partial(down_kernel, flip),
        grid=(1,),
        out_shape=jax.ShapeDtypeStruct(shape, kind),
        in_specs=[whole(p.shape) for p in pieces] + [whole(weight.shape)],
        out_specs=whole(shape),
        compiler_params=pltpu.CompilerParams(vmem_limit_bytes=24 * 2**20),
        cost_estimate=cost(2),
        name="down",
    )(*pieces, weight)


def sent_along_hd(x, dx, dz):
    return lax.ppermute(x, HD, [(i, ((i // 2 + dx) % 4) * 2 + ((i % 2) ^ dz)) for i in range(8)])


def exchange(x, axes):
    return lax.all_to_all(x, axes, split_axis=0, concat_axis=0, tiled=True)


def gather(x, axes):
    n = lax.axis_size(axes)
    return exchange(jnp.broadcast_to(x[None], (n,) + x.shape), axes)


def pick(x, index):
    return lax.dynamic_index_in_dim(x, index, 0, keepdims=False)


def on_device(
    query_nope,
    query_rope,
    latent,
    key_rope,
    key_up,
    value_up,
    output_weight,
    residual,
    norm_gain,
    gate_weight,
    up_weight,
    down_weight,
    rank_tokens,
    request_ids,
):
    slots = latent.shape[0]
    ranks = rank_tokens.shape[0]
    zh, y, c = (lax.axis_index(a) for a in DP)
    rank = (zh * 4 + y) * 2 + c
    chunk = LIVE // 8
    width = residual.shape[1]
    quarter = width // 4
    model = 8 * width

    every = jnp.arange(ranks, dtype=jnp.int32)

    def starts(which):
        return jnp.sum(jnp.where(every < which[..., None], rank_tokens, 0), axis=-1)

    def lengths(which):
        return jnp.sum(jnp.where(every == which[..., None], rank_tokens, 0), axis=-1)

    own_start, own_length = starts(rank), lengths(rank)
    slot = jnp.arange(slots, dtype=jnp.int32)

    pieces = pack(rank_tokens, latent, residual)
    pieces = [pieces[0]] + [shifted(pieces[s], "zh", s) for s in (1, 2, 3)]

    weights = score_weights(
        rank_tokens, query_nope, query_rope, latent, key_rope, key_up, request_ids
    )
    weights = exchange(weights, "zh")
    pieces = repack(*pieces)
    weights, gain, _ = lax.optimization_barrier((weights, norm_gain[None, :], pieces))
    weights = jnp.broadcast_to(weights[None], (4,) + weights.shape)
    pieces = [pieces[0]] + [shifted(pieces[s], "y", s) for s in (1, 2, 3)]
    pieces, weights = lax.optimization_barrier((pieces, weights))
    got = jnp.concatenate(pieces, axis=0)
    got_other = shifted(got, "c", 1)
    weights = exchange(weights, "y").reshape(-1, weights.shape[3])

    four = jnp.arange(4, dtype=jnp.int32)
    eight = jnp.arange(8, dtype=jnp.int32)
    core = jnp.stack([c, 1 - c])[:, None, None]
    ahead = (four[None, None, :] * 4 + four[None, :, None]) * 2 + core
    goes = jnp.where(slot < lengths(ahead)[..., None], starts(ahead)[..., None] + slot, -1)
    goes = goes.reshape(2, 1, -1)
    back = (((zh - four) & 3)[None, None, :] * 4 + ((y - four) & 3)[None, :, None]) * 2 + core
    back_start, back_count = starts(back)[..., None], lengths(back)[..., None]
    goes_back = jnp.where(slot < back_count, back_start + slot, -1).reshape(2, 4, -1)
    goes_back = jnp.pad(goes_back, ((0, 0), (0, 0), (0, 32)), constant_values=-1).reshape(2, 1, -1)
    values = live_values(goes_back, got, got_other, value_up)

    place = (((zh * 2 + (y >> 1)) - back_start) & 7) + 8 * eight
    come = jnp.where(place < back_count, (back_start + place) >> 3, -1)
    come = (come.reshape(2, -1, 1) == jnp.arange(chunk, dtype=jnp.int32)).astype(BF)

    def tn(a, b):
        return lax.dot_general(a, b, (((0,), (0,)), ((), ())), preferred_element_type=F32)

    rows = [a.reshape(4, -1, a.shape[1])[:, 4 * slots :].reshape(-1, a.shape[1]) for a in (got, got_other)]
    rows = tn(rows[0], come[0]) + tn(rows[1], come[1])
    rows = jnp.where(c == 0, rows[:quarter], rows[quarter : 2 * quarter])
    weights, values = lax.optimization_barrier((weights, values))
    weights_other = shifted(weights, "c", 1)
    part = mix_project(goes, weights, weights_other, values, output_weight.T)
    projected = jnp.sum(exchange(part, HD).astype(F32), axis=0).astype(BF)

    swap = []
    for a in range(4):
        for b in range(8):
            for e in range(4):
                for f in range(2):
                    to = (e * 8 + (f * 4 + (b & 3))) * 8 + a * 2 + (b >> 2)
                    swap.append(((a * 8 + b) * 8 + e * 2 + f, to))
    projected = lax.ppermute(projected, DP + HD, swap)
    mixed = (rows + projected.astype(F32)).astype(BF)
    full = jnp.stack([mixed] + [shifted(mixed, "zh", k) for k in (1, 2, 3)])

    full = jnp.stack([full] + [shifted(full, "y", s) for s in (1, 2, 3)])
    full_other = shifted(full, "c", 1)
    ff = down_weight.shape[0]
    arrays = (full, full_other, gain, gate_weight.T, up_weight.T)
    late = [(0, 0), (1, 0), (3, 0), (2, 0)]
    soon = [(0, 1), (1, 1), (3, 1), (2, 1)]
    parts = list(zip(late, gate_up(late, *arrays))) + list(zip(soon, gate_up(soon, *arrays)))
    total = parts[0][1].astype(F32)
    for (dx, dz), part in parts[1:]:
        total = total + sent_along_hd(part, dx, dz).astype(F32)
    scale = lax.rsqrt((total[2 * ff : 2 * ff + 1] + total[2 * ff + 1 : 2 * ff + 2]) / model + 1e-06)
    hidden = (jax.nn.silu(total[:ff] * scale) * (total[ff : 2 * ff] * scale)).astype(BF)
    got_hidden = {(0, 0): hidden}
    for step in soon + late[1:]:
        got_hidden[step] = sent_along_hd(hidden, *step)
    hidden = [got_hidden[r % 4, 1 - r // 4] for r in range(8)]

    sent = shifted(down(1, hidden, down_weight, BF), "c", 1)
    total = down(0, hidden, down_weight, F32) + sent.astype(F32)
    turn = lax.axis_index("x") - y
    pieces = [pick(total, (turn - s) & 3) for s in range(4)]
    total = pieces[0]
    for s in (1, 2, 3):
        total = total + shifted(pieces[s].astype(BF), "y", s).astype(F32)
    spot = y * 2 + c
    begin = starts(every)
    m = ((zh - (spot & 3)) & 3) * 2 + (spot >> 2)
    place = ((m - begin[:, None]) & 7) + 8 * eight[None, :]
    comes = jnp.where(place < rank_tokens[:, None], (begin[:, None] + place) >> 3, -1)
    expand = (comes.reshape(ranks * 8, 1) == jnp.arange(chunk, dtype=jnp.int32)).astype(BF)
    at = [(y - (spot >> 2) * 2 - low) & 3 for low in range(2)]
    pair = [jnp.stack([pick(pick(a, s), spot & 3) for s in at]) for a in (full, full_other)]
    low = jnp.where(c == 0, pair[0], pair[1])
    high = jnp.where(c == 0, pair[1], pair[0])
    own = jnp.stack([low, high], axis=1).reshape(width, chunk)
    here = (jnp.arange(ranks * 8, dtype=jnp.int32) >> 6) == zh
    own = nt(jnp.where(here[:, None], expand, jnp.zeros_like(expand)), own)
    result = (dot(expand, total.astype(BF)) + own).astype(BF).reshape(ranks, 8, width)
    result = exchange(result, DP).reshape(ranks * 8, width)
    source = jnp.arange(ranks, dtype=jnp.int32)
    chunk_of = (((source >> 3) - (source & 3)) & 3) * 2 + ((source >> 2) & 1)
    fits = chunk_of[None, :, None] == ((own_start + slot) & 7)[:, None, None]
    fits = fits & (eight[None, None, :] == (slot >> 3)[:, None, None])
    fits = fits & (slot < own_length)[:, None, None]
    return dot(fits.astype(BF).reshape(slots, ranks * 8), result).astype(BF)


def solution(mesh):
    mesh = Mesh(mesh.devices.reshape(4, 4, 2, 4, 2), DP + HD)
    in_specs = (
        P(DP, HD),
        P(DP, HD),
        P(DP, None),
        P(DP, None),
        P(None, HD),
        P(None, HD),
        P(HD, DP),
        P(DP, HD),
        P(HD),
        P(HD, DP),
        P(HD, DP),
        P(DP, HD),
        P(),
        P(DP, None),
    )
    return jax.shard_map(
        on_device, mesh=mesh, in_specs=in_specs, out_specs=P(DP, HD), check_vma=False
    )
```

```python
import functools

import jax
import jax.numpy as jnp
from jax import lax
from jax.experimental import pallas as pl
from jax.experimental.pallas import tpu as pltpu
from jax.sharding import Mesh, PartitionSpec as P

BF = jnp.bfloat16
F32 = jnp.float32
NOPE = 128
ROPE = 64
VH = 128
WIN = 32
LIVE = 1024
BLK = 128
STEP = 256
DP = ("zh", "y", "c")
HD = ("x", "zl")


def dot(a, b):
    return jnp.dot(a, b, preferred_element_type=F32)


def shifted(x, axis, shift):
    n = lax.axis_size(axis)
    return lax.ppermute(x, axis, [(i, (i + shift) % n) for i in range(n)])


def iota(shape, dim):
    return lax.broadcasted_iota(jnp.int32, shape, dim)


def nt(a, b):
    return lax.dot_general(a, b, (((1,), (1,)), ((), ())), preferred_element_type=F32)


def whole(shape):
    return pl.BlockSpec(shape, lambda *_: (0,) * len(shape), pipeline_mode=pl.Buffered(1))


def cost(us):
    return pl.CostEstimate(flops=us * 10**9, bytes_accessed=us * 3 * 10**6, transcendentals=0)


def rank_here():
    return (lax.axis_index("zh") * 4 + lax.axis_index("y")) * 2 + lax.axis_index("c")


def live_before(counts_ref):
    place = rank_here()
    return lax.fori_loop(
        0,
        counts_ref.shape[0],
        lambda i, a: a + jnp.where(i < place, counts_ref[i], 0),
        jnp.int32(0),
    )


def pack_kernel(counts_ref, lat_ref, res_ref, *refs):
    outs, rows_ref = refs[:4], refs[4]
    slots, width = res_ref.shape
    half, lanes = width // 2, lat_ref.shape[1]
    zh = lax.axis_index("zh")
    start = live_before(counts_ref)
    i_at, slot = iota((slots, slots), 0), iota((slots, slots), 1)
    roll = ((((i_at >> 3) - start) & 7) + 8 * (i_at & 7)) == slot
    rows_ref[...] = dot(jnp.where(roll, 1.0, 0.0).astype(BF), res_ref[...])
    fill = jnp.zeros((16, lanes - half), F32)
    for s in range(4):
        outs[s][:slots, :] = lat_ref[...]
        for high in range(2):
            m = ((zh + s) & 3) * 2 + high
            piece = rows_ref[pl.ds(pl.multiple_of(m * 8, 8), 8), :]
            piece = jnp.concatenate([piece[:, :half], piece[:, half:]], axis=0)
            piece = jnp.concatenate([piece, fill], axis=1)
            outs[s][slots + 16 * high : slots + 16 * (high + 1), :] = piece.astype(BF)


def pack(counts, latent, residual):
    slots, lanes = latent.shape
    shape = (slots + 32, lanes)
    return pl.pallas_call(
        pack_kernel,
        grid=(1,),
        out_shape=[jax.ShapeDtypeStruct(shape, BF)] * 4,
        in_specs=[
            pl.BlockSpec(memory_space=pltpu.SMEM),
            whole(latent.shape),
            whole(residual.shape),
        ],
        out_specs=[whole(shape)] * 4,
        scratch_shapes=[pltpu.VMEM(residual.shape, F32)],
        cost_estimate=cost(2),
        name="pack",
    )(counts, latent, residual)


def repack_kernel(*refs):
    ins, outs, rows_ref = refs[:4], refs[4:8], refs[8]
    slots = ins[0].shape[0] - 32
    y = lax.axis_index("y")
    for t in range(4):
        rows_ref[t] = ins[t][slots:, :].astype(F32)
    for s in range(4):
        at = pl.ds(pl.multiple_of(((y + s) & 3) * 8, 8), 8)
        for t in range(4):
            outs[s][t * slots : (t + 1) * slots, :] = ins[t][:slots, :]
        for t in (0, 2):
            pair = jnp.concatenate([rows_ref[t, at, :], rows_ref[t + 1, at, :]], axis=0)
            outs[s][4 * slots + 8 * t : 4 * slots + 8 * t + 16, :] = pair.astype(BF)


def repack(*pieces):
    rows, lanes = pieces[0].shape
    shape = (4 * (rows - 32) + 32, lanes)
    return pl.pallas_call(
        repack_kernel,
        grid=(1,),
        out_shape=[jax.ShapeDtypeStruct(shape, BF)] * 4,
        in_specs=[whole(pieces[0].shape)] * 4,
        out_specs=[whole(shape)] * 4,
        scratch_shapes=[pltpu.VMEM((4, 32, lanes), F32)],
        cost_estimate=cost(2),
        name="repack",
    )(*pieces)


def score_kernel(counts_ref, qn_ref, qr_ref, lat_ref, kr_ref, ku_ref, req_ref, out_ref, s_ref):
    slots = lat_ref.shape[0]
    heads = ku_ref.shape[1] // NOPE
    before = live_before(counts_ref)
    keys = dot(lat_ref[...], ku_ref[...]).astype(BF)
    key_rope = kr_ref[...]
    s_at, t_at = iota((slots, slots), 0), iota((slots, slots), 1)
    across = jnp.broadcast_to(req_ref[...], (slots, slots))
    down = jnp.sum(jnp.where(s_at == t_at, across, 0), axis=1, keepdims=True)
    allowed = (across == down) & (t_at <= s_at)
    t_row, lane = iota((slots, BLK), 0), iota((slots, BLK), 1)
    lands = ((before + t_row) & (WIN - 1)) == (lane & (WIN - 1))
    per = BLK // WIN
    for h in range(heads):
        rows = slice(h * slots, (h + 1) * slots)
        s = nt(qn_ref[:, h * NOPE : (h + 1) * NOPE], keys[:, h * NOPE : (h + 1) * NOPE])
        s = s + nt(qr_ref[:, h * ROPE : (h + 1) * ROPE], key_rope)
        s_ref[rows, :] = jnp.where(allowed, s * (NOPE + ROPE) ** (-0.5), jnp.float32(-1e30))
    s = s_ref[...]
    raised = jnp.exp(s - jnp.max(s, axis=-1, keepdims=True))
    w = (raised / jnp.sum(raised, axis=-1, keepdims=True)).astype(BF)
    folded = dot(w, jnp.where(lands, 1.0, 0.0).astype(BF))
    for group in range(heads // per):
        out = folded[group * per * slots : (group * per + 1) * slots]
        for i in range(1, per):
            h = group * per + i
            out = jnp.where((lane >> 5) == i, folded[h * slots : (h + 1) * slots], out)
        for copy in range(out_ref.shape[0]):
            out_ref[copy, :, group * BLK : (group + 1) * BLK] = out.astype(BF)


def score_weights(counts, *arrays):
    slots, heads = arrays[2].shape[0], arrays[4].shape[1] // NOPE
    shape = (4, slots, heads * WIN)
    return pl.pallas_call(
        score_kernel,
        grid=(1,),
        out_shape=jax.ShapeDtypeStruct(shape, BF),
        in_specs=[pl.BlockSpec(memory_space=pltpu.SMEM)] + [whole(a.shape) for a in arrays],
        out_specs=whole(shape),
        scratch_shapes=[pltpu.VMEM((slots * heads, slots), F32)],
        cost_estimate=cost(4),
        name="score_weights",
    )(counts, *arrays)


def live_rows(goes_ref, own_ref, other_ref):
    row = iota((STEP, own_ref.shape[0]), 0) + pl.program_id(0) * STEP
    out = dot(jnp.where(goes_ref[0] == row, 1.0, 0.0).astype(BF), own_ref[...])
    out = out + dot(jnp.where(goes_ref[1] == row, 1.0, 0.0).astype(BF), other_ref[...])
    return out.astype(BF)


def values_kernel(goes_ref, own_ref, other_ref, up_ref, out_ref):
    out_ref[...] = dot(live_rows(goes_ref, own_ref, other_ref), up_ref[...]).astype(BF)


def live_values(goes, own, other, up):
    width = up.shape[1]
    return pl.pallas_call(
        values_kernel,
        grid=(LIVE // STEP,),
        out_shape=jax.ShapeDtypeStruct((LIVE, width), BF),
        in_specs=[whole(a.shape) for a in (goes, own, other, up)],
        out_specs=pl.BlockSpec((STEP, width), lambda b: (b, 0)),
        cost_estimate=cost(0),
        compiler_params=pltpu.CompilerParams(vmem_limit_bytes=24 * 2**20),
        name="live_values",
    )(goes, own, other, up)


def mix_kernel(goes_ref, own_ref, other_ref, prev_ref, cur_ref, wo_ref, out_ref, att_ref, all_ref):
    b = pl.program_id(0)
    heads = cur_ref.shape[1] // VH
    r_at, l_at = iota((BLK, BLK), 0), iota((BLK, BLK), 1)
    gap = r_at - l_at
    near = (gap >= 0) & (gap < WIN)
    per = BLK // WIN
    masks = [jnp.where(near & ((l_at >> 5) == q), 1.0, 0.0).astype(BF) for q in range(per)]
    r_at, l_at = iota((WIN, BLK), 0), iota((WIN, BLK), 1)
    before = jnp.where((BLK + r_at - l_at) < WIN, 1.0, 0.0).astype(BF)
    blank = jnp.zeros((BLK - WIN, BLK), BF)
    packed = live_rows(goes_ref, own_ref, other_ref)
    for group in range(heads // per):
        one = packed[:, group * BLK : (group + 1) * BLK].astype(F32)
        turned = [one.astype(BF)]
        for q in range(1, per):
            turned.append(pltpu.roll(one, q * WIN, 1).astype(BF))
        for i in range(per):
            cols = slice((group * per + i) * VH, (group * per + i + 1) * VH)
            last = turned[(per - 1 - i) % per]
            olds = [prev_ref[:, cols], cur_ref[:BLK, cols]]
            for t in range(STEP // BLK):
                rows = slice(t * BLK, (t + 1) * BLK)
                band = turned[(-i) % per][rows] * masks[0]
                for q in range(1, per):
                    band = band + turned[(q - i) % per][rows] * masks[q]
                corner = jnp.concatenate([last[rows][:WIN] * before, blank], axis=0)
                att = dot(
                    jnp.concatenate([corner, band], axis=1),
                    jnp.concatenate([olds[t], cur_ref[rows, cols]], axis=0),
                )
                att_ref[rows, cols] = att.astype(BF)
    part = nt(att_ref[...], wo_ref[...]).astype(BF)
    share = STEP // 8
    r_at, l_at = iota((STEP, STEP), 0), iota((STEP, STEP), 1)
    order = ((r_at & (share - 1)) * 8 + (r_at >> 5)) == l_at
    part = dot(jnp.where(order, 1.0, 0.0).astype(BF), part)
    rows = pl.ds(pl.multiple_of(b * share, share), share)
    for m in range(8):
        all_ref[m, rows, :] = part[m * share : (m + 1) * share]

    @pl.when(b == pl.num_programs(0) - 1)
    def _():
        for m in range(8):
            out_ref[m] = all_ref[m].T.astype(BF)


def mix_project(goes, own, other, values, wo):
    width = values.shape[1]
    n = wo.shape[0]
    shape = (8, n, LIVE // 8)
    return pl.pallas_call(
        mix_kernel,
        grid=(LIVE // STEP,),
        out_shape=jax.ShapeDtypeStruct(shape, BF),
        in_specs=[
            whole(goes.shape),
            whole(own.shape),
            whole(other.shape),
            pl.BlockSpec((BLK, width), lambda b: (jnp.maximum(b * (STEP // BLK) - 1, 0), 0)),
            pl.BlockSpec((STEP, width), lambda b: (b, 0)),
            whole(wo.shape),
        ],
        out_specs=whole(shape),
        scratch_shapes=[pltpu.VMEM((STEP, width), BF), pltpu.VMEM((8, LIVE // 8, n), F32)],
        cost_estimate=cost(9),
        compiler_params=pltpu.CompilerParams(vmem_limit_bytes=50 * 2**20),
        name="mix_project",
    )(goes, own, other, values, values, wo)


def gate_up_kernel(steps, own_ref, other_ref, gain_ref, gate_ref, up_ref, *refs):
    outs, x_ref = refs[:-1], refs[-1]
    core, y = lax.axis_index("c"), lax.axis_index("y")
    x_at, zl = lax.axis_index("x"), lax.axis_index("zl")
    k, chunk = own_ref.shape[2:]
    ff = gate_ref.shape[0]
    gain = jnp.broadcast_to(gain_ref[...], (8, gain_ref.shape[1])).T
    x_ref[:, :8] = gain.astype(F32)
    squares = []
    scaled = []
    for dx, dz in steps:
        spot = ((x_at + dx) & 3) * 2 + (zl ^ dz)
        total = jnp.zeros((1, chunk), F32)
        for low in range(2):
            s = (y - (spot >> 2) * 2 - low) & 3
            one, two = own_ref[s, spot & 3], other_ref[s, spot & 3]
            for half in range(2):
                x = jnp.where(core == half, one, two).astype(F32)
                total = total + jnp.sum(x * x, axis=0, keepdims=True)
                rows = slice((low * 2 + half) * k, (low * 2 + half + 1) * k)
                scaled.append((x * x_ref[rows, :1]).astype(BF))
        squares.append(total)
    columns = [
        jnp.concatenate(scaled[4 * i : 4 * i + 4], axis=0) for i in range(len(steps))
    ]
    x = jnp.concatenate(columns, axis=1)
    gate = dot(gate_ref[...], x).astype(BF)
    up = dot(up_ref[...], x).astype(BF)
    row = iota((16, chunk), 0)
    for i, out_ref in enumerate(outs):
        cols = slice(i * chunk, (i + 1) * chunk)
        high = squares[i].astype(BF).astype(F32)
        extra = jnp.where(row == 0, high, jnp.where(row == 1, squares[i] - high, 0.0))
        out_ref[:ff, :] = gate[:, cols]
        out_ref[ff : 2 * ff, :] = up[:, cols]
        out_ref[2 * ff :, :] = extra.astype(BF)


def gate_up(steps, own, other, gain, gate_weight, up_weight):
    k, chunk = own.shape[2:]
    ff, width = gate_weight.shape
    shape = (2 * ff + 16, chunk)
    arrays = (own, other, gain, gate_weight, up_weight)
    return pl.pallas_call(
        functools.partial(gate_up_kernel, steps),
        grid=(1,),
        out_shape=[jax.ShapeDtypeStruct(shape, BF)] * len(steps),
        in_specs=[whole(a.shape) for a in arrays],
        out_specs=[whole(shape)] * len(steps),
        scratch_shapes=[pltpu.VMEM((width, BLK), F32)],
        cost_estimate=cost(4),
        compiler_params=pltpu.CompilerParams(vmem_limit_bytes=24 * 2**20),
        name="gate_up",
    )(*arrays)


def down_kernel(flip, *refs):
    pieces, (w_ref, out_ref) = refs[:8], refs[8:]
    swapped = lax.axis_index("zl") ^ lax.axis_index("c") ^ flip
    x = jnp.concatenate(
        [
            jnp.where(swapped == 0, pieces[4 + dx][...], pieces[dx][...])
            for dx in range(4)
        ],
        axis=1,
    )
    out = lax.dot_general(
        x, w_ref[...], (((0,), (0,)), ((), ())), preferred_element_type=F32
    )
    out_ref[...] = out.reshape(out_ref.shape).astype(out_ref.dtype)


def down(flip, pieces, weight, kind):
    shape = (4, pieces[0].shape[1], weight.shape[1])
    return pl.pallas_call(
        functools.partial(down_kernel, flip),
        grid=(1,),
        out_shape=jax.ShapeDtypeStruct(shape, kind),
        in_specs=[whole(p.shape) for p in pieces] + [whole(weight.shape)],
        out_specs=whole(shape),
        compiler_params=pltpu.CompilerParams(vmem_limit_bytes=24 * 2**20),
        cost_estimate=cost(2),
        name="down",
    )(*pieces, weight)


def sent_along_hd(x, dx, dz):
    return lax.ppermute(x, HD, [(i, ((i // 2 + dx) % 4) * 2 + ((i % 2) ^ dz)) for i in range(8)])


def exchange(x, axes):
    return lax.all_to_all(x, axes, split_axis=0, concat_axis=0, tiled=True)


def gather(x, axes):
    n = lax.axis_size(axes)
    return exchange(jnp.broadcast_to(x[None], (n,) + x.shape), axes)


def pick(x, index):
    return lax.dynamic_index_in_dim(x, index, 0, keepdims=False)


def on_device(
    query_nope,
    query_rope,
    latent,
    key_rope,
    key_up,
    value_up,
    output_weight,
    residual,
    norm_gain,
    gate_weight,
    up_weight,
    down_weight,
    rank_tokens,
    request_ids,
):
    slots = latent.shape[0]
    ranks = rank_tokens.shape[0]
    zh, y, c = (lax.axis_index(a) for a in DP)
    rank = (zh * 4 + y) * 2 + c
    chunk = LIVE // 8
    width = residual.shape[1]
    quarter = width // 4
    model = 8 * width

    every = jnp.arange(ranks, dtype=jnp.int32)

    def starts(which):
        return jnp.sum(jnp.where(every < which[..., None], rank_tokens, 0), axis=-1)

    def lengths(which):
        return jnp.sum(jnp.where(every == which[..., None], rank_tokens, 0), axis=-1)

    own_start, own_length = starts(rank), lengths(rank)
    slot = jnp.arange(slots, dtype=jnp.int32)

    pieces = pack(rank_tokens, latent, residual)
    pieces = [pieces[0]] + [shifted(pieces[s], "zh", s) for s in (1, 2, 3)]

    weights = score_weights(
        rank_tokens, query_nope, query_rope, latent, key_rope, key_up, request_ids
    )
    pieces, _ = lax.optimization_barrier((pieces, weights))
    weights = exchange(weights, "zh")
    pieces = repack(*pieces)
    gain, _ = lax.optimization_barrier((norm_gain[None, :], weights))
    pieces = [pieces[0]] + [shifted(pieces[s], "y", s) for s in (1, 2, 3)]
    pieces, _ = lax.optimization_barrier((pieces, weights))
    got = jnp.concatenate(pieces, axis=0)
    got_other = shifted(got, "c", 1)
    weights = weights.reshape(-1, weights.shape[2])
    weights = [weights] + [shifted(weights, "y", s) for s in (1, 2, 3)]

    four = jnp.arange(4, dtype=jnp.int32)
    eight = jnp.arange(8, dtype=jnp.int32)
    core = jnp.stack([c, 1 - c])[:, None, None]
    ahead = (four[None, None, :] * 4 + ((y - four) & 3)[None, :, None]) * 2 + core
    goes = jnp.where(slot < lengths(ahead)[..., None], starts(ahead)[..., None] + slot, -1)
    goes = goes.reshape(2, 1, -1)
    back = (((zh - four) & 3)[None, None, :] * 4 + ((y - four) & 3)[None, :, None]) * 2 + core
    back_start, back_count = starts(back)[..., None], lengths(back)[..., None]
    goes_back = jnp.where(slot < back_count, back_start + slot, -1).reshape(2, 4, -1)
    goes_back = jnp.pad(goes_back, ((0, 0), (0, 0), (0, 32)), constant_values=-1).reshape(2, 1, -1)
    values = live_values(goes_back, got, got_other, value_up)

    place = (((zh * 2 + (y >> 1)) - back_start) & 7) + 8 * eight
    come = jnp.where(place < back_count, (back_start + place) >> 3, -1)
    come = (come.reshape(2, -1, 1) == jnp.arange(chunk, dtype=jnp.int32)).astype(BF)

    def tn(a, b):
        return lax.dot_general(a, b, (((0,), (0,)), ((), ())), preferred_element_type=F32)

    rows = [a.reshape(4, -1, a.shape[1])[:, 4 * slots :].reshape(-1, a.shape[1]) for a in (got, got_other)]
    rows = tn(rows[0], come[0]) + tn(rows[1], come[1])
    rows = jnp.where(c == 0, rows[:quarter], rows[quarter : 2 * quarter])
    weights, values = lax.optimization_barrier((weights, values))
    weights = jnp.concatenate(weights, axis=0)
    weights, _ = lax.optimization_barrier((weights, got_other))
    weights_other = shifted(weights, "c", 1)
    part = mix_project(goes, weights, weights_other, values, output_weight.T)
    projected = jnp.sum(exchange(part, HD).astype(F32), axis=0).astype(BF)

    swap = []
    for a in range(4):
        for b in range(8):
            for e in range(4):
                for f in range(2):
                    to = (e * 8 + (f * 4 + (b & 3))) * 8 + a * 2 + (b >> 2)
                    swap.append(((a * 8 + b) * 8 + e * 2 + f, to))
    projected = lax.ppermute(projected, DP + HD, swap)
    mixed = (rows + projected.astype(F32)).astype(BF)
    full = jnp.stack([mixed] + [shifted(mixed, "zh", k) for k in (1, 2, 3)])

    full = jnp.stack([full] + [shifted(full, "y", s) for s in (1, 2, 3)])
    full_other = shifted(full, "c", 1)
    ff = down_weight.shape[0]
    arrays = (full, full_other, gain, gate_weight.T, up_weight.T)
    late = [(0, 0), (1, 0), (3, 0), (2, 0)]
    soon = [(0, 1), (1, 1), (3, 1), (2, 1)]
    parts = list(zip(late, gate_up(late, *arrays))) + list(zip(soon, gate_up(soon, *arrays)))
    total = parts[0][1].astype(F32)
    for (dx, dz), part in parts[1:]:
        total = total + sent_along_hd(part, dx, dz).astype(F32)
    scale = lax.rsqrt((total[2 * ff : 2 * ff + 1] + total[2 * ff + 1 : 2 * ff + 2]) / model + 1e-06)
    hidden = (jax.nn.silu(total[:ff] * scale) * (total[ff : 2 * ff] * scale)).astype(BF)
    got_hidden = {(0, 0): hidden}
    for step in soon + late[1:]:
        got_hidden[step] = sent_along_hd(hidden, *step)
    hidden = [got_hidden[r % 4, 1 - r // 4] for r in range(8)]

    sent = shifted(down(1, hidden, down_weight, BF), "c", 1)
    total = down(0, hidden, down_weight, F32) + sent.astype(F32)
    turn = lax.axis_index("x") - y
    pieces = [pick(total, (turn - s) & 3) for s in range(4)]
    total = pieces[0]
    for s in (1, 2, 3):
        total = total + shifted(pieces[s].astype(BF), "y", s).astype(F32)
    spot = y * 2 + c
    begin = starts(every)
    m = ((zh - (spot & 3)) & 3) * 2 + (spot >> 2)
    place = ((m - begin[:, None]) & 7) + 8 * eight[None, :]
    comes = jnp.where(place < rank_tokens[:, None], (begin[:, None] + place) >> 3, -1)
    expand = (comes.reshape(ranks * 8, 1) == jnp.arange(chunk, dtype=jnp.int32)).astype(BF)
    at = [(y - (spot >> 2) * 2 - low) & 3 for low in range(2)]
    pair = [jnp.stack([pick(pick(a, s), spot & 3) for s in at]) for a in (full, full_other)]
    low = jnp.where(c == 0, pair[0], pair[1])
    high = jnp.where(c == 0, pair[1], pair[0])
    own = jnp.stack([low, high], axis=1).reshape(width, chunk)
    here = (jnp.arange(ranks * 8, dtype=jnp.int32) >> 6) == zh
    own = nt(jnp.where(here[:, None], expand, jnp.zeros_like(expand)), own)
    result = (dot(expand, total.astype(BF)) + own).astype(BF).reshape(ranks, 8, width)
    result = exchange(result, DP).reshape(ranks * 8, width)
    source = jnp.arange(ranks, dtype=jnp.int32)
    chunk_of = (((source >> 3) - (source & 3)) & 3) * 2 + ((source >> 2) & 1)
    fits = chunk_of[None, :, None] == ((own_start + slot) & 7)[:, None, None]
    fits = fits & (eight[None, None, :] == (slot >> 3)[:, None, None])
    fits = fits & (slot < own_length)[:, None, None]
    return dot(fits.astype(BF).reshape(slots, ranks * 8), result).astype(BF)


def solution(mesh):
    mesh = Mesh(mesh.devices.reshape(4, 4, 2, 4, 2), DP + HD)
    in_specs = (
        P(DP, HD),
        P(DP, HD),
        P(DP, None),
        P(DP, None),
        P(None, HD),
        P(None, HD),
        P(HD, DP),
        P(DP, HD),
        P(HD),
        P(HD, DP),
        P(HD, DP),
        P(DP, HD),
        P(),
        P(DP, None),
    )
    return jax.shard_map(
        on_device, mesh=mesh, in_specs=in_specs, out_specs=P(DP, HD), check_vma=False
    )
```

```python
import functools

import jax
import jax.numpy as jnp
from jax import lax
from jax.experimental import pallas as pl
from jax.experimental.pallas import tpu as pltpu
from jax.sharding import Mesh, PartitionSpec as P

BF = jnp.bfloat16
F32 = jnp.float32
NOPE = 128
ROPE = 64
VH = 128
WIN = 32
LIVE = 1024
BLK = 128
STEP = 256
DP = ("zh", "y", "c")
HD = ("x", "zl")


def dot(a, b):
    return jnp.dot(a, b, preferred_element_type=F32)


def shifted(x, axis, shift):
    n = lax.axis_size(axis)
    return lax.ppermute(x, axis, [(i, (i + shift) % n) for i in range(n)])


def iota(shape, dim):
    return lax.broadcasted_iota(jnp.int32, shape, dim)


def nt(a, b):
    return lax.dot_general(a, b, (((1,), (1,)), ((), ())), preferred_element_type=F32)


def whole(shape):
    return pl.BlockSpec(shape, lambda *_: (0,) * len(shape), pipeline_mode=pl.Buffered(1))


def cost(us):
    return pl.CostEstimate(flops=us * 10**9, bytes_accessed=us * 3 * 10**6, transcendentals=0)


def rank_here():
    return (lax.axis_index("zh") * 4 + lax.axis_index("y")) * 2 + lax.axis_index("c")


def live_before(counts_ref):
    place = rank_here()
    return lax.fori_loop(
        0,
        counts_ref.shape[0],
        lambda i, a: a + jnp.where(i < place, counts_ref[i], 0),
        jnp.int32(0),
    )


def pack_kernel(counts_ref, lat_ref, res_ref, *refs):
    outs, rows_ref = refs[:4], refs[4]
    slots, width = res_ref.shape
    half, lanes = width // 2, lat_ref.shape[1]
    zh = lax.axis_index("zh")
    start = live_before(counts_ref)
    i_at, slot = iota((slots, slots), 0), iota((slots, slots), 1)
    roll = ((((i_at >> 3) - start) & 7) + 8 * (i_at & 7)) == slot
    rows_ref[...] = dot(jnp.where(roll, 1.0, 0.0).astype(BF), res_ref[...])
    fill = jnp.zeros((16, lanes - half), F32)
    for s in range(4):
        outs[s][:slots, :] = lat_ref[...]
        for high in range(2):
            m = ((zh + s) & 3) * 2 + high
            piece = rows_ref[pl.ds(pl.multiple_of(m * 8, 8), 8), :]
            piece = jnp.concatenate([piece[:, :half], piece[:, half:]], axis=0)
            piece = jnp.concatenate([piece, fill], axis=1)
            outs[s][slots + 16 * high : slots + 16 * (high + 1), :] = piece.astype(BF)


def pack(counts, latent, residual):
    slots, lanes = latent.shape
    shape = (slots + 32, lanes)
    return pl.pallas_call(
        pack_kernel,
        grid=(1,),
        out_shape=[jax.ShapeDtypeStruct(shape, BF)] * 4,
        in_specs=[
            pl.BlockSpec(memory_space=pltpu.SMEM),
            whole(latent.shape),
            whole(residual.shape),
        ],
        out_specs=[whole(shape)] * 4,
        scratch_shapes=[pltpu.VMEM(residual.shape, F32)],
        cost_estimate=cost(2),
        name="pack",
    )(counts, latent, residual)


def repack_kernel(*refs):
    ins, outs, rows_ref = refs[:4], refs[4:8], refs[8]
    slots = ins[0].shape[0] - 32
    y = lax.axis_index("y")
    for t in range(4):
        rows_ref[t] = ins[t][slots:, :].astype(F32)
    for s in range(4):
        at = pl.ds(pl.multiple_of(((y + s) & 3) * 8, 8), 8)
        for t in range(4):
            outs[s][t * slots : (t + 1) * slots, :] = ins[t][:slots, :]
        for t in (0, 2):
            pair = jnp.concatenate([rows_ref[t, at, :], rows_ref[t + 1, at, :]], axis=0)
            outs[s][4 * slots + 8 * t : 4 * slots + 8 * t + 16, :] = pair.astype(BF)


def repack(*pieces):
    rows, lanes = pieces[0].shape
    shape = (4 * (rows - 32) + 32, lanes)
    return pl.pallas_call(
        repack_kernel,
        grid=(1,),
        out_shape=[jax.ShapeDtypeStruct(shape, BF)] * 4,
        in_specs=[whole(pieces[0].shape)] * 4,
        out_specs=[whole(shape)] * 4,
        scratch_shapes=[pltpu.VMEM((4, 32, lanes), F32)],
        cost_estimate=cost(2),
        name="repack",
    )(*pieces)


def score_kernel(counts_ref, qn_ref, qr_ref, lat_ref, kr_ref, ku_ref, req_ref, out_ref, s_ref):
    slots = lat_ref.shape[0]
    heads = ku_ref.shape[1] // NOPE
    before = live_before(counts_ref)
    keys = dot(lat_ref[...], ku_ref[...]).astype(BF)
    key_rope = kr_ref[...]
    s_at, t_at = iota((slots, slots), 0), iota((slots, slots), 1)
    across = jnp.broadcast_to(req_ref[...], (slots, slots))
    down = jnp.sum(jnp.where(s_at == t_at, across, 0), axis=1, keepdims=True)
    allowed = (across == down) & (t_at <= s_at)
    t_row, lane = iota((slots, BLK), 0), iota((slots, BLK), 1)
    lands = ((before + t_row) & (WIN - 1)) == (lane & (WIN - 1))
    per = BLK // WIN
    for h in range(heads):
        rows = slice(h * slots, (h + 1) * slots)
        s = nt(qn_ref[:, h * NOPE : (h + 1) * NOPE], keys[:, h * NOPE : (h + 1) * NOPE])
        s = s + nt(qr_ref[:, h * ROPE : (h + 1) * ROPE], key_rope)
        s_ref[rows, :] = jnp.where(allowed, s * (NOPE + ROPE) ** (-0.5), jnp.float32(-1e30))
    s = s_ref[...]
    raised = jnp.exp(s - jnp.max(s, axis=-1, keepdims=True))
    w = (raised / jnp.sum(raised, axis=-1, keepdims=True)).astype(BF)
    folded = dot(w, jnp.where(lands, 1.0, 0.0).astype(BF))
    for group in range(heads // per):
        out = folded[group * per * slots : (group * per + 1) * slots]
        for i in range(1, per):
            h = group * per + i
            out = jnp.where((lane >> 5) == i, folded[h * slots : (h + 1) * slots], out)
        for copy in range(out_ref.shape[0]):
            out_ref[copy, :, group * BLK : (group + 1) * BLK] = out.astype(BF)


def score_weights(counts, *arrays):
    slots, heads = arrays[2].shape[0], arrays[4].shape[1] // NOPE
    shape = (4, slots, heads * WIN)
    return pl.pallas_call(
        score_kernel,
        grid=(1,),
        out_shape=jax.ShapeDtypeStruct(shape, BF),
        in_specs=[pl.BlockSpec(memory_space=pltpu.SMEM)] + [whole(a.shape) for a in arrays],
        out_specs=whole(shape),
        scratch_shapes=[pltpu.VMEM((slots * heads, slots), F32)],
        cost_estimate=cost(4),
        name="score_weights",
    )(counts, *arrays)


def live_rows(goes_ref, own_ref, other_ref):
    row = iota((STEP, own_ref.shape[0]), 0) + pl.program_id(0) * STEP
    out = dot(jnp.where(goes_ref[0] == row, 1.0, 0.0).astype(BF), own_ref[...])
    out = out + dot(jnp.where(goes_ref[1] == row, 1.0, 0.0).astype(BF), other_ref[...])
    return out.astype(BF)


def values_kernel(goes_ref, own_ref, other_ref, up_ref, out_ref):
    out_ref[...] = dot(live_rows(goes_ref, own_ref, other_ref), up_ref[...]).astype(BF)


def live_values(goes, own, other, up):
    width = up.shape[1]
    return pl.pallas_call(
        values_kernel,
        grid=(LIVE // STEP,),
        out_shape=jax.ShapeDtypeStruct((LIVE, width), BF),
        in_specs=[whole(a.shape) for a in (goes, own, other, up)],
        out_specs=pl.BlockSpec((STEP, width), lambda b: (b, 0)),
        cost_estimate=cost(0),
        compiler_params=pltpu.CompilerParams(vmem_limit_bytes=24 * 2**20),
        name="live_values",
    )(goes, own, other, up)


def mix_kernel(goes_ref, own_ref, other_ref, prev_ref, cur_ref, wo_ref, out_ref, att_ref, all_ref):
    b = pl.program_id(0)
    heads = cur_ref.shape[1] // VH
    r_at, l_at = iota((BLK, BLK), 0), iota((BLK, BLK), 1)
    gap = r_at - l_at
    near = (gap >= 0) & (gap < WIN)
    per = BLK // WIN
    masks = [jnp.where(near & ((l_at >> 5) == q), 1.0, 0.0).astype(BF) for q in range(per)]
    r_at, l_at = iota((WIN, BLK), 0), iota((WIN, BLK), 1)
    before = jnp.where((BLK + r_at - l_at) < WIN, 1.0, 0.0).astype(BF)
    blank = jnp.zeros((BLK - WIN, BLK), BF)
    packed = live_rows(goes_ref, own_ref, other_ref)
    for group in range(heads // per):
        one = packed[:, group * BLK : (group + 1) * BLK].astype(F32)
        turned = [one.astype(BF)]
        for q in range(1, per):
            turned.append(pltpu.roll(one, q * WIN, 1).astype(BF))
        for i in range(per):
            cols = slice((group * per + i) * VH, (group * per + i + 1) * VH)
            last = turned[(per - 1 - i) % per]
            olds = [prev_ref[:, cols], cur_ref[:BLK, cols]]
            for t in range(STEP // BLK):
                rows = slice(t * BLK, (t + 1) * BLK)
                band = turned[(-i) % per][rows] * masks[0]
                for q in range(1, per):
                    band = band + turned[(q - i) % per][rows] * masks[q]
                corner = jnp.concatenate([last[rows][:WIN] * before, blank], axis=0)
                att = dot(
                    jnp.concatenate([corner, band], axis=1),
                    jnp.concatenate([olds[t], cur_ref[rows, cols]], axis=0),
                )
                att_ref[rows, cols] = att.astype(BF)
    part = nt(att_ref[...], wo_ref[...]).astype(BF)
    share = STEP // 8
    r_at, l_at = iota((STEP, STEP), 0), iota((STEP, STEP), 1)
    order = ((r_at & (share - 1)) * 8 + (r_at >> 5)) == l_at
    part = dot(jnp.where(order, 1.0, 0.0).astype(BF), part)
    rows = pl.ds(pl.multiple_of(b * share, share), share)
    for m in range(8):
        all_ref[m, rows, :] = part[m * share : (m + 1) * share]

    @pl.when(b == pl.num_programs(0) - 1)
    def _():
        for m in range(8):
            out_ref[m] = all_ref[m].T.astype(BF)


def mix_project(goes, own, other, values, wo):
    width = values.shape[1]
    n = wo.shape[0]
    shape = (8, n, LIVE // 8)
    return pl.pallas_call(
        mix_kernel,
        grid=(LIVE // STEP,),
        out_shape=jax.ShapeDtypeStruct(shape, BF),
        in_specs=[
            whole(goes.shape),
            whole(own.shape),
            whole(other.shape),
            pl.BlockSpec((BLK, width), lambda b: (jnp.maximum(b * (STEP // BLK) - 1, 0), 0)),
            pl.BlockSpec((STEP, width), lambda b: (b, 0)),
            whole(wo.shape),
        ],
        out_specs=whole(shape),
        scratch_shapes=[pltpu.VMEM((STEP, width), BF), pltpu.VMEM((8, LIVE // 8, n), F32)],
        cost_estimate=cost(9),
        compiler_params=pltpu.CompilerParams(vmem_limit_bytes=50 * 2**20),
        name="mix_project",
    )(goes, own, other, values, values, wo)


def gate_up_kernel(steps, own_ref, other_ref, gain_ref, gate_ref, up_ref, *refs):
    outs, x_ref = refs[:-1], refs[-1]
    core, y = lax.axis_index("c"), lax.axis_index("y")
    x_at, zl = lax.axis_index("x"), lax.axis_index("zl")
    k, chunk = own_ref.shape[2:]
    ff = gate_ref.shape[0]
    gain = jnp.broadcast_to(gain_ref[...], (8, gain_ref.shape[1])).T
    x_ref[:, :8] = gain.astype(F32)
    squares = []
    scaled = []
    for dx, dz in steps:
        spot = ((x_at + dx) & 3) * 2 + (zl ^ dz)
        total = jnp.zeros((1, chunk), F32)
        for low in range(2):
            s = (y - (spot >> 2) * 2 - low) & 3
            one, two = own_ref[s, spot & 3], other_ref[s, spot & 3]
            for half in range(2):
                x = jnp.where(core == half, one, two).astype(F32)
                total = total + jnp.sum(x * x, axis=0, keepdims=True)
                rows = slice((low * 2 + half) * k, (low * 2 + half + 1) * k)
                scaled.append((x * x_ref[rows, :1]).astype(BF))
        squares.append(total)
    columns = [
        jnp.concatenate(scaled[4 * i : 4 * i + 4], axis=0) for i in range(len(steps))
    ]
    x = jnp.concatenate(columns, axis=1)
    gate = dot(gate_ref[...], x).astype(BF)
    up = dot(up_ref[...], x).astype(BF)
    row = iota((16, chunk), 0)
    for i, out_ref in enumerate(outs):
        cols = slice(i * chunk, (i + 1) * chunk)
        high = squares[i].astype(BF).astype(F32)
        extra = jnp.where(row == 0, high, jnp.where(row == 1, squares[i] - high, 0.0))
        out_ref[:ff, :] = gate[:, cols]
        out_ref[ff : 2 * ff, :] = up[:, cols]
        out_ref[2 * ff :, :] = extra.astype(BF)


def gate_up(steps, own, other, gain, gate_weight, up_weight):
    k, chunk = own.shape[2:]
    ff, width = gate_weight.shape
    shape = (2 * ff + 16, chunk)
    arrays = (own, other, gain, gate_weight, up_weight)
    return pl.pallas_call(
        functools.partial(gate_up_kernel, steps),
        grid=(1,),
        out_shape=[jax.ShapeDtypeStruct(shape, BF)] * len(steps),
        in_specs=[whole(a.shape) for a in arrays],
        out_specs=[whole(shape)] * len(steps),
        scratch_shapes=[pltpu.VMEM((width, BLK), F32)],
        cost_estimate=cost(4),
        compiler_params=pltpu.CompilerParams(vmem_limit_bytes=24 * 2**20),
        name="gate_up",
    )(*arrays)


def down_kernel(flip, *refs):
    pieces, (w_ref, out_ref) = refs[:8], refs[8:]
    swapped = lax.axis_index("zl") ^ lax.axis_index("c") ^ flip
    x = jnp.concatenate(
        [
            jnp.where(swapped == 0, pieces[4 + dx][...], pieces[dx][...])
            for dx in range(4)
        ],
        axis=1,
    )
    out = lax.dot_general(
        x, w_ref[...], (((0,), (0,)), ((), ())), preferred_element_type=F32
    )
    out_ref[...] = out.reshape(out_ref.shape).astype(out_ref.dtype)


def down(flip, pieces, weight, kind):
    shape = (4, pieces[0].shape[1], weight.shape[1])
    return pl.pallas_call(
        functools.partial(down_kernel, flip),
        grid=(1,),
        out_shape=jax.ShapeDtypeStruct(shape, kind),
        in_specs=[whole(p.shape) for p in pieces] + [whole(weight.shape)],
        out_specs=whole(shape),
        compiler_params=pltpu.CompilerParams(vmem_limit_bytes=24 * 2**20),
        cost_estimate=cost(2),
        name="down",
    )(*pieces, weight)


def sent_along_hd(x, dx, dz):
    return lax.ppermute(x, HD, [(i, ((i // 2 + dx) % 4) * 2 + ((i % 2) ^ dz)) for i in range(8)])


def exchange(x, axes):
    return lax.all_to_all(x, axes, split_axis=0, concat_axis=0, tiled=True)


def gather(x, axes):
    n = lax.axis_size(axes)
    return exchange(jnp.broadcast_to(x[None], (n,) + x.shape), axes)


def pick(x, index):
    return lax.dynamic_index_in_dim(x, index, 0, keepdims=False)


def on_device(
    query_nope,
    query_rope,
    latent,
    key_rope,
    key_up,
    value_up,
    output_weight,
    residual,
    norm_gain,
    gate_weight,
    up_weight,
    down_weight,
    rank_tokens,
    request_ids,
):
    slots = latent.shape[0]
    ranks = rank_tokens.shape[0]
    zh, y, c = (lax.axis_index(a) for a in DP)
    rank = (zh * 4 + y) * 2 + c
    chunk = LIVE // 8
    width = residual.shape[1]
    quarter = width // 4
    model = 8 * width

    every = jnp.arange(ranks, dtype=jnp.int32)

    def starts(which, counts=rank_tokens):
        return jnp.sum(jnp.where(every < which[..., None], counts, 0), axis=-1)

    def lengths(which, counts=rank_tokens):
        return jnp.sum(jnp.where(every == which[..., None], counts, 0), axis=-1)

    own_start, own_length = starts(rank), lengths(rank)
    slot = jnp.arange(slots, dtype=jnp.int32)

    pieces = pack(rank_tokens, latent, residual)
    pieces = [pieces[0]] + [shifted(pieces[s], "zh", s) for s in (1, 2, 3)]

    weights = score_weights(
        rank_tokens, query_nope, query_rope, latent, key_rope, key_up, request_ids
    )
    pieces, _ = lax.optimization_barrier((pieces, weights))
    weights = exchange(weights, "zh")
    pieces = repack(*pieces)

    late, _ = lax.optimization_barrier((rank_tokens, pieces[3]))
    four = jnp.arange(4, dtype=jnp.int32)
    eight = jnp.arange(8, dtype=jnp.int32)
    core = jnp.stack([c, 1 - c])[:, None, None]
    ahead = (four[None, None, :] * 4 + ((y - four) & 3)[None, :, None]) * 2 + core
    goes = jnp.where(slot < lengths(ahead, late)[..., None], starts(ahead, late)[..., None] + slot, -1)
    goes = goes.reshape(2, 1, -1)
    back = (((zh - four) & 3)[None, None, :] * 4 + ((y - four) & 3)[None, :, None]) * 2 + core
    back_start, back_count = starts(back, late)[..., None], lengths(back, late)[..., None]
    goes_back = jnp.where(slot < back_count, back_start + slot, -1).reshape(2, 4, -1)
    goes_back = jnp.pad(goes_back, ((0, 0), (0, 0), (0, 32)), constant_values=-1).reshape(2, 1, -1)
    place = (((zh * 2 + (y >> 1)) - back_start) & 7) + 8 * eight
    come = jnp.where(place < back_count, (back_start + place) >> 3, -1)
    come = (come.reshape(2, -1, 1) == jnp.arange(chunk, dtype=jnp.int32)).astype(BF)

    gain, _ = lax.optimization_barrier((norm_gain[None, :], weights))
    pieces = [pieces[0]] + [shifted(pieces[s], "y", s) for s in (1, 2, 3)]
    last, goes, goes_back, come, _ = lax.optimization_barrier(
        (pieces[3], goes, goes_back, come, weights)
    )
    got = jnp.concatenate(pieces[:3] + [last], axis=0)
    got_other = shifted(got, "c", 1)
    weights = weights.reshape(-1, weights.shape[2])
    weights = [weights] + [shifted(weights, "y", s) for s in (1, 2, 3)]

    values = live_values(goes_back, got, got_other, value_up)

    def tn(a, b):
        return lax.dot_general(a, b, (((0,), (0,)), ((), ())), preferred_element_type=F32)

    rows = [a.reshape(4, -1, a.shape[1])[:, 4 * slots :].reshape(-1, a.shape[1]) for a in (got, got_other)]
    rows = tn(rows[0], come[0]) + tn(rows[1], come[1])
    rows = jnp.where(c == 0, rows[:quarter], rows[quarter : 2 * quarter])
    weights, values = lax.optimization_barrier((weights, values))
    weights = jnp.concatenate(weights, axis=0)
    weights, _ = lax.optimization_barrier((weights, got_other))
    weights_other = shifted(weights, "c", 1)
    part = mix_project(goes, weights, weights_other, values, output_weight.T)
    projected = jnp.sum(exchange(part, HD).astype(F32), axis=0).astype(BF)

    swap = []
    for a in range(4):
        for b in range(8):
            for e in range(4):
                for f in range(2):
                    to = (e * 8 + (f * 4 + (b & 3))) * 8 + a * 2 + (b >> 2)
                    swap.append(((a * 8 + b) * 8 + e * 2 + f, to))
    projected = lax.ppermute(projected, DP + HD, swap)
    mixed = (rows + projected.astype(F32)).astype(BF)
    full = jnp.stack([mixed] + [shifted(mixed, "zh", k) for k in (1, 2, 3)])

    full = jnp.stack([full] + [shifted(full, "y", s) for s in (1, 2, 3)])
    full_other = shifted(full, "c", 1)
    ff = down_weight.shape[0]
    arrays = (full, full_other, gain, gate_weight.T, up_weight.T)
    late = [(0, 0), (1, 0), (3, 0), (2, 0)]
    soon = [(0, 1), (1, 1), (3, 1), (2, 1)]
    parts = list(zip(late, gate_up(late, *arrays))) + list(zip(soon, gate_up(soon, *arrays)))
    total = parts[0][1].astype(F32)
    for (dx, dz), part in parts[1:]:
        total = total + sent_along_hd(part, dx, dz).astype(F32)
    scale = lax.rsqrt((total[2 * ff : 2 * ff + 1] + total[2 * ff + 1 : 2 * ff + 2]) / model + 1e-06)
    hidden = (jax.nn.silu(total[:ff] * scale) * (total[ff : 2 * ff] * scale)).astype(BF)
    got_hidden = {(0, 0): hidden}
    for step in soon + late[1:]:
        got_hidden[step] = sent_along_hd(hidden, *step)
    hidden = [got_hidden[r % 4, 1 - r // 4] for r in range(8)]

    sent = shifted(down(1, hidden, down_weight, BF), "c", 1)
    total = down(0, hidden, down_weight, F32) + sent.astype(F32)
    turn = lax.axis_index("x") - y
    pieces = [pick(total, (turn - s) & 3) for s in range(4)]
    total = pieces[0]
    for s in (1, 2, 3):
        total = total + shifted(pieces[s].astype(BF), "y", s).astype(F32)
    spot = y * 2 + c
    begin = starts(every)
    m = ((zh - (spot & 3)) & 3) * 2 + (spot >> 2)
    place = ((m - begin[:, None]) & 7) + 8 * eight[None, :]
    comes = jnp.where(place < rank_tokens[:, None], (begin[:, None] + place) >> 3, -1)
    expand = (comes.reshape(ranks * 8, 1) == jnp.arange(chunk, dtype=jnp.int32)).astype(BF)
    at = [(y - (spot >> 2) * 2 - low) & 3 for low in range(2)]
    pair = [jnp.stack([pick(pick(a, s), spot & 3) for s in at]) for a in (full, full_other)]
    low = jnp.where(c == 0, pair[0], pair[1])
    high = jnp.where(c == 0, pair[1], pair[0])
    own = jnp.stack([low, high], axis=1).reshape(width, chunk)
    here = (jnp.arange(ranks * 8, dtype=jnp.int32) >> 6) == zh
    own = nt(jnp.where(here[:, None], expand, jnp.zeros_like(expand)), own)
    result = (dot(expand, total.astype(BF)) + own).astype(BF).reshape(ranks, 8, width)
    result = exchange(result, DP).reshape(ranks * 8, width)
    source = jnp.arange(ranks, dtype=jnp.int32)
    chunk_of = (((source >> 3) - (source & 3)) & 3) * 2 + ((source >> 2) & 1)
    fits = chunk_of[None, :, None] == ((own_start + slot) & 7)[:, None, None]
    fits = fits & (eight[None, None, :] == (slot >> 3)[:, None, None])
    fits = fits & (slot < own_length)[:, None, None]
    return dot(fits.astype(BF).reshape(slots, ranks * 8), result).astype(BF)


def solution(mesh):
    mesh = Mesh(mesh.devices.reshape(4, 4, 2, 4, 2), DP + HD)
    in_specs = (
        P(DP, HD),
        P(DP, HD),
        P(DP, None),
        P(DP, None),
        P(None, HD),
        P(None, HD),
        P(HD, DP),
        P(DP, HD),
        P(HD),
        P(HD, DP),
        P(HD, DP),
        P(DP, HD),
        P(),
        P(DP, None),
    )
    return jax.shard_map(
        on_device, mesh=mesh, in_specs=in_specs, out_specs=P(DP, HD), check_vma=False
    )
```

```python
import functools

import jax
import jax.numpy as jnp
from jax import lax
from jax.experimental import pallas as pl
from jax.experimental.pallas import tpu as pltpu
from jax.sharding import Mesh, PartitionSpec as P

BF = jnp.bfloat16
F32 = jnp.float32
NOPE = 128
ROPE = 64
VH = 128
WIN = 32
LIVE = 1024
BLK = 128
STEP = 256
DP = ("zh", "y", "c")
HD = ("x", "zl")


def dot(a, b):
    return jnp.dot(a, b, preferred_element_type=F32)


def shifted(x, axis, shift):
    n = lax.axis_size(axis)
    return lax.ppermute(x, axis, [(i, (i + shift) % n) for i in range(n)])


def iota(shape, dim):
    return lax.broadcasted_iota(jnp.int32, shape, dim)


def nt(a, b):
    return lax.dot_general(a, b, (((1,), (1,)), ((), ())), preferred_element_type=F32)


def whole(shape):
    return pl.BlockSpec(shape, lambda *_: (0,) * len(shape), pipeline_mode=pl.Buffered(1))


def cost(us):
    return pl.CostEstimate(flops=us * 10**9, bytes_accessed=us * 3 * 10**6, transcendentals=0)


def rank_here():
    return (lax.axis_index("zh") * 4 + lax.axis_index("y")) * 2 + lax.axis_index("c")


def live_before(counts_ref):
    place = rank_here()
    return lax.fori_loop(
        0,
        counts_ref.shape[0],
        lambda i, a: a + jnp.where(i < place, counts_ref[i], 0),
        jnp.int32(0),
    )


def pack_kernel(counts_ref, lat_ref, res_ref, *refs):
    outs, rows_ref = refs[:4], refs[4]
    slots, width = res_ref.shape
    half, lanes = width // 2, lat_ref.shape[1]
    zh = lax.axis_index("zh")
    start = live_before(counts_ref)
    i_at, slot = iota((slots, slots), 0), iota((slots, slots), 1)
    roll = ((((i_at >> 3) - start) & 7) + 8 * (i_at & 7)) == slot
    rows_ref[...] = dot(jnp.where(roll, 1.0, 0.0).astype(BF), res_ref[...])
    fill = jnp.zeros((16, lanes - half), F32)
    for s in range(4):
        outs[s][:slots, :] = lat_ref[...]
        for high in range(2):
            m = ((zh + s) & 3) * 2 + high
            piece = rows_ref[pl.ds(pl.multiple_of(m * 8, 8), 8), :]
            piece = jnp.concatenate([piece[:, :half], piece[:, half:]], axis=0)
            piece = jnp.concatenate([piece, fill], axis=1)
            outs[s][slots + 16 * high : slots + 16 * (high + 1), :] = piece.astype(BF)


def pack(counts, latent, residual):
    slots, lanes = latent.shape
    shape = (slots + 32, lanes)
    return pl.pallas_call(
        pack_kernel,
        grid=(1,),
        out_shape=[jax.ShapeDtypeStruct(shape, BF)] * 4,
        in_specs=[
            pl.BlockSpec(memory_space=pltpu.SMEM),
            whole(latent.shape),
            whole(residual.shape),
        ],
        out_specs=[whole(shape)] * 4,
        scratch_shapes=[pltpu.VMEM(residual.shape, F32)],
        cost_estimate=cost(2),
        name="pack",
    )(counts, latent, residual)


def repack_kernel(*refs):
    ins, outs, rows_ref = refs[:4], refs[4:8], refs[8]
    slots = ins[0].shape[0] - 32
    y = lax.axis_index("y")
    for t in range(4):
        rows_ref[t] = ins[t][slots:, :].astype(F32)
    for s in range(4):
        at = pl.ds(pl.multiple_of(((y + s) & 3) * 8, 8), 8)
        for t in range(4):
            outs[s][t * slots : (t + 1) * slots, :] = ins[t][:slots, :]
        for t in (0, 2):
            pair = jnp.concatenate([rows_ref[t, at, :], rows_ref[t + 1, at, :]], axis=0)
            outs[s][4 * slots + 8 * t : 4 * slots + 8 * t + 16, :] = pair.astype(BF)


def repack(*pieces):
    rows, lanes = pieces[0].shape
    shape = (4 * (rows - 32) + 32, lanes)
    return pl.pallas_call(
        repack_kernel,
        grid=(1,),
        out_shape=[jax.ShapeDtypeStruct(shape, BF)] * 4,
        in_specs=[whole(pieces[0].shape)] * 4,
        out_specs=[whole(shape)] * 4,
        scratch_shapes=[pltpu.VMEM((4, 32, lanes), F32)],
        cost_estimate=cost(2),
        name="repack",
    )(*pieces)


def score_kernel(counts_ref, qn_ref, qr_ref, lat_ref, kr_ref, ku_ref, req_ref, out_ref, s_ref):
    slots = lat_ref.shape[0]
    heads = ku_ref.shape[1] // NOPE
    before = live_before(counts_ref)
    keys = dot(lat_ref[...], ku_ref[...]).astype(BF)
    key_rope = kr_ref[...]
    s_at, t_at = iota((slots, slots), 0), iota((slots, slots), 1)
    across = jnp.broadcast_to(req_ref[...], (slots, slots))
    down = jnp.sum(jnp.where(s_at == t_at, across, 0), axis=1, keepdims=True)
    allowed = (across == down) & (t_at <= s_at)
    t_row, lane = iota((slots, BLK), 0), iota((slots, BLK), 1)
    lands = ((before + t_row) & (WIN - 1)) == (lane & (WIN - 1))
    per = BLK // WIN
    for h in range(heads):
        rows = slice(h * slots, (h + 1) * slots)
        s = nt(qn_ref[:, h * NOPE : (h + 1) * NOPE], keys[:, h * NOPE : (h + 1) * NOPE])
        s = s + nt(qr_ref[:, h * ROPE : (h + 1) * ROPE], key_rope)
        s_ref[rows, :] = jnp.where(allowed, s * (NOPE + ROPE) ** (-0.5), jnp.float32(-1e30))
    s = s_ref[...]
    raised = jnp.exp(s - jnp.max(s, axis=-1, keepdims=True))
    w = (raised / jnp.sum(raised, axis=-1, keepdims=True)).astype(BF)
    folded = dot(w, jnp.where(lands, 1.0, 0.0).astype(BF))
    for group in range(heads // per):
        out = folded[group * per * slots : (group * per + 1) * slots]
        for i in range(1, per):
            h = group * per + i
            out = jnp.where((lane >> 5) == i, folded[h * slots : (h + 1) * slots], out)
        for copy in range(out_ref.shape[0]):
            out_ref[copy, :, group * BLK : (group + 1) * BLK] = out.astype(BF)


def score_weights(counts, *arrays):
    slots, heads = arrays[2].shape[0], arrays[4].shape[1] // NOPE
    shape = (4, slots, heads * WIN)
    return pl.pallas_call(
        score_kernel,
        grid=(1,),
        out_shape=jax.ShapeDtypeStruct(shape, BF),
        in_specs=[pl.BlockSpec(memory_space=pltpu.SMEM)] + [whole(a.shape) for a in arrays],
        out_specs=whole(shape),
        scratch_shapes=[pltpu.VMEM((slots * heads, slots), F32)],
        cost_estimate=cost(4),
        name="score_weights",
    )(counts, *arrays)


def live_rows(goes_ref, own_ref, other_ref):
    row = iota((STEP, own_ref.shape[0]), 0) + pl.program_id(0) * STEP
    out = dot(jnp.where(goes_ref[0] == row, 1.0, 0.0).astype(BF), own_ref[...])
    out = out + dot(jnp.where(goes_ref[1] == row, 1.0, 0.0).astype(BF), other_ref[...])
    return out.astype(BF)


def values_kernel(goes_ref, own_ref, other_ref, up_ref, out_ref):
    out_ref[...] = dot(live_rows(goes_ref, own_ref, other_ref), up_ref[...]).astype(BF)


def live_values(goes, own, other, up):
    width = up.shape[1]
    return pl.pallas_call(
        values_kernel,
        grid=(LIVE // STEP,),
        out_shape=jax.ShapeDtypeStruct((LIVE, width), BF),
        in_specs=[whole(a.shape) for a in (goes, own, other, up)],
        out_specs=pl.BlockSpec((STEP, width), lambda b: (b, 0)),
        cost_estimate=cost(0),
        compiler_params=pltpu.CompilerParams(vmem_limit_bytes=24 * 2**20),
        name="live_values",
    )(goes, own, other, up)


def mix_kernel(goes_ref, own_ref, other_ref, prev_ref, cur_ref, wo_ref, *refs):
    outs, att_ref, all_ref = refs[:8], refs[8], refs[9]
    b = pl.program_id(0)
    heads = cur_ref.shape[1] // VH
    r_at, l_at = iota((BLK, BLK), 0), iota((BLK, BLK), 1)
    gap = r_at - l_at
    near = (gap >= 0) & (gap < WIN)
    per = BLK // WIN
    masks = [jnp.where(near & ((l_at >> 5) == q), 1.0, 0.0).astype(BF) for q in range(per)]
    r_at, l_at = iota((WIN, BLK), 0), iota((WIN, BLK), 1)
    before = jnp.where((BLK + r_at - l_at) < WIN, 1.0, 0.0).astype(BF)
    blank = jnp.zeros((BLK - WIN, BLK), BF)
    packed = live_rows(goes_ref, own_ref, other_ref)
    for group in range(heads // per):
        one = packed[:, group * BLK : (group + 1) * BLK].astype(F32)
        turned = [one.astype(BF)]
        for q in range(1, per):
            turned.append(pltpu.roll(one, q * WIN, 1).astype(BF))
        for i in range(per):
            cols = slice((group * per + i) * VH, (group * per + i + 1) * VH)
            last = turned[(per - 1 - i) % per]
            olds = [prev_ref[:, cols], cur_ref[:BLK, cols]]
            for t in range(STEP // BLK):
                rows = slice(t * BLK, (t + 1) * BLK)
                band = turned[(-i) % per][rows] * masks[0]
                for q in range(1, per):
                    band = band + turned[(q - i) % per][rows] * masks[q]
                corner = jnp.concatenate([last[rows][:WIN] * before, blank], axis=0)
                att = dot(
                    jnp.concatenate([corner, band], axis=1),
                    jnp.concatenate([olds[t], cur_ref[rows, cols]], axis=0),
                )
                att_ref[rows, cols] = att.astype(BF)
    part = nt(att_ref[...], wo_ref[...]).astype(BF)
    share = STEP // 8
    r_at, l_at = iota((STEP, STEP), 0), iota((STEP, STEP), 1)
    order = ((r_at & (share - 1)) * 8 + (r_at >> 5)) == l_at
    part = dot(jnp.where(order, 1.0, 0.0).astype(BF), part)
    rows = pl.ds(pl.multiple_of(b * share, share), share)
    for m in range(8):
        all_ref[m, rows, :] = part[m * share : (m + 1) * share]

    @pl.when(b == pl.num_programs(0) - 1)
    def _():
        x_at, zl = lax.axis_index("x"), lax.axis_index("zl")
        for r in range(8):
            outs[r][...] = all_ref[((x_at + r // 2) & 3) * 2 + (zl ^ (r % 2))].T.astype(BF)


def mix_project(goes, own, other, values, wo):
    width = values.shape[1]
    n = wo.shape[0]
    shape = (n, LIVE // 8)
    return pl.pallas_call(
        mix_kernel,
        grid=(LIVE // STEP,),
        out_shape=[jax.ShapeDtypeStruct(shape, BF)] * 8,
        in_specs=[
            whole(goes.shape),
            whole(own.shape),
            whole(other.shape),
            pl.BlockSpec((BLK, width), lambda b: (jnp.maximum(b * (STEP // BLK) - 1, 0), 0)),
            pl.BlockSpec((STEP, width), lambda b: (b, 0)),
            whole(wo.shape),
        ],
        out_specs=[whole(shape)] * 8,
        scratch_shapes=[pltpu.VMEM((STEP, width), BF), pltpu.VMEM((8, LIVE // 8, n), F32)],
        cost_estimate=cost(9),
        compiler_params=pltpu.CompilerParams(vmem_limit_bytes=50 * 2**20),
        name="mix_project",
    )(goes, own, other, values, values, wo)


def gate_up_kernel(steps, own_ref, other_ref, gain_ref, gate_ref, up_ref, *refs):
    outs, x_ref = refs[:-1], refs[-1]
    core, y = lax.axis_index("c"), lax.axis_index("y")
    x_at, zl = lax.axis_index("x"), lax.axis_index("zl")
    k, chunk = own_ref.shape[2:]
    ff = gate_ref.shape[0]
    gain = jnp.broadcast_to(gain_ref[...], (8, gain_ref.shape[1])).T
    x_ref[:, :8] = gain.astype(F32)
    squares = []
    scaled = []
    for dx, dz in steps:
        spot = ((x_at + dx) & 3) * 2 + (zl ^ dz)
        total = jnp.zeros((1, chunk), F32)
        for low in range(2):
            s = (y - (spot >> 2) * 2 - low) & 3
            one, two = own_ref[s, spot & 3], other_ref[s, spot & 3]
            for half in range(2):
                x = jnp.where(core == half, one, two).astype(F32)
                total = total + jnp.sum(x * x, axis=0, keepdims=True)
                rows = slice((low * 2 + half) * k, (low * 2 + half + 1) * k)
                scaled.append((x * x_ref[rows, :1]).astype(BF))
        squares.append(total)
    columns = [
        jnp.concatenate(scaled[4 * i : 4 * i + 4], axis=0) for i in range(len(steps))
    ]
    x = jnp.concatenate(columns, axis=1)
    gate = dot(gate_ref[...], x).astype(BF)
    up = dot(up_ref[...], x).astype(BF)
    row = iota((16, chunk), 0)
    for i, out_ref in enumerate(outs):
        cols = slice(i * chunk, (i + 1) * chunk)
        high = squares[i].astype(BF).astype(F32)
        extra = jnp.where(row == 0, high, jnp.where(row == 1, squares[i] - high, 0.0))
        out_ref[:ff, :] = gate[:, cols]
        out_ref[ff : 2 * ff, :] = up[:, cols]
        out_ref[2 * ff :, :] = extra.astype(BF)


def gate_up(steps, own, other, gain, gate_weight, up_weight):
    k, chunk = own.shape[2:]
    ff, width = gate_weight.shape
    shape = (2 * ff + 16, chunk)
    arrays = (own, other, gain, gate_weight, up_weight)
    return pl.pallas_call(
        functools.partial(gate_up_kernel, steps),
        grid=(1,),
        out_shape=[jax.ShapeDtypeStruct(shape, BF)] * len(steps),
        in_specs=[whole(a.shape) for a in arrays],
        out_specs=[whole(shape)] * len(steps),
        scratch_shapes=[pltpu.VMEM((width, BLK), F32)],
        cost_estimate=cost(4),
        compiler_params=pltpu.CompilerParams(vmem_limit_bytes=24 * 2**20),
        name="gate_up",
    )(*arrays)


def down_kernel(flip, *refs):
    pieces, (w_ref, out_ref) = refs[:8], refs[8:]
    swapped = lax.axis_index("zl") ^ lax.axis_index("c") ^ flip
    x = jnp.concatenate(
        [
            jnp.where(swapped == 0, pieces[4 + dx][...], pieces[dx][...])
            for dx in range(4)
        ],
        axis=1,
    )
    out = lax.dot_general(
        x, w_ref[...], (((0,), (0,)), ((), ())), preferred_element_type=F32
    )
    out_ref[...] = out.reshape(out_ref.shape).astype(out_ref.dtype)


def down(flip, pieces, weight, kind):
    shape = (4, pieces[0].shape[1], weight.shape[1])
    return pl.pallas_call(
        functools.partial(down_kernel, flip),
        grid=(1,),
        out_shape=jax.ShapeDtypeStruct(shape, kind),
        in_specs=[whole(p.shape) for p in pieces] + [whole(weight.shape)],
        out_specs=whole(shape),
        compiler_params=pltpu.CompilerParams(vmem_limit_bytes=24 * 2**20),
        cost_estimate=cost(2),
        name="down",
    )(*pieces, weight)


def sent_along_hd(x, dx, dz):
    return lax.ppermute(x, HD, [(i, ((i // 2 + dx) % 4) * 2 + ((i % 2) ^ dz)) for i in range(8)])


def exchange(x, axes):
    return lax.all_to_all(x, axes, split_axis=0, concat_axis=0, tiled=True)


def gather(x, axes):
    n = lax.axis_size(axes)
    return exchange(jnp.broadcast_to(x[None], (n,) + x.shape), axes)


def pick(x, index):
    return lax.dynamic_index_in_dim(x, index, 0, keepdims=False)


def on_device(
    query_nope,
    query_rope,
    latent,
    key_rope,
    key_up,
    value_up,
    output_weight,
    residual,
    norm_gain,
    gate_weight,
    up_weight,
    down_weight,
    rank_tokens,
    request_ids,
):
    slots = latent.shape[0]
    ranks = rank_tokens.shape[0]
    zh, y, c = (lax.axis_index(a) for a in DP)
    rank = (zh * 4 + y) * 2 + c
    chunk = LIVE // 8
    width = residual.shape[1]
    quarter = width // 4
    model = 8 * width

    every = jnp.arange(ranks, dtype=jnp.int32)

    def starts(which, counts=rank_tokens):
        return jnp.sum(jnp.where(every < which[..., None], counts, 0), axis=-1)

    def lengths(which, counts=rank_tokens):
        return jnp.sum(jnp.where(every == which[..., None], counts, 0), axis=-1)

    own_start, own_length = starts(rank), lengths(rank)
    slot = jnp.arange(slots, dtype=jnp.int32)

    pieces = pack(rank_tokens, latent, residual)
    pieces = [pieces[0]] + [shifted(pieces[s], "zh", s) for s in (1, 2, 3)]

    weights = score_weights(
        rank_tokens, query_nope, query_rope, latent, key_rope, key_up, request_ids
    )
    weights = exchange(weights, "zh")
    pieces = repack(*pieces)

    late, _ = lax.optimization_barrier((rank_tokens, pieces[3]))
    four = jnp.arange(4, dtype=jnp.int32)
    eight = jnp.arange(8, dtype=jnp.int32)
    core = jnp.stack([c, 1 - c])[:, None, None]
    ahead = (four[None, None, :] * 4 + four[None, :, None]) * 2 + core
    goes = jnp.where(slot < lengths(ahead, late)[..., None], starts(ahead, late)[..., None] + slot, -1)
    goes = goes.reshape(2, 1, -1)
    back = (((zh - four) & 3)[None, None, :] * 4 + ((y - four) & 3)[None, :, None]) * 2 + core
    back_start, back_count = starts(back, late)[..., None], lengths(back, late)[..., None]
    goes_back = jnp.where(slot < back_count, back_start + slot, -1).reshape(2, 4, -1)
    goes_back = jnp.pad(goes_back, ((0, 0), (0, 0), (0, 32)), constant_values=-1).reshape(2, 1, -1)
    place = (((zh * 2 + (y >> 1)) - back_start) & 7) + 8 * eight
    come = jnp.where(place < back_count, (back_start + place) >> 3, -1)
    come = (come.reshape(2, -1, 1) == jnp.arange(chunk, dtype=jnp.int32)).astype(BF)

    weights, gain, _ = lax.optimization_barrier((weights, norm_gain[None, :], pieces))
    weights = jnp.broadcast_to(weights[None], (4,) + weights.shape)
    pieces = [pieces[0]] + [shifted(pieces[s], "y", s) for s in (1, 2, 3)]
    pieces, weights, goes, goes_back, come = lax.optimization_barrier(
        (pieces, weights, goes, goes_back, come)
    )
    got = jnp.concatenate(pieces, axis=0)
    got_other = shifted(got, "c", 1)
    weights = exchange(weights, "y").reshape(-1, weights.shape[3])

    values = live_values(goes_back, got, got_other, value_up)

    def tn(a, b):
        return lax.dot_general(a, b, (((0,), (0,)), ((), ())), preferred_element_type=F32)

    rows = [a.reshape(4, -1, a.shape[1])[:, 4 * slots :].reshape(-1, a.shape[1]) for a in (got, got_other)]
    rows = tn(rows[0], come[0]) + tn(rows[1], come[1])
    rows = jnp.where(c == 0, rows[:quarter], rows[quarter : 2 * quarter])
    weights, values = lax.optimization_barrier((weights, values))
    weights_other = shifted(weights, "c", 1)
    part = mix_project(goes, weights, weights_other, values, output_weight.T)
    projected = part[0].astype(F32)
    for r in (2, 6, 4, 3, 7, 5, 1):
        projected = projected + sent_along_hd(part[r], r // 2, r % 2).astype(F32)
    projected = projected.astype(BF)

    swap = []
    for a in range(4):
        for b in range(8):
            for e in range(4):
                for f in range(2):
                    to = (e * 8 + (f * 4 + (b & 3))) * 8 + a * 2 + (b >> 2)
                    swap.append(((a * 8 + b) * 8 + e * 2 + f, to))
    projected = lax.ppermute(projected, DP + HD, swap)
    mixed = (rows + projected.astype(F32)).astype(BF)
    full = jnp.stack([mixed] + [shifted(mixed, "zh", k) for k in (1, 2, 3)])

    full = jnp.stack([full] + [shifted(full, "y", s) for s in (1, 2, 3)])
    full_other = shifted(full, "c", 1)
    ff = down_weight.shape[0]
    arrays = (full, full_other, gain, gate_weight.T, up_weight.T)
    late = [(0, 0), (1, 0), (3, 0), (2, 0)]
    soon = [(0, 1), (1, 1), (3, 1), (2, 1)]
    parts = list(zip(late, gate_up(late, *arrays))) + list(zip(soon, gate_up(soon, *arrays)))
    total = parts[0][1].astype(F32)
    for (dx, dz), part in parts[1:]:
        total = total + sent_along_hd(part, dx, dz).astype(F32)
    scale = lax.rsqrt((total[2 * ff : 2 * ff + 1] + total[2 * ff + 1 : 2 * ff + 2]) / model + 1e-06)
    hidden = (jax.nn.silu(total[:ff] * scale) * (total[ff : 2 * ff] * scale)).astype(BF)
    got_hidden = {(0, 0): hidden}
    for step in soon + late[1:]:
        got_hidden[step] = sent_along_hd(hidden, *step)
    hidden = [got_hidden[r % 4, 1 - r // 4] for r in range(8)]

    sent = shifted(down(1, hidden, down_weight, BF), "c", 1)
    total = down(0, hidden, down_weight, F32) + sent.astype(F32)
    turn = lax.axis_index("x") - y
    pieces = [pick(total, (turn - s) & 3) for s in range(4)]
    total = pieces[0]
    for s in (1, 2, 3):
        total = total + shifted(pieces[s].astype(BF), "y", s).astype(F32)
    spot = y * 2 + c
    begin = starts(every)
    m = ((zh - (spot & 3)) & 3) * 2 + (spot >> 2)
    place = ((m - begin[:, None]) & 7) + 8 * eight[None, :]
    comes = jnp.where(place < rank_tokens[:, None], (begin[:, None] + place) >> 3, -1)
    expand = (comes.reshape(ranks * 8, 1) == jnp.arange(chunk, dtype=jnp.int32)).astype(BF)
    at = [(y - (spot >> 2) * 2 - low) & 3 for low in range(2)]
    pair = [jnp.stack([pick(pick(a, s), spot & 3) for s in at]) for a in (full, full_other)]
    low = jnp.where(c == 0, pair[0], pair[1])
    high = jnp.where(c == 0, pair[1], pair[0])
    own = jnp.stack([low, high], axis=1).reshape(width, chunk)
    here = (jnp.arange(ranks * 8, dtype=jnp.int32) >> 6) == zh
    own = nt(jnp.where(here[:, None], expand, jnp.zeros_like(expand)), own)
    result = (dot(expand, total.astype(BF)) + own).astype(BF).reshape(ranks, 8, width)
    result = exchange(result, DP).reshape(ranks * 8, width)
    source = jnp.arange(ranks, dtype=jnp.int32)
    chunk_of = (((source >> 3) - (source & 3)) & 3) * 2 + ((source >> 2) & 1)
    fits = chunk_of[None, :, None] == ((own_start + slot) & 7)[:, None, None]
    fits = fits & (eight[None, None, :] == (slot >> 3)[:, None, None])
    fits = fits & (slot < own_length)[:, None, None]
    return dot(fits.astype(BF).reshape(slots, ranks * 8), result).astype(BF)


def solution(mesh):
    mesh = Mesh(mesh.devices.reshape(4, 4, 2, 4, 2), DP + HD)
    in_specs = (
        P(DP, HD),
        P(DP, HD),
        P(DP, None),
        P(DP, None),
        P(None, HD),
        P(None, HD),
        P(HD, DP),
        P(DP, HD),
        P(HD),
        P(HD, DP),
        P(HD, DP),
        P(DP, HD),
        P(),
        P(DP, None),
    )
    return jax.shard_map(
        on_device, mesh=mesh, in_specs=in_specs, out_specs=P(DP, HD), check_vma=False
    )
```
